32 devices in a mesh: section: 2 (over x), ctx: 4 (over y, core), fsdp: 4 (over z).
Axes of the slice: x: 2, y: 2, z: 4, core: 2. Of those that a mesh axis runs over, the one named last changes fastest.
Arguments:
- inputs: bfloat16 [2, 4, 256, 2048], P(None, 'fsdp', 'ctx'), may hold values from -6 to 6
- cotangent: bfloat16 [2, 4, 256, 2048], P(None, 'fsdp', 'ctx'), may hold values from -6 to 6
- norm_gains: bfloat16 [2, 2, 2048], P('section', None, 'fsdp'), may hold values from 0.5 to 1.5
- head_params: bfloat16 [2, 3, 48], P('section', None, 'fsdp'), may hold values from -4 to 0
- conv_params: bfloat16 [2, 5, 3584], P('section', None, 'fsdp'), may hold values from -0.5 to 0.5
- ssm_gain: bfloat16 [2, 3072], P('section', 'fsdp'), may hold values from 0.5 to 1.5
- w_in: bfloat16 [2, 2048, 6704], P('section', 'fsdp'), may hold values from -0.125 to 0.125
- w_out: bfloat16 [2, 3072, 2048], P('section', 'fsdp'), may hold values from -0.109375 to 0.109375
- w_qkv: bfloat16 [2, 2048, 1536], P('section', 'fsdp'), may hold values from -0.125 to 0.125
- w_o: bfloat16 [2, 1024, 2048], P('section', 'fsdp'), may hold values from -1.5 to 1.5
- w_gu: bfloat16 [2, 2048, 8192], P('section', 'fsdp'), may hold values from -0.125 to 0.125
- w_down: bfloat16 [2, 4096, 2048], P('section', 'fsdp'), may hold values from -0.09375 to 0.09375
Outputs:
- layer_outputs: bfloat16 [2, 2, 4, 256, 2048], P('section', None, 'fsdp', 'ctx')
- grad_inputs: bfloat16 [2, 2, 4, 256, 2048], P('section', None, 'fsdp', 'ctx')
- grad_norm_gains: float32 [2, 2, 2048], P('section', None, 'fsdp')
- grad_head_params: float32 [2, 3, 48], P('section', None, 'fsdp')
- grad_conv_params: float32 [2, 5, 3584], P('section', None, 'fsdp')
- grad_ssm_gain: float32 [2, 3072], P('section', 'fsdp')
- grad_w_in: float32 [2, 2048, 6704], P('section', 'fsdp')
- grad_w_out: float32 [2, 3072, 2048], P('section', 'fsdp')
- grad_w_qkv: float32 [2, 2048, 1536], P('section', 'fsdp')
- grad_w_o: float32 [2, 1024, 2048], P('section', 'fsdp')
- grad_w_gu: float32 [2, 2048, 8192], P('section', 'fsdp')
- grad_w_down: float32 [2, 4096, 2048], P('section', 'fsdp')
The draws below stay inside these ranges and needn't reach their ends.
All inputs are finite; a program needn't handle non-finite values.
Results may differ from the reference program's by a relative error of at most 0.024.
Values may be sent and summed in bfloat16 or wider, within the bound.
A program may use at most 448 MiB of HBM per device.

```python
import jax
import jax.numpy as jnp
from jax import lax

D = 2048
FF = 4096
SSM_HEADS = 48
SSM_HEAD = 64
STATE = 256
Q_HEADS = 8
KV_HEADS = 2
HEAD_DIM = 128
CONV_K = 4
MB = 2
D_SSM = 3072
CONV_W = 3584
D_IN = 6704
ATT = 1024
QKV = 1536
SEQ = 256
SEQS = 4
LAYERS = 2


def shard_levels(key, dims, split, least, top_value):
    gain, own = 1.0, jax.random.fold_in(key, 6)
    for dim, blocks in split:
        draws = jnp.exp(jax.random.uniform(jax.random.fold_in(own, dim), (blocks,), jnp.float32, least / len(split), top_value / len(split)))
        gain = gain * jnp.repeat(draws, dims[dim] // blocks).reshape([-1 if axis == dim else 1 for axis in range(len(dims))])
    return gain


def noise(rng, extent, spread, bound, pieces=(), kind=jnp.bfloat16):
    entries = spread * jax.random.normal(rng, extent, jnp.float32)
    if pieces:
        entries = entries * shard_levels(rng, extent, pieces, -0.22, 0.18)
    return jnp.clip(entries, -bound, bound).astype(kind)


def setup_inputs(seed: int = 0) -> dict:
    arg_keys = jax.random.split(jax.random.key(seed), 13)
    inputs = noise(arg_keys[0], (MB, SEQS, SEQ, D), 1.0, 6.0, ((1, 4), (2, 4)))
    cotangent = noise(arg_keys[1], (MB, SEQS, SEQ, D), 1.0, 6.0, ((1, 4), (2, 4)))
    norm_gains = jnp.clip(1.0 + 0.1 * jax.random.normal(arg_keys[2], (LAYERS, 2, D), jnp.float32), 0.5, 1.5).astype(jnp.bfloat16)
    head_params = jnp.clip(-4.0 + 4.0 * jax.random.uniform(arg_keys[3], (LAYERS, 3, SSM_HEADS), jnp.float32) ** shard_levels(arg_keys[3], (LAYERS, 3, SSM_HEADS), ((0, 2), (2, 4)), -0.2, 0.2), -4.0, 0.0).astype(jnp.bfloat16)
    conv_params = jnp.clip(jax.random.uniform(arg_keys[4], (LAYERS, CONV_K + 1, CONV_W), jnp.float32, -0.5, 0.5) * shard_levels(arg_keys[4], (LAYERS, CONV_K + 1, CONV_W), ((0, 2), (2, 4)), -0.4, 0.0), -0.5, 0.5).astype(jnp.bfloat16)
    ssm_gain = jnp.clip(1.0 + 0.1 * jax.random.normal(arg_keys[5], (LAYERS, D_SSM), jnp.float32), 0.5, 1.5).astype(jnp.bfloat16)
    w_in = noise(arg_keys[6], (LAYERS, D, D_IN), D ** -0.5, 0.125, ((0, 2), (1, 4)))
    w_out = noise(arg_keys[7], (LAYERS, D_SSM, D), D_SSM ** -0.5, 0.109375, ((0, 2), (1, 4)))
    w_qkv = noise(arg_keys[8], (LAYERS, D, QKV), D ** -0.5, 0.125, ((0, 2), (1, 4)))
    w_o = noise(arg_keys[9], (LAYERS, ATT, D), (ATT // 64) ** -0.5, 1.5, ((0, 2), (1, 4)))
    w_gu = noise(arg_keys[10], (LAYERS, D, 2 * FF), D ** -0.5, 0.125, ((0, 2), (1, 4)))
    w_down = noise(arg_keys[11], (LAYERS, FF, D), FF ** -0.5, 0.09375, ((0, 2), (1, 4)))
    return dict(inputs=inputs, cotangent=cotangent, norm_gains=norm_gains, head_params=head_params, conv_params=conv_params, ssm_gain=ssm_gain, w_in=w_in, w_out=w_out, w_qkv=w_qkv, w_o=w_o, w_gu=w_gu, w_down=w_down)


@jax.custom_vjp
def low(v):
    return lax.optimization_barrier(v.astype(jnp.bfloat16)).astype(jnp.float32)

@jax.custom_vjp
def low_back(v):
    return v

def low_keep(v):
    return (low(v), None)

def low_pass(kept, grad):
    return (grad,)

def back_keep(v):
    return (v, None)

def back_low(kept, grad):
    return (low(grad),)
low.defvjp(low_keep, low_pass)
low_back.defvjp(back_keep, back_low)
HIGHEST = lax.Precision.HIGHEST
EPSILON = 1e-05
ROPE_BASE = 10000.0
NEGATIVE = -1e+30

def matmul(left_side, right_side):
    return jnp.dot(left_side, right_side, precision=HIGHEST, preferred_element_type=jnp.float32)

def rms_scale(values, gain_row):
    return values * lax.rsqrt(lax.optimization_barrier(jnp.mean(values * values, axis=-1, keepdims=True)) + EPSILON) * gain_row

def rotary(values, head_count):
    length = values.shape[0]
    half_dim = HEAD_DIM // 2
    frequency = ROPE_BASE ** (-jnp.arange(half_dim, dtype=jnp.float32) / half_dim)
    angles = jnp.arange(length, dtype=jnp.float32)[:, None] * frequency[None, :]
    cosine = jnp.cos(angles)[:, None, :]
    sine_part = jnp.sin(angles)[:, None, :]
    halves = values.reshape(length, head_count, 2, half_dim)
    first_half = halves[:, :, 0]
    second_half = halves[:, :, 1]
    turned = jnp.stack([first_half * cosine - second_half * sine_part, second_half * cosine + first_half * sine_part], axis=2)
    return turned.reshape(length, head_count * HEAD_DIM)

def attention(query_in, key_in, value_in):
    length = query_in.shape[0]
    group_size = Q_HEADS // KV_HEADS
    query_heads = query_in.reshape(length, KV_HEADS, group_size, HEAD_DIM)
    key_heads = key_in.reshape(length, KV_HEADS, HEAD_DIM)
    value_heads = value_in.reshape(length, KV_HEADS, HEAD_DIM)
    scores = low_back(jnp.einsum('qkgd,skd->kgqs', query_heads, key_heads, precision=HIGHEST) * HEAD_DIM ** (-0.5))
    position = jnp.arange(length)
    scores = jnp.where(position[:, None] >= position[None, :], scores, NEGATIVE)
    maximum = lax.optimization_barrier(jnp.max(scores, axis=-1, keepdims=True))
    weights = jnp.exp(scores - maximum)
    probabilities = weights / lax.optimization_barrier(jnp.sum(weights, axis=-1, keepdims=True))
    mixed_out = jnp.einsum('kgqs,skd->qkgd', low(probabilities), value_heads, precision=HIGHEST)
    return low_back(low(mixed_out.reshape(length, Q_HEADS * HEAD_DIM)))

def ssd_scan(ssm_input, dt_raw, head_table):
    length = ssm_input.shape[0]
    x_heads = ssm_input[:, :D_SSM].reshape(length, SSM_HEADS, SSM_HEAD)
    b_rows = ssm_input[:, D_SSM:D_SSM + STATE]
    c_rows = ssm_input[:, D_SSM + STATE:]
    dt_step = jax.nn.softplus(dt_raw + head_table[0])
    running = jnp.cumsum(-dt_step * jnp.exp(head_table[1]), axis=0)
    position = jnp.arange(length)
    allowed = (position[:, None] >= position[None, :])[:, :, None]
    log_gap = jnp.where(allowed, running[:, None, :] - running[None, :, :], 0.0)
    decay_table = jnp.where(allowed, jnp.exp(log_gap), 0.0)
    weights = decay_table * matmul(c_rows, b_rows.T)[:, :, None] * dt_step[None, :, :]
    result = jnp.einsum('tsh,shp->thp', weights, x_heads, precision=HIGHEST) + head_table[2][None, :, None] * x_heads
    return result.reshape(length, D_SSM)

def mamba_branch(normed_first, params):
    length = normed_first.shape[0]
    zx_proj = low_back(matmul(normed_first, params['w_in']))
    gate_z = zx_proj[:, :D_SSM]
    xbc_rows = low(zx_proj[:, D_SSM:D_SSM + CONV_W])
    dt_raw = zx_proj[:, D_SSM + CONV_W:]
    conv_table = params['conv_params']
    padded = jnp.pad(xbc_rows, ((CONV_K - 1, 0), (0, 0)))
    running = conv_table[CONV_K]
    for tap_index in range(CONV_K):
        running = running + conv_table[tap_index] * padded[tap_index:tap_index + length]
    ssm_input = low(jax.nn.silu(running))
    ssm_out = ssd_scan(ssm_input, dt_raw, params['head_params'])
    normed_ssm = low(rms_scale(ssm_out * jax.nn.silu(gate_z), params['ssm_gain']))
    return low_back(matmul(normed_ssm, params['w_out']))

def layer_step(hidden_in, params):
    entering = low_back(hidden_in)
    normed_first = low(rms_scale(entering, params['norm_gains'][0]))
    qkv_proj = low_back(matmul(normed_first, params['w_qkv']))
    kv_width = KV_HEADS * HEAD_DIM
    query_in = low(rotary(qkv_proj[:, :ATT], Q_HEADS))
    key_in = low(rotary(qkv_proj[:, ATT:ATT + kv_width], KV_HEADS))
    value_in = low(qkv_proj[:, ATT + kv_width:])
    attn_out = low_back(matmul(attention(query_in, key_in, value_in), params['w_o']))
    mixed_out = mamba_branch(normed_first, params)
    mid_state = entering + attn_out + mixed_out
    normed_second = low(rms_scale(mid_state, params['norm_gains'][1]))
    gate_up = low_back(matmul(normed_second, params['w_gu']))
    activated = low(jax.nn.silu(gate_up[:, :FF]) * gate_up[:, FF:])
    return low(mid_state + low_back(matmul(activated, params['w_down'])))

def reference(inputs, cotangent, norm_gains, head_params, conv_params, ssm_gain, w_in, w_out, w_qkv, w_o, w_gu, w_down):
    param_names = ('norm_gains', 'head_params', 'conv_params', 'ssm_gain', 'w_in', 'w_out', 'w_qkv', 'w_o', 'w_gu', 'w_down')
    arrays = (norm_gains, head_params, conv_params, ssm_gain, w_in, w_out, w_qkv, w_o, w_gu, w_down)
    params = {name_text: array.astype(jnp.float32) for name_text, array in zip(param_names, arrays)}
    begin_state = inputs.astype(jnp.float32).reshape(MB * SEQS, SEQ, D)
    input_probe = jnp.zeros((LAYERS, MB * SEQS, SEQ, D), jnp.float32)

    def forward(probe_values, param_values):
        hidden_state = begin_state
        layer_states = []
        for layer_index in range(LAYERS):
            chosen = {name_text: param_values[name_text][layer_index] for name_text in param_names}
            hidden_state = hidden_state + probe_values[layer_index]
            runner = jax.checkpoint(lambda sequence, chosen=chosen: layer_step(sequence, chosen))
            hidden_state = lax.map(runner, hidden_state)
            layer_states.append(hidden_state)
        return jnp.stack(layer_states)
    layer_states, pull_back = jax.vjp(forward, input_probe, params)
    cot_full = jnp.zeros_like(layer_states).at[LAYERS - 1].set(cotangent.astype(jnp.float32).reshape(MB * SEQS, SEQ, D))
    grad_probe, grad_params = pull_back(cot_full)
    full_shape = (LAYERS, MB, SEQS, SEQ, D)
    return (layer_states.reshape(full_shape).astype(jnp.bfloat16), grad_probe.reshape(full_shape).astype(jnp.bfloat16), grad_params['norm_gains'], grad_params['head_params'], grad_params['conv_params'], grad_params['ssm_gain'], grad_params['w_in'], grad_params['w_out'], grad_params['w_qkv'], grad_params['w_o'], grad_params['w_gu'], grad_params['w_down'])
```

```python
import functools

import jax
import jax.numpy as jnp
from jax import lax
from jax.experimental import pallas as pl
from jax.experimental.pallas import tpu as pltpu
from jax.sharding import Mesh
from jax.sharding import PartitionSpec as P

D = 2048
FF = 4096
SSM_HEADS = 48
SSM_HEAD = 64
STATE = 256
Q_HEADS = 8
KV_HEADS = 2
HEAD_DIM = 128
CONV_K = 4
D_SSM = 3072
CONV_W = 3584
D_IN = 6704
ATT = 1024
KV = 256
EPSILON = 1e-05
ROPE_BASE = 10000.0
NEGATIVE = -1e30
HIGHEST = lax.Precision.HIGHEST

RANKS = 4
R_HEADS = SSM_HEADS // RANKS
R_SSM = D_SSM // RANKS
R_BC = 2 * STATE // RANKS
R_CONV = R_SSM + R_BC
R_ATT = ATT // RANKS
R_FF = FF // RANKS
R_OUT = R_SSM + R_ATT
HALF = 1024
MESH = pl.DeviceIdType.MESH
BF = jnp.bfloat16
F32 = jnp.float32


def rank_place():
    return 2 * lax.axis_index("section") + lax.axis_index("y")


def rank_id(rank):
    return {"section": rank // 2, "y": lax.rem(rank, 2)}


def greet(me):
    barrier = pltpu.get_barrier_semaphore()
    for step in range(1, RANKS):
        pl.semaphore_signal(
            barrier, inc=1, device_id=rank_id(lax.rem(me + step, RANKS)), device_id_type=MESH
        )
    pl.semaphore_wait(barrier, RANKS - 1)


def swap_kernel(with_stat, *refs):
    if with_stat:
        send_ref, stat_ref, out_ref, all_stat_ref, send_sem, recv_sem, stat_send, stat_recv = refs
    else:
        send_ref, out_ref, send_sem, recv_sem = refs
    me = rank_place()
    greet(me)
    copies = []
    for step in range(1, RANKS):
        other = lax.rem(me + step, RANKS)
        copies.append(
            pltpu.make_async_remote_copy(
                src_ref=send_ref.at[other] if len(send_ref.shape) == 3 else send_ref,
                dst_ref=out_ref.at[me],
                send_sem=send_sem.at[step - 1],
                recv_sem=recv_sem.at[step - 1],
                device_id=rank_id(other),
                device_id_type=MESH,
            )
        )
        if with_stat:
            copies.append(
                pltpu.make_async_remote_copy(
                    src_ref=stat_ref,
                    dst_ref=all_stat_ref.at[me],
                    send_sem=stat_send.at[step - 1],
                    recv_sem=stat_recv.at[step - 1],
                    device_id=rank_id(other),
                    device_id_type=MESH,
                )
            )
    for copy in copies:
        copy.start()
    if len(send_ref.shape) == 3:
        out_ref[me] = send_ref[me]
    else:
        out_ref[me] = send_ref[...]
    if with_stat:
        all_stat_ref[me] = stat_ref[...]
    for copy in copies:
        copy.wait()


VMEM_SPEC = pl.BlockSpec(memory_space=pltpu.VMEM)


def swap(values, collective_id, stat=None):
    out_shape = [jax.ShapeDtypeStruct((RANKS,) + values.shape[-2:], values.dtype)]
    scratch = [pltpu.SemaphoreType.DMA((RANKS - 1,)), pltpu.SemaphoreType.DMA((RANKS - 1,))]
    args = [values]
    if stat is not None:
        out_shape.append(jax.ShapeDtypeStruct((RANKS,) + stat.shape, stat.dtype))
        scratch += scratch
        args.append(stat)
    out = pl.pallas_call(
        functools.partial(swap_kernel, stat is not None),
        out_shape=out_shape,
        in_specs=[VMEM_SPEC] * len(args),
        out_specs=[VMEM_SPEC] * len(out_shape),
        scratch_shapes=scratch,
        compiler_params=pltpu.CompilerParams(
            collective_id=collective_id, has_side_effects=True, vmem_limit_bytes=32 * 2**20
        ),
    )(*args)
    return out if stat is not None else out[0]


def scatter_sum(me, rows, part_ref, slots, send_sem, recv_sem):
    copies = []
    for step in range(1, RANKS):
        other = lax.rem(me + step, RANKS)
        copies.append(
            pltpu.make_async_remote_copy(
                src_ref=part_ref.at[pl.ds(pl.multiple_of(other * rows, rows), rows)],
                dst_ref=slots.at[step - 1],
                send_sem=send_sem.at[step - 1],
                recv_sem=recv_sem.at[step - 1],
                device_id=rank_id(other),
                device_id_type=MESH,
            )
        )
    for copy in copies:
        copy.start()
    total = part_ref[pl.ds(pl.multiple_of(me * rows, rows), rows), :].astype(F32)
    for step, copy in enumerate(copies):
        copy.wait()
        total = total + slots[step].astype(F32)
    return total


def spread(me, rows, out_ref, send_sem, recv_sem):
    here = pl.ds(pl.multiple_of(me * rows, rows), rows)
    copies = []
    for step in range(1, RANKS):
        copies.append(
            pltpu.make_async_remote_copy(
                src_ref=out_ref.at[here],
                dst_ref=out_ref.at[here],
                send_sem=send_sem.at[step - 1],
                recv_sem=recv_sem.at[step - 1],
                device_id=rank_id(lax.rem(me + step, RANKS)),
                device_id_type=MESH,
            )
        )
    for copy in copies:
        copy.start()
    for copy in copies:
        copy.wait()


def mid_kernel(part_ref, resid_ref, gain_ref, mid_ref, out_ref, slots, s1, r1, s2, r2):
    rows = resid_ref.shape[0]
    me = rank_place()
    greet(me)
    mid = scatter_sum(me, rows, part_ref, slots, s1, r1) + resid_ref[...].astype(F32)
    mid_ref[...] = mid
    scale = lax.rsqrt(jnp.mean(mid * mid, axis=-1, keepdims=True) + EPSILON)
    out_ref[pl.ds(pl.multiple_of(me * rows, rows), rows), :] = (
        mid * scale * gain_ref[...].astype(F32)
    ).astype(BF)
    spread(me, rows, out_ref, s2, r2)


def end_kernel(part_ref, resid_ref, out_ref, slots, s1, r1, s2, r2):
    rows = resid_ref.shape[0]
    me = rank_place()
    greet(me)
    total = scatter_sum(me, rows, part_ref, slots, s1, r1) + resid_ref[...]
    out_ref[pl.ds(pl.multiple_of(me * rows, rows), rows), :] = total.astype(BF)
    spread(me, rows, out_ref, s2, r2)


def back_kernel(
    part_ref, given_ref, value_ref, gain_ref, wide_ref, out_ref, gain_grad_ref, slots, s1, r1, s2, r2
):
    rows = given_ref.shape[0]
    me = rank_place()
    greet(me)
    grad = scatter_sum(me, rows, part_ref, slots, s1, r1)
    value = value_ref[...]
    scale = lax.rsqrt(jnp.mean(value * value, axis=-1, keepdims=True) + EPSILON)
    unit = value * scale
    gain_grad_ref[...] = jnp.sum(grad * unit, axis=0, keepdims=True)
    scaled = grad * gain_ref[...].astype(F32)
    total = given_ref[...] + scale * (
        scaled - unit * jnp.mean(scaled * unit, axis=-1, keepdims=True)
    )
    wide_ref[...] = total
    out_ref[pl.ds(pl.multiple_of(me * rows, rows), rows), :] = total.astype(BF)
    spread(me, rows, out_ref, s2, r2)


def rank_call(kernel, out_shape, collective_id, rows, *args):
    return pl.pallas_call(
        kernel,
        out_shape=out_shape,
        in_specs=[VMEM_SPEC] * len(args),
        out_specs=[VMEM_SPEC] * len(out_shape),
        scratch_shapes=[pltpu.VMEM((RANKS - 1, rows, D), BF)]
        + [pltpu.SemaphoreType.DMA((RANKS - 1,))] * 4,
        compiler_params=pltpu.CompilerParams(
            collective_id=collective_id, has_side_effects=True, vmem_limit_bytes=32 * 2**20
        ),
    )(*args)


def mid_step(part, resid, gain):
    rows = resid.shape[0]
    return rank_call(
        mid_kernel,
        [jax.ShapeDtypeStruct((rows, D), F32), jax.ShapeDtypeStruct(part.shape, BF)],
        3,
        rows,
        part,
        resid,
        gain[None],
    )


def end_step(part, resid):
    rows = resid.shape[0]
    return rank_call(end_kernel, [jax.ShapeDtypeStruct(part.shape, BF)], 4, rows, part, resid)[0]


def back_step(part, given, value, gain):
    rows = given.shape[0]
    return rank_call(
        back_kernel,
        [
            jax.ShapeDtypeStruct((rows, D), F32),
            jax.ShapeDtypeStruct(part.shape, BF),
            jax.ShapeDtypeStruct((1, D), F32),
        ],
        5,
        rows,
        part,
        given,
        value,
        gain[None],
    )


def narrow(values):
    return values.astype(BF)


def dot(left, right):
    return jnp.dot(left, right, preferred_element_type=F32)


def dot_t(left, right):
    return lax.dot_general(left, right, (((1,), (1,)), ((), ())), preferred_element_type=F32)


def t_dot(left, right):
    return lax.dot_general(left, right, (((0,), (0,)), ((), ())), preferred_element_type=F32)


def columns(array, start, width):
    return lax.dynamic_slice_in_dim(array, start, width, axis=1)


def cut_rows(array, start, width):
    return lax.dynamic_slice_in_dim(array, start, width, axis=0)


def rms(values, gain):
    return values * lax.rsqrt(jnp.mean(values * values, axis=-1, keepdims=True) + EPSILON) * gain


def rotary(values, turning):
    length, width = values.shape
    half = HEAD_DIM // 2
    frequency = ROPE_BASE ** (-jnp.arange(half, dtype=F32) / half)
    angles = jnp.arange(length, dtype=F32)[:, None] * frequency[None, :]
    cosine = jnp.cos(angles)[:, None, :]
    sine = turning * jnp.sin(angles)[:, None, :]
    halves = values.reshape(length, width // HEAD_DIM, 2, half)
    first, second = halves[:, :, 0], halves[:, :, 1]
    return jnp.stack(
        [first * cosine - second * sine, second * cosine + first * sine], axis=2
    ).reshape(length, width)


def causal(length):
    position = jnp.arange(length)
    return position[:, None] >= position[None, :]


def shifted(values, steps):
    if steps == 0:
        return values
    blank = jnp.zeros((abs(steps), values.shape[1]), values.dtype)
    if steps > 0:
        return jnp.concatenate([blank, values[:-steps]], axis=0)
    return jnp.concatenate([values[-steps:], blank], axis=0)


def conv_sum(rows, table):
    wide = rows.astype(F32)
    total = table[CONV_K][None, :]
    for tap in range(CONV_K):
        total = total + table[tap][None, :] * shifted(wide, CONV_K - 1 - tap)
    return total


def decays(dt_raw, heads):
    dt = jax.nn.softplus(dt_raw + heads[0][None, :])
    step = -dt * jnp.exp(heads[1])[None, :]
    length = dt.shape[0]
    running = jnp.dot(causal(length).astype(F32), step, precision=HIGHEST)
    return dt, step, running


def decay_table(running):
    length = running.shape[0]
    turned = running.T
    gap = turned[:, :, None] - turned[:, None, :]
    return jnp.exp(jnp.where(causal(length)[None], gap, NEGATIVE))


def by_head(values):
    return values.reshape(values.shape[0], R_HEADS, SSM_HEAD)


def scan_forward(x, b_rows, c_rows, dt_raw, heads):
    dt, _, running = decays(dt_raw, heads)
    mixing = dot_t(c_rows, b_rows)
    weights = narrow(decay_table(running) * mixing[None] * dt.T[:, None, :])
    x_heads = by_head(x)
    result = jnp.einsum("hts,shp->thp", weights, x_heads, preferred_element_type=F32)
    return (result + heads[2][None, :, None] * x_heads.astype(F32)).reshape(x.shape)


def scan_backward(x, b_rows, c_rows, dt_raw, heads, grad_y):
    dt, step, running = decays(dt_raw, heads)
    length = x.shape[0]
    mixing = dot_t(c_rows, b_rows)
    table = decay_table(running)
    dt_t = dt.T
    x_heads = by_head(x)
    grad_heads = by_head(narrow(grad_y))
    grad_weights = jnp.einsum("thp,shp->hts", grad_heads, x_heads, preferred_element_type=F32)
    faded = grad_weights * table
    weights = table * mixing[None] * dt_t[:, None, :]
    grad_x = jnp.einsum("hts,thp->shp", narrow(weights), grad_heads, preferred_element_type=F32)
    grad_y_heads = by_head(grad_y)
    grad_x = grad_x + heads[2][None, :, None] * grad_y_heads
    grad_skip = jnp.sum(grad_y_heads * x_heads.astype(F32), axis=(0, 2))
    grad_mixing = narrow(jnp.sum(faded * dt_t[:, None, :], axis=0))
    grad_c = dot(grad_mixing, b_rows)
    grad_b = t_dot(grad_mixing, c_rows)
    plain = faded * mixing[None]
    grad_dt = jnp.sum(plain, axis=1)
    grad_gap = plain * dt_t[:, None, :]
    grad_running = jnp.sum(grad_gap, axis=2) - jnp.sum(grad_gap, axis=1)
    grad_step = jnp.dot(grad_running, causal(length).astype(F32), precision=HIGHEST).T
    grad_dt = grad_dt.T - grad_step * jnp.exp(heads[1])[None, :]
    grad_log = jnp.sum(grad_step * step, axis=0)
    grad_raw = grad_dt * jax.nn.sigmoid(dt_raw + heads[0][None, :])
    grad_table = jnp.stack([jnp.sum(grad_raw, axis=0), grad_log, grad_skip])
    return grad_x.reshape(x.shape), grad_b, grad_c, grad_raw, grad_table


def attend(query, key, value):
    length = query.shape[0]
    heads = query.reshape(length, -1, HEAD_DIM)
    scores = jnp.einsum("qhd,sd->hqs", heads, key, preferred_element_type=F32) * HEAD_DIM**-0.5
    scores = jnp.where(causal(length)[None], scores, NEGATIVE)
    weights = jnp.exp(scores - jnp.max(scores, axis=-1, keepdims=True))
    probs = weights / jnp.sum(weights, axis=-1, keepdims=True)
    mixed = jnp.einsum("hqs,sd->qhd", narrow(probs), value, preferred_element_type=F32)
    return narrow(mixed.reshape(query.shape)), probs


def attend_back(query, key, value, probs, grad_out):
    length = query.shape[0]
    heads = query.reshape(length, -1, HEAD_DIM)
    grad_heads = grad_out.reshape(length, -1, HEAD_DIM)
    grad_probs = jnp.einsum("qhd,sd->hqs", grad_heads, value, preferred_element_type=F32)
    grad_scores = narrow(
        probs * (grad_probs - jnp.sum(probs * grad_probs, axis=-1, keepdims=True))
    )
    scale = HEAD_DIM**-0.5
    grad_query = jnp.einsum("hqs,sd->qhd", grad_scores, key, preferred_element_type=F32) * scale
    grad_key = jnp.einsum("hqs,qhd->sd", grad_scores, heads, preferred_element_type=F32) * scale
    grad_value = jnp.einsum("hqs,qhd->sd", narrow(probs), grad_heads, preferred_element_type=F32)
    return grad_query.reshape(query.shape), grad_key, grad_value


def flip(value, axis):
    return lax.ppermute(value, axis, [(0, 1), (1, 0)])


def layer_forward(entering, resid, weights, small, first):
    s, y = lax.axis_index("section"), lax.axis_index("y")
    length = entering.shape[0]
    x1 = narrow(rms(entering.astype(F32), small["gain0"][None, :]))
    left = dot(x1, weights["in"][0])
    right = dot(x1, weights["in"][1])
    dt_raw = columns(dot(x1, weights["dt"]), R_HEADS * (2 * s + y), R_HEADS)
    xbc = narrow(left[:, :R_CONV])
    u = narrow(jax.nn.silu(conv_sum(xbc, small["conv"])))
    kv_raw = left[:, R_CONV:]
    kv = narrow(jnp.where(y == 0, rotary(kv_raw, 1.0), kv_raw))
    shared = swap(jnp.concatenate([u[:, R_SSM:], kv], axis=1), 0)
    b_rows = jnp.concatenate([shared[0, :, :R_BC], shared[1, :, :R_BC]], axis=1)
    c_rows = jnp.concatenate([shared[2, :, :R_BC], shared[3, :, :R_BC]], axis=1)
    pair = lax.dynamic_slice_in_dim(shared, 2 * s, 2, axis=0)[:, :, R_BC:]
    key, value = pair[0], pair[1]
    z = right[:, :R_SSM]
    query = narrow(rotary(right[:, R_SSM:], 1.0))
    o, probs = attend(query, key, value)
    x = u[:, :R_SSM]
    scan = scan_forward(x, b_rows, c_rows, dt_raw, small["heads"])
    gated = scan * jax.nn.silu(z)
    squares = jnp.sum(gated * gated, axis=1)
    scaled = narrow(gated * small["ssm_gain"][None, :])
    message = to_rows(scaled, o)
    stat = jnp.broadcast_to(squares[None, :], (8, length))
    got, stats = swap(message, 1, stat)
    spread_of = lax.rsqrt(jnp.sum(stats[:, 0, :], axis=0) / D_SSM + EPSILON)
    wide = jnp.transpose(got, (1, 0, 2)).reshape(length, R_OUT)
    is_ssm = small["is_ssm"][None, :]
    mo = narrow(jnp.where(is_ssm, wide.astype(F32) * spread_of[:, None], wide.astype(F32)))
    part = jnp.concatenate([dot(mo, weights["out"][0]), dot(mo, weights["out"][1])], axis=1)
    mid, x2 = mid_step(narrow(part), resid, small["gain1"])
    gate = dot(x2, weights["gu"][0])
    up = dot(x2, weights["gu"][1])
    act = narrow(jax.nn.silu(gate) * up)
    part2 = jnp.concatenate([dot(act, weights["down"][0]), dot(act, weights["down"][1])], axis=1)
    leaving = end_step(narrow(part2), mid)
    kept = dict(
        resid=resid, x1=x1, xbc=xbc, u=u, b=b_rows, c=c_rows, key=key, value=value, query=query,
        probs=probs, z=z, dt_raw=dt_raw, scan=scan, spread=spread_of, mo=mo, mid=mid, x2=x2,
        gate=gate, up=up, act=act,
    )
    return leaving, kept


def to_rows(ssm_part, att_part):
    length = ssm_part.shape[0]
    nz = lax.axis_size("fsdp")
    inner = nz // RANKS
    a = ssm_part.reshape(length, inner, RANKS, R_SSM // nz)
    b = att_part.reshape(length, inner, RANKS, R_ATT // nz)
    both = jnp.concatenate([a, b], axis=3)
    return jnp.transpose(both, (2, 0, 1, 3)).reshape(RANKS, length, R_OUT // RANKS)


def from_rows(got):
    length = got.shape[1]
    nz = lax.axis_size("fsdp")
    inner = nz // RANKS
    both = jnp.transpose(got.reshape(RANKS, length, inner, R_OUT // nz), (1, 2, 0, 3))
    a = both[..., : R_SSM // nz].reshape(length, R_SSM)
    b = both[..., R_SSM // nz :].reshape(length, R_ATT)
    return a, b


def layer_backward(grad, given, kept, weights, small):
    s, y = lax.axis_index("section"), lax.axis_index("y")
    core = lax.axis_index("core")
    length = grad.shape[0]
    down, gu, out, win = weights["down"], weights["gu"], weights["out"], weights["in"]

    def product(left, right, order):
        mine = jnp.where(core == 0, right[0], right[1])
        theirs = jnp.where(core == 0, right[1], right[0])
        left_two = jnp.concatenate([left, flip(left, "core")], axis=0)
        right_two = jnp.concatenate([mine, flip(theirs, "core")], axis=0)
        return narrow(t_dot(left_two, right_two))

    halves = lambda v: (v[:, :HALF], v[:, HALF:])
    g0, g1 = halves(grad)
    grad_act = dot_t(g0, down[0]) + dot_t(g1, down[1])
    gate, up = kept["gate"], kept["up"]
    sig = jax.nn.sigmoid(gate)
    d_gate = narrow(grad_act * up * (sig * (1.0 + gate * (1.0 - sig))))
    d_up = narrow(grad_act * gate * sig)
    part = dot_t(d_gate, gu[0]) + dot_t(d_up, gu[1])
    d_mid, db, grad_gain1 = back_step(narrow(part), given, kept["mid"], small["gain1"])
    b0, b1 = halves(db)
    d_mo = dot_t(b0, out[0]) + dot_t(b1, out[1])
    mo = kept["mo"]
    is_ssm = small["is_ssm"][None, :]
    stat_row = jnp.sum(jnp.where(is_ssm, d_mo * mo.astype(F32), 0.0), axis=1)
    stat = jnp.broadcast_to(stat_row[None, :], (8, length))
    blocks = jnp.transpose(narrow(d_mo).reshape(length, RANKS, R_OUT // RANKS), (1, 0, 2))
    got, stats = swap(blocks, 1, stat)
    overlap = jnp.sum(stats[:, 0, :], axis=0)[:, None]
    d_norm, d_o = from_rows(got)
    d_norm = d_norm.astype(F32)
    spread_of = kept["spread"][:, None]
    scan, z = kept["scan"], kept["z"]
    sig_z = jax.nn.sigmoid(z)
    silu_z = z * sig_z
    gated = scan * silu_z
    grad_ssm_gain = jnp.sum(d_norm * gated * spread_of, axis=0)
    d_gated = spread_of * d_norm * small["ssm_gain"][None, :] - gated * (
        spread_of * spread_of * overlap * (1.0 / D_SSM)
    )
    d_scan = d_gated * silu_z
    d_z = d_gated * scan * (sig_z * (1.0 + z * (1.0 - sig_z)))
    d_query, d_key, d_value = attend_back(
        kept["query"], kept["key"], kept["value"], kept["probs"], d_o
    )
    u = kept["u"]
    d_x, d_b, d_c, d_dt, grad_heads = scan_backward(
        u[:, :R_SSM], kept["b"], kept["c"], kept["dt_raw"], small["heads"], d_scan
    )
    message = jnp.stack(
        [
            jnp.concatenate([d_b[:, :R_BC], d_key], axis=1),
            jnp.concatenate([d_b[:, R_BC:], d_value], axis=1),
            jnp.concatenate([d_c[:, :R_BC], d_key], axis=1),
            jnp.concatenate([d_c[:, R_BC:], d_value], axis=1),
        ]
    )
    back = swap(narrow(message), 2).astype(F32)
    d_bc = back[0, :, :R_BC] + back[1, :, :R_BC] + back[2, :, :R_BC] + back[3, :, :R_BC]
    d_kv = jnp.sum(lax.dynamic_slice_in_dim(back, 2 * s, 2, axis=0)[:, :, R_BC:], axis=0)
    d_kv = jnp.where(y == 0, rotary(d_kv, -1.0), d_kv)
    d_u = jnp.concatenate([d_x, d_bc], axis=1)
    xbc = kept["xbc"]
    table = small["conv"]
    before = conv_sum(xbc, table)
    sig_c = jax.nn.sigmoid(before)
    d_before = d_u * (sig_c * (1.0 + before * (1.0 - sig_c)))
    wide = xbc.astype(F32)
    grad_conv = jnp.stack(
        [jnp.sum(d_before * shifted(wide, CONV_K - 1 - tap), axis=0) for tap in range(CONV_K)]
        + [jnp.sum(d_before, axis=0)]
    )
    d_xbc = 0.0
    for tap in range(CONV_K):
        d_xbc = d_xbc + table[tap][None, :] * shifted(d_before, tap - CONV_K + 1)
    d_left = narrow(jnp.concatenate([d_xbc, d_kv], axis=1))
    d_right = narrow(jnp.concatenate([d_z, rotary(d_query, -1.0)], axis=1))
    d_dt_b = narrow(d_dt)
    dt_own = columns(weights["dt"], R_HEADS * (2 * s + y), R_HEADS)
    part = dot_t(d_left, win[0]) + dot_t(d_right, win[1]) + dot_t(d_dt_b, dt_own)
    _, entering_grad, grad_gain0 = back_step(
        narrow(part), d_mid, kept["resid"].astype(F32), small["gain0"]
    )
    shards = dict(
        down=product(kept["act"], (g0, g1), 0),
        gu=product(kept["x2"], (d_gate, d_up), 1),
        out=product(mo, (b0, b1), 2),
    )
    shards["in"] = product(kept["x1"], (d_left, d_right), 3)
    grad_dt_w = t_dot(kept["x1"], d_dt_b)
    ranked = jnp.concatenate(
        [grad_heads.reshape(-1), grad_conv.reshape(-1), grad_ssm_gain, grad_dt_w.reshape(-1)]
    )
    gains = jnp.concatenate([grad_gain0[0], grad_gain1[0]])
    return entering_grad, shards, ranked, gains


def body(
    inputs, cotangent, norm_gains, head_params, conv_params, ssm_gain,
    w_in, w_out, w_qkv, w_o, w_gu, w_down,
):
    s, y = lax.axis_index("section"), lax.axis_index("y")
    core = lax.axis_index("core")
    nz = lax.axis_size("fsdp")
    z_place = lax.axis_index("fsdp")
    rank = 2 * s + y
    rows = inputs.shape[2]
    length = RANKS * rows
    w_in, w_out, w_qkv, w_o, w_gu, w_down = (
        w[0] for w in (w_in, w_out, w_qkv, w_o, w_gu, w_down)
    )

    flat = jnp.concatenate(
        [
            norm_gains[0].reshape(-1),
            head_params[0].reshape(-1),
            conv_params[0].reshape(-1),
            ssm_gain[0],
            w_in[:, D_SSM + CONV_W :].reshape(-1),
        ]
    )
    everything = lax.all_gather(flat, ("section", "fsdp"), axis=0).reshape(2, nz, -1)

    def unpack(layer):
        part = everything[layer]
        sizes = [2 * D // nz, 3 * SSM_HEADS // nz, 5 * CONV_W // nz, D_SSM // nz]
        starts = [0]
        for size in sizes:
            starts.append(starts[-1] + size)
        join = lambda k, lead: jnp.transpose(
            part[:, starts[k] : starts[k + 1]].reshape(nz, lead, -1), (1, 0, 2)
        ).reshape(lead, -1).astype(F32)
        gains, heads, conv, gain = join(0, 2), join(1, 3), join(2, 5), join(3, 1)[0]
        conv_own = jnp.concatenate(
            [columns(conv, R_SSM * rank, R_SSM), columns(conv, D_SSM + R_BC * rank, R_BC)], axis=1
        )
        channel = jnp.arange(R_OUT) % (R_OUT // nz)
        small = dict(
            gain0=gains[0],
            gain1=gains[1],
            heads=columns(heads, R_HEADS * rank, R_HEADS),
            conv=conv_own,
            ssm_gain=lax.dynamic_slice_in_dim(gain, R_SSM * rank, R_SSM),
            is_ssm=channel < R_SSM // nz,
        )
        return small, part[:, starts[4] :].reshape(D, SSM_HEADS)

    def pieces(section):
        rk = 2 * section + y
        first = columns(w_in, jnp.where(core == 0, D_SSM, 0) + R_SSM * rk, R_SSM)
        second = jnp.where(
            core == 0,
            columns(w_in, 2 * D_SSM + R_BC * rk, R_BC),
            columns(w_qkv, R_ATT * rk, HEAD_DIM),
        )
        third = columns(
            w_qkv,
            jnp.where(core == 0, ATT + KV * y + HEAD_DIM * section, R_ATT * rk + HEAD_DIM),
            HEAD_DIM,
        )
        side = HALF * core
        out_rows, o_rows, down_rows = R_SSM // nz, R_ATT // nz, R_FF // nz
        ff = R_FF // nz
        return {
            "in": jnp.concatenate([first, second, third], axis=1),
            "out": jnp.concatenate(
                [
                    lax.dynamic_slice(w_out, (out_rows * rk, side), (out_rows, HALF)),
                    lax.dynamic_slice(w_o, (o_rows * rk, side), (o_rows, HALF)),
                ],
                axis=0,
            ),
            "gu": jnp.concatenate(
                [
                    columns(w_gu, FF * core + (FF // nz) * k + ff * rk, ff) for k in range(nz)
                ],
                axis=1,
            ),
            "down": lax.dynamic_slice(w_down, (down_rows * rk, side), (down_rows, HALF)),
        }

    names = ("in", "out", "gu", "down")
    own, other = pieces(s), pieces(1 - s)
    arrived = {name: flip(other[name], "section") for name in names}

    def gathered(layer):
        result = {}
        for name in names:
            piece = jnp.where(s == layer, own[name], arrived[name])
            whole = lax.all_gather(piece, ("core", "fsdp"), axis=0)
            result[name] = whole.reshape(2, nz * piece.shape[0], HALF)
        return result

    def whole_sequence(own_rows):
        place = 2 * y + core
        result = jnp.zeros((RANKS, rows, D), BF)
        result = lax.dynamic_update_index_in_dim(
            result, lax.dynamic_index_in_dim(own_rows, core, 0, False), place, 0
        )
        for dy, dc in ((0, 1), (1, 0), (1, 1)):
            sent = lax.dynamic_index_in_dim(own_rows, core ^ dc, 0, False)
            pairs = [
                (2 * a + b, 2 * (a ^ dy) + (b ^ dc)) for a in range(2) for b in range(2)
            ]
            here = lax.ppermute(sent, ("y", "core"), pairs)
            result = lax.dynamic_update_index_in_dim(
                result, here, 2 * (y ^ dy) + (core ^ dc), 0
            )
        return result.reshape(length, D)

    def rank_rows(whole):
        return cut_rows(whole, rows * rank, rows)

    smalls = []
    weights = []
    for layer in range(2):
        small, dt_w = unpack(layer)
        smalls.append(small)
        weights.append(dict(gathered(layer), dt=dt_w))
    hidden = whole_sequence(inputs[:, 0])
    grad = whole_sequence(cotangent[:, 0])
    outs, kept = [], []
    for layer in range(2):
        hidden, keep = layer_forward(
            hidden, rank_rows(hidden), weights[layer], smalls[layer], layer == 0
        )
        outs.append(hidden)
        kept.append(keep)
    grads = [None, None]
    shards, ranked, gains = [None, None], [None, None], [None, None]
    for layer in (1, 0):
        grad, shards[layer], ranked[layer], gains[layer] = layer_backward(
            grad, rank_rows(grad).astype(F32), kept[layer], weights[layer], smalls[layer]
        )
        grads[layer] = grad

    def block_rows(pair):
        chosen = jnp.where(s == 0, pair[0], pair[1]).reshape(RANKS, rows, D)
        mine = lax.dynamic_index_in_dim(chosen, 2 * y + core, 0, False)
        sent = lax.dynamic_index_in_dim(chosen, 2 * y + (1 - core), 0, False)
        theirs = flip(sent, "core")
        both = jnp.where(core == 0, jnp.stack([mine, theirs]), jnp.stack([theirs, mine]))
        return both[None, :, None]

    def assembled(name):
        parts = []
        for layer in (1, 0):
            blocks = shards[layer][name]
            parts.append(lax.psum_scatter(blocks, "fsdp", scatter_dimension=0, tiled=True))
        one, zero = parts
        mine = jnp.where(s == 0, zero, one)
        sent = jnp.where(s == 0, one, zero)
        theirs = flip(sent, "section")
        both = jnp.where(s == 0, jnp.stack([mine, theirs]), jnp.stack([theirs, mine]))
        whole = lax.all_gather(both, ("y", "core"), axis=0)
        return whole.reshape(2, 2, 2, blocks.shape[0] // nz, HALF)

    ranks = [(a, b) for a in range(2) for b in range(2)]

    def by_rank(whole, rk, side):
        return whole[rk[1], side, rk[0]]

    got_down = assembled("down")
    got_gu = assembled("gu")
    got_out = assembled("out")
    got_in = assembled("in")

    out_rows, o_rows = R_SSM // nz, R_ATT // nz
    rows_of = lambda whole, lo, hi: jnp.concatenate(
        [
            jnp.concatenate([by_rank(whole, rk, side)[lo:hi] for side in range(2)], axis=1)
            for rk in ranks
        ],
        axis=0,
    ).astype(F32)
    grad_w_down = rows_of(got_down, 0, R_FF // nz)
    grad_w_out = rows_of(got_out, 0, out_rows)
    grad_w_o = rows_of(got_out, out_rows, out_rows + o_rows)
    ff = R_FF // nz
    grad_w_gu = jnp.concatenate(
        [
            by_rank(got_gu, rk, side)[:, ff * k : ff * (k + 1)]
            for side in range(2)
            for k in range(nz)
            for rk in ranks
        ],
        axis=1,
    ).astype(F32)

    vector = jnp.concatenate([ranked[0], ranked[1], gains[0], gains[1]])
    count = vector.shape[0]
    padded = jnp.pad(vector, (0, -count % 1024)).reshape(-1, 128)
    summed = lax.psum(padded, ("core", "fsdp"))
    all_ranks = lax.all_gather(summed, ("section", "y"), axis=0).reshape(RANKS, -1)
    per = ranked[0].shape[0]
    mine = jnp.where(s == 0, all_ranks[:, :per], all_ranks[:, per : 2 * per])
    gain_all = jnp.sum(all_ranks[:, 2 * per : 2 * per + 4 * D], axis=0).reshape(2, 2, D)
    gain_mine = jnp.where(s == 0, gain_all[0], gain_all[1])
    a0 = 3 * R_HEADS
    a1 = a0 + 5 * R_CONV
    a2 = a1 + R_SSM
    head_all = jnp.concatenate([mine[k, :a0].reshape(3, R_HEADS) for k in range(RANKS)], axis=1)
    convs = [mine[k, a0:a1].reshape(5, R_CONV) for k in range(RANKS)]
    conv_all = jnp.concatenate(
        [c[:, :R_SSM] for c in convs] + [c[:, R_SSM:] for c in convs], axis=1
    )
    ssm_all = mine[:, a1:a2].reshape(-1)
    dt_all = jnp.concatenate([mine[k, a2:].reshape(D, R_HEADS) for k in range(RANKS)], axis=1)

    def shard(array, axis):
        width = array.shape[axis] // nz
        return lax.dynamic_slice_in_dim(array, width * z_place, width, axis)

    grad_w_in = jnp.concatenate(
        [by_rank(got_in, rk, 1)[:, :R_SSM].astype(F32) for rk in ranks]
        + [by_rank(got_in, rk, 0)[:, :R_SSM].astype(F32) for rk in ranks]
        + [by_rank(got_in, rk, 0)[:, R_SSM:R_CONV].astype(F32) for rk in ranks]
        + [shard(dt_all, 0)],
        axis=1,
    )
    grad_w_qkv = jnp.concatenate(
        [by_rank(got_in, rk, 1)[:, R_SSM:] for rk in ranks]
        + [by_rank(got_in, (head, part), 0)[:, R_CONV:] for part in range(2) for head in range(2)],
        axis=1,
    ).astype(F32)
    return (
        block_rows(outs),
        block_rows(grads),
        shard(gain_mine, 1)[None],
        shard(head_all, 1)[None],
        shard(conv_all, 1)[None],
        shard(ssm_all, 0)[None],
        grad_w_in[None],
        grad_w_out[None],
        grad_w_qkv[None],
        grad_w_o[None],
        grad_w_gu[None],
        grad_w_down[None],
    )


def solution(mesh):
    sections, ctx, fsdp = mesh.devices.shape
    fine = Mesh(
        mesh.devices.reshape(sections, ctx // 2, 2, fsdp), ("section", "y", "core", "fsdp")
    )
    tokens = ("y", "core")
    in_specs = (
        P(None, "fsdp", tokens, None),
        P(None, "fsdp", tokens, None),
        P("section", None, "fsdp"),
        P("section", None, "fsdp"),
        P("section", None, "fsdp"),
        P("section", "fsdp"),
    ) + (P("section", "fsdp", None),) * 6
    out_specs = (
        P("section", None, "fsdp", tokens, None),
        P("section", None, "fsdp", tokens, None),
        P("section", None, "fsdp"),
        P("section", None, "fsdp"),
        P("section", None, "fsdp"),
        P("section", "fsdp"),
    ) + (P("section", "fsdp", None),) * 6
    return jax.shard_map(body, mesh=fine, in_specs=in_specs, out_specs=out_specs, check_vma=False)
```

```python
import functools

import jax
import jax.numpy as jnp
from jax import lax
from jax.experimental import pallas as pl
from jax.experimental.pallas import tpu as pltpu
from jax.sharding import Mesh
from jax.sharding import PartitionSpec as P

D = 2048
FF = 4096
SSM_HEADS = 48
SSM_HEAD = 64
STATE = 256
Q_HEADS = 8
KV_HEADS = 2
HEAD_DIM = 128
CONV_K = 4
D_SSM = 3072
CONV_W = 3584
D_IN = 6704
ATT = 1024
KV = 256
EPSILON = 1e-05
ROPE_BASE = 10000.0
NEGATIVE = -1e30
HIGHEST = lax.Precision.HIGHEST

RANKS = 4
R_HEADS = SSM_HEADS // RANKS
R_SSM = D_SSM // RANKS
R_BC = 2 * STATE // RANKS
R_CONV = R_SSM + R_BC
R_ATT = ATT // RANKS
R_FF = FF // RANKS
R_OUT = R_SSM + R_ATT
HALF = 1024
MESH = pl.DeviceIdType.MESH
BF = jnp.bfloat16
F32 = jnp.float32


def rank_place():
    return 2 * lax.axis_index("section") + lax.axis_index("y")


def rank_id(rank):
    return {"section": rank // 2, "y": lax.rem(rank, 2)}


def greet(me):
    barrier = pltpu.get_barrier_semaphore()
    for step in range(1, RANKS):
        pl.semaphore_signal(
            barrier, inc=1, device_id=rank_id(lax.rem(me + step, RANKS)), device_id_type=MESH
        )
    pl.semaphore_wait(barrier, RANKS - 1)


def swap_kernel(with_stat, *refs):
    if with_stat:
        send_ref, stat_ref, out_ref, all_stat_ref, send_sem, recv_sem, stat_send, stat_recv = refs
    else:
        send_ref, out_ref, send_sem, recv_sem = refs
    me = rank_place()
    greet(me)
    copies = []
    for step in range(1, RANKS):
        other = lax.rem(me + step, RANKS)
        copies.append(
            pltpu.make_async_remote_copy(
                src_ref=send_ref.at[other] if len(send_ref.shape) == 3 else send_ref,
                dst_ref=out_ref.at[me],
                send_sem=send_sem.at[step - 1],
                recv_sem=recv_sem.at[step - 1],
                device_id=rank_id(other),
                device_id_type=MESH,
            )
        )
        if with_stat:
            copies.append(
                pltpu.make_async_remote_copy(
                    src_ref=stat_ref,
                    dst_ref=all_stat_ref.at[me],
                    send_sem=stat_send.at[step - 1],
                    recv_sem=stat_recv.at[step - 1],
                    device_id=rank_id(other),
                    device_id_type=MESH,
                )
            )
    for copy in copies:
        copy.start()
    if len(send_ref.shape) == 3:
        out_ref[me] = send_ref[me]
    else:
        out_ref[me] = send_ref[...]
    if with_stat:
        all_stat_ref[me] = stat_ref[...]
    for copy in copies:
        copy.wait()


CHANNELS = {}


def channel(name, *operands):
    key = (name,) + tuple((o.shape, str(o.dtype)) for o in operands)
    return CHANNELS.setdefault(key, len(CHANNELS))


def lasting(us):
    return pl.CostEstimate(flops=0, transcendentals=0, bytes_accessed=int(us * 850000))


VMEM_SPEC = pl.BlockSpec(memory_space=pltpu.VMEM)
ANY_SPEC = pl.BlockSpec(memory_space=pl.ANY)


def ignoring(kernel, used, extra):
    if not extra:
        return kernel
    return lambda *refs: kernel(*refs[:used], *refs[used + extra :])


def swap(values, stat=None, after=()):
    out_shape = [jax.ShapeDtypeStruct((RANKS,) + values.shape[-2:], values.dtype)]
    scratch = [pltpu.SemaphoreType.DMA((RANKS - 1,)), pltpu.SemaphoreType.DMA((RANKS - 1,))]
    args = [values]
    if stat is not None:
        out_shape.append(jax.ShapeDtypeStruct((RANKS,) + stat.shape, stat.dtype))
        scratch += scratch
        args.append(stat)
    out = pl.pallas_call(
        ignoring(functools.partial(swap_kernel, stat is not None), len(args), len(after)),
        out_shape=out_shape,
        in_specs=[VMEM_SPEC] * len(args) + [pl.BlockSpec(memory_space=pl.ANY)] * len(after),
        out_specs=[VMEM_SPEC] * len(out_shape),
        scratch_shapes=scratch,
        cost_estimate=lasting(9),
        compiler_params=pltpu.CompilerParams(
            collective_id=channel("swap", *args, *after),
            has_side_effects=True,
            vmem_limit_bytes=32 * 2**20,
        ),
    )(*args, *after)
    return out if stat is not None else out[0]


def scatter_sum(me, rows, part_ref, slots, send_sem, recv_sem):
    copies = []
    for step in range(1, RANKS):
        other = lax.rem(me + step, RANKS)
        copies.append(
            pltpu.make_async_remote_copy(
                src_ref=part_ref.at[pl.ds(pl.multiple_of(other * rows, rows), rows)],
                dst_ref=slots.at[step - 1],
                send_sem=send_sem.at[step - 1],
                recv_sem=recv_sem.at[step - 1],
                device_id=rank_id(other),
                device_id_type=MESH,
            )
        )
    for copy in copies:
        copy.start()
    total = part_ref[pl.ds(pl.multiple_of(me * rows, rows), rows), :].astype(F32)
    for step, copy in enumerate(copies):
        copy.wait()
        total = total + slots[step].astype(F32)
    return total


def spread(me, rows, out_ref, send_sem, recv_sem):
    here = pl.ds(pl.multiple_of(me * rows, rows), rows)
    copies = []
    for step in range(1, RANKS):
        copies.append(
            pltpu.make_async_remote_copy(
                src_ref=out_ref.at[here],
                dst_ref=out_ref.at[here],
                send_sem=send_sem.at[step - 1],
                recv_sem=recv_sem.at[step - 1],
                device_id=rank_id(lax.rem(me + step, RANKS)),
                device_id_type=MESH,
            )
        )
    for copy in copies:
        copy.start()
    for copy in copies:
        copy.wait()


def mid_kernel(part_ref, resid_ref, gain_ref, mid_ref, out_ref, slots, s1, r1, s2, r2):
    rows = resid_ref.shape[0]
    me = rank_place()
    greet(me)
    mid = scatter_sum(me, rows, part_ref, slots, s1, r1) + resid_ref[...].astype(F32)
    mid_ref[...] = mid
    scale = lax.rsqrt(jnp.mean(mid * mid, axis=-1, keepdims=True) + EPSILON)
    out_ref[pl.ds(pl.multiple_of(me * rows, rows), rows), :] = (
        mid * scale * gain_ref[...].astype(F32)
    ).astype(BF)
    spread(me, rows, out_ref, s2, r2)


def end_kernel(part_ref, resid_ref, out_ref, slots, s1, r1, s2, r2):
    rows = resid_ref.shape[0]
    me = rank_place()
    greet(me)
    total = scatter_sum(me, rows, part_ref, slots, s1, r1) + resid_ref[...]
    out_ref[pl.ds(pl.multiple_of(me * rows, rows), rows), :] = total.astype(BF)
    spread(me, rows, out_ref, s2, r2)


def back_kernel(
    part_ref, given_ref, value_ref, gain_ref, wide_ref, out_ref, gain_grad_ref, slots, s1, r1, s2, r2
):
    rows = given_ref.shape[0]
    me = rank_place()
    greet(me)
    grad = scatter_sum(me, rows, part_ref, slots, s1, r1)
    value = value_ref[...]
    scale = lax.rsqrt(jnp.mean(value * value, axis=-1, keepdims=True) + EPSILON)
    unit = value * scale
    gain_grad_ref[...] = jnp.sum(grad * unit, axis=0, keepdims=True)
    scaled = grad * gain_ref[...].astype(F32)
    total = given_ref[...] + scale * (
        scaled - unit * jnp.mean(scaled * unit, axis=-1, keepdims=True)
    )
    wide_ref[...] = total
    out_ref[pl.ds(pl.multiple_of(me * rows, rows), rows), :] = total.astype(BF)
    spread(me, rows, out_ref, s2, r2)


def rank_call(kernel, out_shape, rows, *args, after=()):
    return pl.pallas_call(
        ignoring(kernel, len(args), len(after)),
        out_shape=out_shape,
        in_specs=[VMEM_SPEC] * len(args) + [pl.BlockSpec(memory_space=pl.ANY)] * len(after),
        out_specs=[VMEM_SPEC] * len(out_shape),
        scratch_shapes=[pltpu.VMEM((RANKS - 1, rows, D), BF)]
        + [pltpu.SemaphoreType.DMA((RANKS - 1,))] * 4,
        cost_estimate=lasting(27),
        compiler_params=pltpu.CompilerParams(
            collective_id=channel(kernel.__name__, *args, *after),
            has_side_effects=True,
            vmem_limit_bytes=32 * 2**20,
        ),
    )(*args, *after)


def mid_step(part, resid, gain):
    rows = resid.shape[0]
    return rank_call(
        mid_kernel,
        [jax.ShapeDtypeStruct((rows, D), F32), jax.ShapeDtypeStruct(part.shape, BF)],
        rows,
        part,
        resid,
        gain[None],
    )


def end_step(part, resid):
    rows = resid.shape[0]
    return rank_call(end_kernel, [jax.ShapeDtypeStruct(part.shape, BF)], rows, part, resid)[0]


def back_step(part, given, value, gain, after=()):
    rows = given.shape[0]
    return rank_call(
        back_kernel,
        [
            jax.ShapeDtypeStruct((rows, D), F32),
            jax.ShapeDtypeStruct(part.shape, BF),
            jax.ShapeDtypeStruct((1, D), F32),
        ],
        rows,
        part,
        given,
        value,
        gain[None],
        after=after,
    )


def copy_kernel(value_ref, out_ref):
    out_ref[...] = value_ref[...]


def copy_after(value, *tokens):
    rows, width = value.shape
    tile = min(rows, 128)
    block = pl.BlockSpec((tile, width), lambda i: (i, 0))
    return pl.pallas_call(
        ignoring(copy_kernel, 1, len(tokens)),
        grid=(rows // tile,),
        out_shape=jax.ShapeDtypeStruct(value.shape, value.dtype),
        in_specs=[block] + [ANY_SPEC] * len(tokens),
        out_specs=block,
    )(value, *tokens)


def product_kernel(left_a, left_b, right_a, right_b, out_ref):
    turned = lambda left, right: lax.dot_general(
        left[...], right[...], (((0,), (0,)), ((), ())), preferred_element_type=F32
    )
    out_ref[...] = (turned(left_a, right_a) + turned(left_b, right_b)).astype(BF)


def outer_sum(left, right, tokens):
    rows, width = left[0].shape
    columns_right = right[0].shape[1]
    tile = 256
    left_block = pl.BlockSpec((rows, tile), lambda i: (0, i))
    right_block = pl.BlockSpec((rows, columns_right), lambda i: (0, 0))
    return pl.pallas_call(
        ignoring(product_kernel, 4, len(tokens)),
        grid=(width // tile,),
        out_shape=jax.ShapeDtypeStruct((width, columns_right), BF),
        in_specs=[left_block] * 2 + [right_block] * 2 + [ANY_SPEC] * len(tokens),
        out_specs=pl.BlockSpec((tile, columns_right), lambda i: (i, 0)),
        cost_estimate=lasting(3),
    )(*left, *right, *tokens)


def share_kernel(one_ref, zero_ref, *refs):
    own, own_c, across, across_c, local_sem, send_sem, recv_sem = refs[-7:]
    s, y, core = (lax.axis_index(name) for name in ("section", "y", "core"))
    rows = one_ref.shape[0]
    half = rows // 2
    barrier = pltpu.get_barrier_semaphore()
    ids = {"section": {"section": 1 - s}, "y": {"y": 1 - y}, "core": {"core": 1 - core}}
    for who in ids.values():
        pl.semaphore_signal(barrier, inc=1, device_id=who, device_id_type=MESH)
    pl.semaphore_wait(barrier, 3)

    def remote(k, src, dst, axis):
        return pltpu.make_async_remote_copy(
            src_ref=src, dst_ref=dst, send_sem=send_sem.at[k], recv_sem=recv_sem.at[k],
            device_id=ids[axis], device_id_type=MESH,
        )

    part = lambda ref, k: ref.at[pl.ds(half * k, half)]
    slot = lambda ref, place, k: ref.at[place, pl.ds(half * k, half)]
    for section, mine, sent in ((0, zero_ref, one_ref), (1, one_ref, zero_ref)):

        @pl.when(s == section)
        def _():
            for k in range(2):
                remote(k, part(sent, k), slot(own, section, k), "section").start()
            for k in range(2):
                remote(2 + k, part(mine, k), slot(across, section, k), "y").start()
            remote(6, mine, own_c.at[section], "core").start()
            keep = pltpu.make_async_copy(mine, own.at[section], local_sem)
            keep.start()
            for k in range(2):
                remote(k, part(sent, k), slot(own, 1 - section, k), "section").wait_recv()
                remote(4 + k, slot(own, 1 - section, k), slot(across, 1 - section, k), "y").start()
                remote(
                    7 + k, slot(own, 1 - section, k), slot(own_c, 1 - section, k), "core"
                ).start()
            for k in range(2):
                remote(2 + k, part(mine, k), slot(across, section, k), "y").wait_recv()
                remote(
                    9 + k, slot(across, section, k), slot(across_c, section, k), "core"
                ).start()
            for k in range(2):
                there = slot(across, 1 - section, k)
                remote(4 + k, slot(own, 1 - section, k), there, "y").wait_recv()
                remote(11 + k, there, slot(across_c, 1 - section, k), "core").start()
            remote(6, mine, own_c.at[section], "core").wait_recv()
            for k in range(2):
                there = slot(own_c, 1 - section, k)
                remote(7 + k, slot(own, 1 - section, k), there, "core").wait_recv()
                there = slot(across_c, section, k)
                remote(9 + k, slot(across, section, k), there, "core").wait_recv()
                there = slot(across_c, 1 - section, k)
                remote(11 + k, slot(across, 1 - section, k), there, "core").wait_recv()
            for k in range(2):
                remote(k, part(sent, k), slot(own, section, k), "section").wait_send()
                remote(2 + k, part(mine, k), slot(across, section, k), "y").wait_send()
                there = slot(across, 1 - section, k)
                remote(4 + k, slot(own, 1 - section, k), there, "y").wait_send()
                there = slot(own_c, 1 - section, k)
                remote(7 + k, slot(own, 1 - section, k), there, "core").wait_send()
                there = slot(across_c, section, k)
                remote(9 + k, slot(across, section, k), there, "core").wait_send()
                there = slot(across_c, 1 - section, k)
                remote(11 + k, slot(across, 1 - section, k), there, "core").wait_send()
            remote(6, mine, own_c.at[section], "core").wait_send()
            keep.wait()


def share(one, zero, us, after=()):
    shape = jax.ShapeDtypeStruct((2,) + one.shape, one.dtype)
    return pl.pallas_call(
        ignoring(share_kernel, 2, len(after)),
        out_shape=[shape] * 4,
        in_specs=[ANY_SPEC] * (2 + len(after)),
        out_specs=[ANY_SPEC] * 4,
        scratch_shapes=[
            pltpu.SemaphoreType.DMA,
            pltpu.SemaphoreType.DMA((13,)),
            pltpu.SemaphoreType.DMA((13,)),
        ],
        cost_estimate=lasting(us),
        compiler_params=pltpu.CompilerParams(
            collective_id=channel("share", one, zero, *after), has_side_effects=True
        ),
    )(one, zero, *after)


def chosen(place_ref, refs):
    y, core = place_ref[0], place_ref[1]
    values = [ref[...] for ref in refs]
    found = [[None, None], [None, None]]
    for side in range(2):
        flat = [jnp.where(core == side, values[2 * k], values[2 * k + 1]) for k in range(2)]
        for row in range(2):
            found[row][side] = jnp.where(y == row, flat[0], flat[1])
    return found


def rows_kernel(place_ref, a, b, c, d, out_ref):
    found = chosen(place_ref, (a, b, c, d))
    row = lax.rem(pl.program_id(0), 2)
    for side in range(2):
        value = jnp.where(row == 0, found[0][side][0], found[1][side][0])
        out_ref[:, HALF * side : HALF * (side + 1)] = value.astype(F32)


PLACE_SPEC = pl.BlockSpec(memory_space=pltpu.SMEM)


def spread_rows(place, pieces, first, count, tile):
    steps = count // tile
    block = pl.BlockSpec((1, tile, HALF), lambda r, i: (r // 2, first // tile + i, 0))
    return pl.pallas_call(
        rows_kernel,
        grid=(RANKS, steps),
        out_shape=jax.ShapeDtypeStruct((RANKS * count, D), F32),
        in_specs=[PLACE_SPEC] + [block] * 4,
        out_specs=pl.BlockSpec((tile, D), lambda r, i: (r * steps + i, 0)),
        compiler_params=pltpu.CompilerParams(vmem_limit_bytes=32 * 2**20),
    )(place, *pieces)


def gate_up_kernel(nz, place_ref, a, b, c, d, out_ref):
    found = chosen(place_ref, (a, b, c, d))
    width = R_FF // nz
    for side in range(2):
        for shard in range(nz):
            for rank in range(RANKS):
                start = FF * side + (FF // nz) * shard + width * rank
                out_ref[:, start : start + width] = found[rank % 2][side][
                    rank // 2, :, width * shard : width * (shard + 1)
                ].astype(F32)


def spread_gate_up(place, pieces, nz):
    rows = pieces[0].shape[1]
    tile = min(rows, 64)
    block = pl.BlockSpec((2, tile, HALF), lambda i: (0, i, 0))
    return pl.pallas_call(
        functools.partial(gate_up_kernel, nz),
        grid=(rows // tile,),
        out_shape=jax.ShapeDtypeStruct((rows, 2 * FF), F32),
        in_specs=[PLACE_SPEC] + [block] * 4,
        out_specs=pl.BlockSpec((tile, 2 * FF), lambda i: (i, 0)),
        compiler_params=pltpu.CompilerParams(vmem_limit_bytes=32 * 2**20),
    )(place, *pieces)


def in_kernel(place_ref, a, b, c, d, dt_ref, in_ref, qkv_ref):
    found = chosen(place_ref, (a, b, c, d))
    for rank in range(RANKS):
        left, right = (found[rank % 2][side][rank // 2].astype(F32) for side in range(2))
        in_ref[R_SSM * rank : R_SSM * (rank + 1)] = right[:, :R_SSM].T
        start = D_SSM + R_SSM * rank
        in_ref[start : start + R_SSM] = left[:, :R_SSM].T
        start = 2 * D_SSM + R_BC * rank
        in_ref[start : start + R_BC] = left[:, R_SSM:R_CONV].T
        qkv_ref[:, R_ATT * rank : R_ATT * (rank + 1)] = right[:, R_SSM:]
        start = ATT + KV * (rank % 2) + HEAD_DIM * (rank // 2)
        qkv_ref[:, start : start + HEAD_DIM] = left[:, R_CONV:]
    in_ref[D_SSM + CONV_W :] = dt_ref[...]


def spread_in(place, pieces, dt):
    rows = pieces[0].shape[1]
    tile = min(rows, 128)
    block = pl.BlockSpec((2, tile, HALF), lambda i: (0, i, 0))
    return pl.pallas_call(
        in_kernel,
        grid=(rows // tile,),
        out_shape=[
            jax.ShapeDtypeStruct((D_IN, rows), F32),
            jax.ShapeDtypeStruct((rows, ATT + 2 * KV), F32),
        ],
        in_specs=[PLACE_SPEC]
        + [block] * 4
        + [pl.BlockSpec((SSM_HEADS, tile), lambda i: (0, i))],
        out_specs=[
            pl.BlockSpec((D_IN, tile), lambda i: (0, i)),
            pl.BlockSpec((tile, ATT + 2 * KV), lambda i: (i, 0)),
        ],
        compiler_params=pltpu.CompilerParams(vmem_limit_bytes=40 * 2**20),
    )(place, *pieces, dt)


def narrow(values):
    return values.astype(BF)


def dot(left, right):
    return jnp.dot(left, right, preferred_element_type=F32)


def dot_t(left, right):
    return lax.dot_general(left, right, (((1,), (1,)), ((), ())), preferred_element_type=F32)


def t_dot(left, right):
    return lax.dot_general(left, right, (((0,), (0,)), ((), ())), preferred_element_type=F32)


def columns(array, start, width):
    return lax.dynamic_slice_in_dim(array, start, width, axis=1)


def cut_rows(array, start, width):
    return lax.dynamic_slice_in_dim(array, start, width, axis=0)


def rms(values, gain):
    return values * lax.rsqrt(jnp.mean(values * values, axis=-1, keepdims=True) + EPSILON) * gain


def rotary(values, turning):
    length, width = values.shape
    half = HEAD_DIM // 2
    frequency = ROPE_BASE ** (-jnp.arange(half, dtype=F32) / half)
    angles = jnp.arange(length, dtype=F32)[:, None] * frequency[None, :]
    cosine = jnp.cos(angles)[:, None, :]
    sine = turning * jnp.sin(angles)[:, None, :]
    halves = values.reshape(length, width // HEAD_DIM, 2, half)
    first, second = halves[:, :, 0], halves[:, :, 1]
    return jnp.stack(
        [first * cosine - second * sine, second * cosine + first * sine], axis=2
    ).reshape(length, width)


def causal(length):
    position = jnp.arange(length)
    return position[:, None] >= position[None, :]


def shifted(values, steps):
    if steps == 0:
        return values
    blank = jnp.zeros((abs(steps), values.shape[1]), values.dtype)
    if steps > 0:
        return jnp.concatenate([blank, values[:-steps]], axis=0)
    return jnp.concatenate([values[-steps:], blank], axis=0)


def conv_sum(rows, table):
    wide = rows.astype(F32)
    total = table[CONV_K][None, :]
    for tap in range(CONV_K):
        total = total + table[tap][None, :] * shifted(wide, CONV_K - 1 - tap)
    return total


def decays(dt_raw, heads):
    dt = jax.nn.softplus(dt_raw + heads[0][None, :])
    step = -dt * jnp.exp(heads[1])[None, :]
    length = dt.shape[0]
    running = jnp.dot(causal(length).astype(F32), step, precision=HIGHEST)
    return dt, step, running


def decay_table(running):
    length = running.shape[0]
    turned = running.T
    gap = turned[:, :, None] - turned[:, None, :]
    return jnp.exp(jnp.where(causal(length)[None], gap, NEGATIVE))


def by_head(values):
    return values.reshape(values.shape[0], R_HEADS, SSM_HEAD)


def scan_forward(x, b_rows, c_rows, dt_raw, heads):
    dt, _, running = decays(dt_raw, heads)
    mixing = dot_t(c_rows, b_rows)
    weights = narrow(decay_table(running) * mixing[None] * dt.T[:, None, :])
    x_heads = by_head(x)
    result = jnp.einsum("hts,shp->thp", weights, x_heads, preferred_element_type=F32)
    return (result + heads[2][None, :, None] * x_heads.astype(F32)).reshape(x.shape)


def scan_backward(x, b_rows, c_rows, dt_raw, heads, grad_y):
    dt, step, running = decays(dt_raw, heads)
    length = x.shape[0]
    mixing = dot_t(c_rows, b_rows)
    table = decay_table(running)
    dt_t = dt.T
    x_heads = by_head(x)
    grad_heads = by_head(narrow(grad_y))
    grad_weights = jnp.einsum("thp,shp->hts", grad_heads, x_heads, preferred_element_type=F32)
    faded = grad_weights * table
    weights = table * mixing[None] * dt_t[:, None, :]
    grad_x = jnp.einsum("hts,thp->shp", narrow(weights), grad_heads, preferred_element_type=F32)
    grad_y_heads = by_head(grad_y)
    grad_x = grad_x + heads[2][None, :, None] * grad_y_heads
    grad_skip = jnp.sum(grad_y_heads * x_heads.astype(F32), axis=(0, 2))
    grad_mixing = narrow(jnp.sum(faded * dt_t[:, None, :], axis=0))
    grad_c = dot(grad_mixing, b_rows)
    grad_b = t_dot(grad_mixing, c_rows)
    plain = faded * mixing[None]
    grad_dt = jnp.sum(plain, axis=1)
    grad_gap = plain * dt_t[:, None, :]
    grad_running = jnp.sum(grad_gap, axis=2) - jnp.sum(grad_gap, axis=1)
    grad_step = jnp.dot(grad_running, causal(length).astype(F32), precision=HIGHEST).T
    grad_dt = grad_dt.T - grad_step * jnp.exp(heads[1])[None, :]
    grad_log = jnp.sum(grad_step * step, axis=0)
    grad_raw = grad_dt * jax.nn.sigmoid(dt_raw + heads[0][None, :])
    grad_table = jnp.stack([jnp.sum(grad_raw, axis=0), grad_log, grad_skip])
    return grad_x.reshape(x.shape), grad_b, grad_c, grad_raw, grad_table


def attend(query, key, value):
    length = query.shape[0]
    heads = query.reshape(length, -1, HEAD_DIM)
    scores = jnp.einsum("qhd,sd->hqs", heads, key, preferred_element_type=F32) * HEAD_DIM**-0.5
    scores = jnp.where(causal(length)[None], scores, NEGATIVE)
    weights = jnp.exp(scores - jnp.max(scores, axis=-1, keepdims=True))
    probs = weights / jnp.sum(weights, axis=-1, keepdims=True)
    mixed = jnp.einsum("hqs,sd->qhd", narrow(probs), value, preferred_element_type=F32)
    return narrow(mixed.reshape(query.shape)), probs


def attend_back(query, key, value, probs, grad_out):
    length = query.shape[0]
    heads = query.reshape(length, -1, HEAD_DIM)
    grad_heads = grad_out.reshape(length, -1, HEAD_DIM)
    grad_probs = jnp.einsum("qhd,sd->hqs", grad_heads, value, preferred_element_type=F32)
    grad_scores = narrow(
        probs * (grad_probs - jnp.sum(probs * grad_probs, axis=-1, keepdims=True))
    )
    scale = HEAD_DIM**-0.5
    grad_query = jnp.einsum("hqs,sd->qhd", grad_scores, key, preferred_element_type=F32) * scale
    grad_key = jnp.einsum("hqs,qhd->sd", grad_scores, heads, preferred_element_type=F32) * scale
    grad_value = jnp.einsum("hqs,qhd->sd", narrow(probs), grad_heads, preferred_element_type=F32)
    return grad_query.reshape(query.shape), grad_key, grad_value


def flip(value, axis):
    return lax.ppermute(value, axis, [(0, 1), (1, 0)])


def layer_forward(entering, resid, weights, small, first):
    s, y = lax.axis_index("section"), lax.axis_index("y")
    length = entering.shape[0]
    x1 = narrow(rms(entering.astype(F32), small["gain0"][None, :]))
    left = dot(x1, weights["in"][0])
    right = dot(x1, weights["in"][1])
    dt_raw = columns(dot(x1, weights["dt"]), R_HEADS * (2 * s + y), R_HEADS)
    xbc = narrow(left[:, :R_CONV])
    u = narrow(jax.nn.silu(conv_sum(xbc, small["conv"])))
    kv_raw = left[:, R_CONV:]
    kv = narrow(jnp.where(y == 0, rotary(kv_raw, 1.0), kv_raw))
    shared = swap(jnp.concatenate([u[:, R_SSM:], kv], axis=1))
    b_rows = jnp.concatenate([shared[0, :, :R_BC], shared[1, :, :R_BC]], axis=1)
    c_rows = jnp.concatenate([shared[2, :, :R_BC], shared[3, :, :R_BC]], axis=1)
    pair = lax.dynamic_slice_in_dim(shared, 2 * s, 2, axis=0)[:, :, R_BC:]
    key, value = pair[0], pair[1]
    z = right[:, :R_SSM]
    query = narrow(rotary(right[:, R_SSM:], 1.0))
    o, probs = attend(query, key, value)
    x = u[:, :R_SSM]
    scan = scan_forward(x, b_rows, c_rows, dt_raw, small["heads"])
    gated = scan * jax.nn.silu(z)
    squares = jnp.sum(gated * gated, axis=1)
    scaled = narrow(gated * small["ssm_gain"][None, :])
    message = to_rows(scaled, o)
    stat = jnp.broadcast_to(squares[None, :], (8, length))
    got, stats = swap(message, stat)
    spread_of = lax.rsqrt(jnp.sum(stats[:, 0, :], axis=0) / D_SSM + EPSILON)
    wide = jnp.transpose(got, (1, 0, 2)).reshape(length, R_OUT)
    is_ssm = small["is_ssm"][None, :]
    mo = narrow(jnp.where(is_ssm, wide.astype(F32) * spread_of[:, None], wide.astype(F32)))
    part = jnp.concatenate([dot(mo, weights["out"][0]), dot(mo, weights["out"][1])], axis=1)
    mid, x2 = mid_step(narrow(part), resid, small["gain1"])
    gate = dot(x2, weights["gu"][0])
    up = dot(x2, weights["gu"][1])
    act = narrow(jax.nn.silu(gate) * up)
    part2 = jnp.concatenate([dot(act, weights["down"][0]), dot(act, weights["down"][1])], axis=1)
    leaving = end_step(narrow(part2), mid)
    kept = dict(
        resid=resid, x1=x1, xbc=xbc, u=u, b=b_rows, c=c_rows, key=key, value=value, query=query,
        probs=probs, z=z, dt_raw=dt_raw, scan=scan, spread=spread_of, mo=mo, mid=mid, x2=x2,
        gate=gate, up=up, act=act,
    )
    return leaving, kept


def to_rows(ssm_part, att_part):
    length = ssm_part.shape[0]
    nz = lax.axis_size("fsdp")
    inner = nz // RANKS
    a = ssm_part.reshape(length, inner, RANKS, R_SSM // nz)
    b = att_part.reshape(length, inner, RANKS, R_ATT // nz)
    both = jnp.concatenate([a, b], axis=3)
    return jnp.transpose(both, (2, 0, 1, 3)).reshape(RANKS, length, R_OUT // RANKS)


def from_rows(got):
    length = got.shape[1]
    nz = lax.axis_size("fsdp")
    inner = nz // RANKS
    both = jnp.transpose(got.reshape(RANKS, length, inner, R_OUT // nz), (1, 2, 0, 3))
    a = both[..., : R_SSM // nz].reshape(length, R_SSM)
    b = both[..., R_SSM // nz :].reshape(length, R_ATT)
    return a, b


def layer_backward(grad, given, kept, weights, small, queue, layer, first=()):
    s, y = lax.axis_index("section"), lax.axis_index("y")
    core = lax.axis_index("core")
    length = grad.shape[0]
    down, gu, out, win = weights["down"], weights["gu"], weights["out"], weights["in"]

    def product(left, right, *tokens):
        mine = jnp.where(core == 0, right[0], right[1])
        theirs = jnp.where(core == 0, right[1], right[0])
        return outer_sum((left, flip(left, "core")), (mine, flip(theirs, "core")), tokens)

    def reduce(name, block):
        nonlocal queue
        if queue:
            block, queue["last"] = lax.optimization_barrier((block, queue["last"]))
        queue[name] = queue["last"] = lax.psum_scatter(
            block, "fsdp", scatter_dimension=0, tiled=True
        )

    def due(point):
        return [queue[k] for k in WAITS[layer].get(point, ())]

    halves = lambda v: (v[:, :HALF], v[:, HALF:])
    g0, g1 = halves(grad)
    down_block = product(kept["act"], (g0, g1))
    if layer == 1:
        reduce("down1", down_block)
    grad_act = dot_t(g0, down[0]) + dot_t(g1, down[1])
    gate, up = kept["gate"], kept["up"]
    sig = jax.nn.sigmoid(gate)
    d_gate = narrow(grad_act * up * (sig * (1.0 + gate * (1.0 - sig))))
    d_up = narrow(grad_act * gate * sig)
    if layer == 1:
        reduce("gu1", product(kept["x2"], (d_gate, d_up), *first))
    part = dot_t(d_gate, gu[0]) + dot_t(d_up, gu[1])
    d_mid, db, grad_gain1 = back_step(
        narrow(part), given, kept["mid"], small["gain1"], due("mlp") + list(first)
    )
    b0, b1 = halves(db)
    d_mo = dot_t(b0, out[0]) + dot_t(b1, out[1])
    mo = kept["mo"]
    is_ssm = small["is_ssm"][None, :]
    stat_row = jnp.sum(jnp.where(is_ssm, d_mo * mo.astype(F32), 0.0), axis=1)
    stat = jnp.broadcast_to(stat_row[None, :], (8, length))
    blocks = jnp.transpose(narrow(d_mo).reshape(length, RANKS, R_OUT // RANKS), (1, 0, 2))
    got, stats = swap(blocks, stat, due("norm"))
    overlap = jnp.sum(stats[:, 0, :], axis=0)[:, None]
    if layer == 0:
        reduce("gu0", product(kept["x2"], (d_gate, d_up), got))
    else:
        reduce("out1", product(kept["mo"], (b0, b1), got))
    d_norm, d_o = from_rows(got)
    d_norm = d_norm.astype(F32)
    spread_of = kept["spread"][:, None]
    scan, z = kept["scan"], kept["z"]
    sig_z = jax.nn.sigmoid(z)
    silu_z = z * sig_z
    gated = scan * silu_z
    grad_ssm_gain = jnp.sum(d_norm * gated * spread_of, axis=0)
    d_gated = spread_of * d_norm * small["ssm_gain"][None, :] - gated * (
        spread_of * spread_of * overlap * (1.0 / D_SSM)
    )
    d_scan = d_gated * silu_z
    d_z = d_gated * scan * (sig_z * (1.0 + z * (1.0 - sig_z)))
    d_query, d_key, d_value = attend_back(
        kept["query"], kept["key"], kept["value"], kept["probs"], d_o
    )
    u = kept["u"]
    d_x, d_b, d_c, d_dt, grad_heads = scan_backward(
        u[:, :R_SSM], kept["b"], kept["c"], kept["dt_raw"], small["heads"], d_scan
    )
    message = jnp.stack(
        [
            jnp.concatenate([d_b[:, :R_BC], d_key], axis=1),
            jnp.concatenate([d_b[:, R_BC:], d_value], axis=1),
            jnp.concatenate([d_c[:, :R_BC], d_key], axis=1),
            jnp.concatenate([d_c[:, R_BC:], d_value], axis=1),
        ]
    )
    back = swap(narrow(message), None, due("scan"))
    back = back.astype(F32)
    d_bc = back[0, :, :R_BC] + back[1, :, :R_BC] + back[2, :, :R_BC] + back[3, :, :R_BC]
    d_kv = jnp.sum(lax.dynamic_slice_in_dim(back, 2 * s, 2, axis=0)[:, :, R_BC:], axis=0)
    d_kv = jnp.where(y == 0, rotary(d_kv, -1.0), d_kv)
    d_u = jnp.concatenate([d_x, d_bc], axis=1)
    xbc = kept["xbc"]
    table = small["conv"]
    before = conv_sum(xbc, table)
    sig_c = jax.nn.sigmoid(before)
    d_before = d_u * (sig_c * (1.0 + before * (1.0 - sig_c)))
    wide = xbc.astype(F32)
    grad_conv = jnp.stack(
        [jnp.sum(d_before * shifted(wide, CONV_K - 1 - tap), axis=0) for tap in range(CONV_K)]
        + [jnp.sum(d_before, axis=0)]
    )
    d_xbc = 0.0
    for tap in range(CONV_K):
        d_xbc = d_xbc + table[tap][None, :] * shifted(d_before, tap - CONV_K + 1)
    d_left = narrow(jnp.concatenate([d_xbc, d_kv], axis=1))
    d_right = narrow(jnp.concatenate([d_z, rotary(d_query, -1.0)], axis=1))
    d_dt_b = narrow(d_dt)
    dt_own = columns(weights["dt"], R_HEADS * (2 * s + y), R_HEADS)
    reduce(f"in{layer}", product(kept["x1"], (d_left, d_right)))
    part = dot_t(d_left, win[0]) + dot_t(d_right, win[1]) + dot_t(d_dt_b, dt_own)
    got_gu = None
    if layer == 0:
        got_gu = share(queue["gu1"], queue["gu0"], 50)
    _, entering_grad, grad_gain0 = back_step(
        narrow(part),
        d_mid,
        kept["resid"].astype(F32),
        small["gain0"],
        due("in") + list(got_gu or ())[:1],
    )
    if layer == 0:
        reduce("out0", product(kept["mo"], (b0, b1), got_gu[0]))
    two = lambda v: jnp.concatenate([v, flip(v, "core")], axis=0)
    grad_dt_w = t_dot(two(jnp.pad(d_dt_b, ((0, 0), (0, 4)))), two(kept["x1"]))
    smalls_grad = dict(
        heads=grad_heads, conv=grad_conv, ssm=grad_ssm_gain[None], dt=grad_dt_w,
        gains=jnp.concatenate([grad_gain0, grad_gain1], axis=0),
    )
    return entering_grad, smalls_grad, (down_block, reduce, got_gu)


WAITS = (
    {"mlp": ("out1",), "scan": ("in1",)},
    {"norm": ("down1",), "in": ("gu1",)},
)


def body(
    inputs, cotangent, norm_gains, head_params, conv_params, ssm_gain,
    w_in, w_out, w_qkv, w_o, w_gu, w_down,
):
    s, y = lax.axis_index("section"), lax.axis_index("y")
    core = lax.axis_index("core")
    nz = lax.axis_size("fsdp")
    z_place = lax.axis_index("fsdp")
    rank = 2 * s + y
    rows = inputs.shape[2]
    length = RANKS * rows
    w_in, w_out, w_qkv, w_o, w_gu, w_down = (
        w[0] for w in (w_in, w_out, w_qkv, w_o, w_gu, w_down)
    )

    flat = jnp.concatenate(
        [
            norm_gains[0].reshape(-1),
            head_params[0].reshape(-1),
            conv_params[0].reshape(-1),
            ssm_gain[0],
            w_in[:, D_SSM + CONV_W :].reshape(-1),
        ]
    )
    count = flat.shape[0]
    flat = jnp.pad(flat, (0, -count % 2048)).reshape(-1, 128)
    everything = lax.all_gather(flat, ("section", "fsdp"), axis=0).reshape(2, nz, -1)[..., :count]

    def unpack(layer):
        part = everything[layer]
        sizes = [2 * D // nz, 3 * SSM_HEADS // nz, 5 * CONV_W // nz, D_SSM // nz]
        starts = [0]
        for size in sizes:
            starts.append(starts[-1] + size)
        join = lambda k, lead: jnp.transpose(
            part[:, starts[k] : starts[k + 1]].reshape(nz, lead, -1), (1, 0, 2)
        ).reshape(lead, -1).astype(F32)
        gains, heads, conv, gain = join(0, 2), join(1, 3), join(2, 5), join(3, 1)[0]
        conv_own = jnp.concatenate(
            [columns(conv, R_SSM * rank, R_SSM), columns(conv, D_SSM + R_BC * rank, R_BC)], axis=1
        )
        channel = jnp.arange(R_OUT) % (R_OUT // nz)
        small = dict(
            gain0=gains[0],
            gain1=gains[1],
            heads=columns(heads, R_HEADS * rank, R_HEADS),
            conv=conv_own,
            ssm_gain=lax.dynamic_slice_in_dim(gain, R_SSM * rank, R_SSM),
            is_ssm=channel < R_SSM // nz,
        )
        return small, part[:, starts[4] :].reshape(D, SSM_HEADS)

    def pieces(section):
        rk = 2 * section + y
        first = columns(w_in, jnp.where(core == 0, D_SSM, 0) + R_SSM * rk, R_SSM)
        second = jnp.where(
            core == 0,
            columns(w_in, 2 * D_SSM + R_BC * rk, R_BC),
            columns(w_qkv, R_ATT * rk, HEAD_DIM),
        )
        third = columns(
            w_qkv,
            jnp.where(core == 0, ATT + KV * y + HEAD_DIM * section, R_ATT * rk + HEAD_DIM),
            HEAD_DIM,
        )
        side = HALF * core
        out_rows, o_rows, down_rows = R_SSM // nz, R_ATT // nz, R_FF // nz
        ff = R_FF // nz
        return {
            "in": jnp.concatenate([first, second, third], axis=1),
            "out": jnp.concatenate(
                [
                    lax.dynamic_slice(w_out, (out_rows * rk, side), (out_rows, HALF)),
                    lax.dynamic_slice(w_o, (o_rows * rk, side), (o_rows, HALF)),
                ],
                axis=0,
            ),
            "gu": jnp.concatenate(
                [
                    columns(w_gu, FF * core + (FF // nz) * k + ff * rk, ff) for k in range(nz)
                ],
                axis=1,
            ),
            "down": lax.dynamic_slice(w_down, (down_rows * rk, side), (down_rows, HALF)),
        }

    order = []

    def in_turn(value):
        if order:
            value, order[-1] = lax.optimization_barrier((value, order[-1]))
        return value

    def gather(piece):
        order.append(lax.all_gather(in_turn(piece), ("core", "fsdp"), axis=0))
        return order[-1]

    own, other = pieces(s), pieces(1 - s)
    out_own = gather(own["out"])
    mlp = lambda found: jnp.concatenate([found["gu"], found["down"]], axis=0)
    in_arrived = flip(other["in"], "section")
    out_sent, in_arrived = lax.optimization_barrier((other["out"], in_arrived))
    out_arrived = flip(out_sent, "section")
    mlp_own = mlp(own)
    mlp_sent, out_arrived = lax.optimization_barrier((mlp(other), out_arrived))
    mlp_arrived = flip(mlp_sent, "section")
    of_layer = lambda layer, mine, theirs: jnp.where(s == layer, mine, theirs)
    flat_rows = lambda whole: whole.reshape(2, -1, HALF)
    in0 = gather(copy_after(of_layer(0, own["in"], in_arrived), everything))
    out_other = gather(copy_after(out_arrived, in0))
    wide = own["gu"].shape[0]
    mlp0, mlp1 = (of_layer(layer, mlp_own, mlp_arrived) for layer in range(2))
    gu0 = gather(mlp0[:wide])
    down0 = gather(mlp0[wide:])
    in1 = gather(of_layer(1, own["in"], in_arrived))
    gu1 = gather(mlp1[:wide])
    down1 = gather(mlp1[wide:])
    weights = [
        dict(
            out=flat_rows(of_layer(layer, out_own, out_other)),
            **{"in": flat_rows((in0, in1)[layer])},
        )
        for layer in range(2)
    ]
    weights[0]["gu"] = flat_rows(gu0)
    weights[0]["down"] = flat_rows(down0)
    weights[1]["gu"] = flat_rows(gu1)
    weights[1]["down"] = flat_rows(down1)

    def whole_sequence(own_rows):
        place = 2 * y + core
        result = jnp.zeros((RANKS, rows, D), BF)
        result = lax.dynamic_update_index_in_dim(
            result, lax.dynamic_index_in_dim(own_rows, core, 0, False), place, 0
        )
        for dy, dc in ((0, 1), (1, 0), (1, 1)):
            sent = lax.dynamic_index_in_dim(own_rows, core ^ dc, 0, False)
            pairs = [
                (2 * a + b, 2 * (a ^ dy) + (b ^ dc)) for a in range(2) for b in range(2)
            ]
            here = lax.ppermute(sent, ("y", "core"), pairs)
            result = lax.dynamic_update_index_in_dim(
                result, here, 2 * (y ^ dy) + (core ^ dc), 0
            )
        return result.reshape(length, D)

    def rank_rows(whole):
        return cut_rows(whole, rows * rank, rows)

    smalls = []
    for layer in range(2):
        small, weights[layer]["dt"] = unpack(layer)
        smalls.append(small)
    hidden = whole_sequence(inputs[:, 0])
    grad = whole_sequence(cotangent[:, 0])
    outs, kept = [], []
    for layer in range(2):
        hidden, keep = layer_forward(
            hidden, rank_rows(hidden), weights[layer], smalls[layer], layer == 0
        )
        outs.append(hidden)
        kept.append(keep)
    grads = [None, None]
    smalls_grad, queue = [None, None], {}
    for layer in (1, 0):
        grad, smalls_grad[layer], blocks = layer_backward(
            grad,
            rank_rows(grad).astype(F32),
            kept[layer],
            weights[layer],
            smalls[layer],
            queue,
            layer,
            (outs[1],) if layer == 1 else (),
        )
        grads[layer] = grad

    def block_rows(pair):
        chosen = jnp.where(s == 0, pair[0], pair[1]).reshape(RANKS, rows, D)
        mine = lax.dynamic_index_in_dim(chosen, 2 * y + core, 0, False)
        sent = lax.dynamic_index_in_dim(chosen, 2 * y + (1 - core), 0, False)
        theirs = flip(sent, "core")
        both = jnp.where(core == 0, jnp.stack([mine, theirs]), jnp.stack([theirs, mine]))
        return both[None, :, None]

    down_block, reduce, got_gu = blocks
    fan = lambda array, axis: jnp.moveaxis(
        array.reshape(array.shape[:axis] + (nz, -1) + array.shape[axis + 1 :]), axis, 0
    )
    dt_rows = jnp.concatenate([fan(g["dt"], 1) for g in smalls_grad], axis=2)
    dt_rows = jnp.pad(dt_rows, ((0, 0), (0, 0), (0, HALF - dt_rows.shape[2])))

    def placed(array, total, starts):
        whole = jnp.zeros((array.shape[0], total), F32)
        at = 0
        for start, width in starts:
            whole = lax.dynamic_update_slice(whole, array[:, at : at + width], (0, start))
            at += width
        return fan(whole, 1).reshape(nz, -1)

    listed = []
    for g in smalls_grad:
        listed.append(fan(g["gains"], 1).reshape(nz, -1))
        listed.append(placed(g["heads"], SSM_HEADS, [(R_HEADS * rank, R_HEADS)]))
        listed.append(
            placed(g["conv"], CONV_W, [(R_SSM * rank, R_SSM), (D_SSM + R_BC * rank, R_BC)])
        )
        listed.append(placed(g["ssm"], D_SSM, [(R_SSM * rank, R_SSM)]))
    packed = jnp.concatenate(listed, axis=1)
    packed = packed + flip(packed, "core")
    amount = packed.shape[1]
    packed = jnp.pad(packed, ((0, 0), (0, -amount % (16 * HALF)))).reshape(nz, -1, HALF)
    down_rows = R_FF // nz
    extra = jnp.concatenate([dt_rows, packed], axis=1)
    extra_count = extra.shape[1]
    last = jnp.concatenate([down_block.reshape(nz, down_rows, HALF), narrow(extra)], axis=1)
    reduce("down0", last.reshape(-1, HALF))
    down0, extra = queue["down0"][:down_rows], queue["down0"][down_rows:]

    place = jnp.stack([y, core]).astype(jnp.int32)
    grad_w_gu = spread_gate_up(place, got_gu, nz)
    got_in = share(queue["in1"], queue["in0"], 50)
    got_out = share(queue["out1"], queue["out0"], 30, (got_in[0],))
    shared = swap(extra).astype(F32)
    got_down = share(queue["down1"], down0, 30)
    out_rows, o_rows = R_SSM // nz, R_ATT // nz
    grad_w_out = spread_rows(place, got_out, 0, out_rows, o_rows)
    grad_w_o = spread_rows(place, got_out, out_rows, o_rows, o_rows)
    grad_w_down = spread_rows(place, got_down, 0, down_rows, min(down_rows, 128))

    width = D // nz
    dt_all = jnp.where(s == 0, shared[:, :12, :width], shared[:, :12, width : 2 * width])
    grad_w_in, grad_w_qkv = spread_in(place, got_in, dt_all.reshape(SSM_HEADS, width))
    grad_w_in = grad_w_in.T
    small_sum = jnp.sum(shared[:, 16:], axis=0).reshape(-1)[:amount].reshape(2, -1)
    small_sum = jnp.where(s == 0, small_sum[0], small_sum[1])
    cuts, at = [], 0
    for lead, total in ((2, D), (3, SSM_HEADS), (5, CONV_W), (1, D_SSM)):
        size = lead * total // nz
        cuts.append(small_sum[at : at + size].reshape(lead, total // nz))
        at += size
    return (
        block_rows(outs),
        block_rows(grads),
        cuts[0][None],
        cuts[1][None],
        cuts[2][None],
        cuts[3],
        grad_w_in[None],
        grad_w_out[None],
        grad_w_qkv[None],
        grad_w_o[None],
        grad_w_gu[None],
        grad_w_down[None],
    )


def solution(mesh):
    CHANNELS.clear()
    sections, ctx, fsdp = mesh.devices.shape
    fine = Mesh(
        mesh.devices.reshape(sections, ctx // 2, 2, fsdp), ("section", "y", "core", "fsdp")
    )
    tokens = ("y", "core")
    in_specs = (
        P(None, "fsdp", tokens, None),
        P(None, "fsdp", tokens, None),
        P("section", None, "fsdp"),
        P("section", None, "fsdp"),
        P("section", None, "fsdp"),
        P("section", "fsdp"),
    ) + (P("section", "fsdp", None),) * 6
    out_specs = (
        P("section", None, "fsdp", tokens, None),
        P("section", None, "fsdp", tokens, None),
        P("section", None, "fsdp"),
        P("section", None, "fsdp"),
        P("section", None, "fsdp"),
        P("section", "fsdp"),
    ) + (P("section", "fsdp", None),) * 6
    return jax.shard_map(body, mesh=fine, in_specs=in_specs, out_specs=out_specs, check_vma=False)
```

```python
import functools

import jax
import jax.numpy as jnp
from jax import lax
from jax.experimental import pallas as pl
from jax.experimental.pallas import tpu as pltpu
from jax.sharding import Mesh
from jax.sharding import PartitionSpec as P

D = 2048
FF = 4096
SSM_HEADS = 48
SSM_HEAD = 64
STATE = 256
Q_HEADS = 8
KV_HEADS = 2
HEAD_DIM = 128
CONV_K = 4
D_SSM = 3072
CONV_W = 3584
D_IN = 6704
ATT = 1024
KV = 256
EPSILON = 1e-05
ROPE_BASE = 10000.0
NEGATIVE = -1e30
HIGHEST = lax.Precision.HIGHEST

RANKS = 4
R_HEADS = SSM_HEADS // RANKS
R_SSM = D_SSM // RANKS
R_BC = 2 * STATE // RANKS
R_CONV = R_SSM + R_BC
R_ATT = ATT // RANKS
R_FF = FF // RANKS
R_OUT = R_SSM + R_ATT
HALF = 1024
MESH = pl.DeviceIdType.MESH
BF = jnp.bfloat16
F32 = jnp.float32


def rank_place():
    return 2 * lax.axis_index("section") + lax.axis_index("y")


def rank_id(rank):
    return {"section": rank // 2, "y": lax.rem(rank, 2)}


def greet(me):
    barrier = pltpu.get_barrier_semaphore()
    for step in range(1, RANKS):
        pl.semaphore_signal(
            barrier, inc=1, device_id=rank_id(lax.rem(me + step, RANKS)), device_id_type=MESH
        )
    pl.semaphore_wait(barrier, RANKS - 1)


def swap_kernel(with_stat, *refs):
    if with_stat:
        send_ref, stat_ref, out_ref, all_stat_ref, send_sem, recv_sem, stat_send, stat_recv = refs
    else:
        send_ref, out_ref, send_sem, recv_sem = refs
    me = rank_place()
    greet(me)
    copies = []
    for step in range(1, RANKS):
        other = lax.rem(me + step, RANKS)
        copies.append(
            pltpu.make_async_remote_copy(
                src_ref=send_ref.at[other] if len(send_ref.shape) == 3 else send_ref,
                dst_ref=out_ref.at[me],
                send_sem=send_sem.at[step - 1],
                recv_sem=recv_sem.at[step - 1],
                device_id=rank_id(other),
                device_id_type=MESH,
            )
        )
        if with_stat:
            copies.append(
                pltpu.make_async_remote_copy(
                    src_ref=stat_ref,
                    dst_ref=all_stat_ref.at[me],
                    send_sem=stat_send.at[step - 1],
                    recv_sem=stat_recv.at[step - 1],
                    device_id=rank_id(other),
                    device_id_type=MESH,
                )
            )
    for copy in copies:
        copy.start()
    if len(send_ref.shape) == 3:
        out_ref[me] = send_ref[me]
    else:
        out_ref[me] = send_ref[...]
    if with_stat:
        all_stat_ref[me] = stat_ref[...]
    for copy in copies:
        copy.wait()


CHANNELS = {}


def channel(name, *operands):
    key = (name,) + tuple((o.shape, str(o.dtype)) for o in operands)
    return CHANNELS.setdefault(key, len(CHANNELS))


def lasting(us):
    return pl.CostEstimate(flops=0, transcendentals=0, bytes_accessed=int(us * 850000))


VMEM_SPEC = pl.BlockSpec(memory_space=pltpu.VMEM)
ANY_SPEC = pl.BlockSpec(memory_space=pl.ANY)


def ignoring(kernel, used, extra):
    if not extra:
        return kernel
    return lambda *refs: kernel(*refs[:used], *refs[used + extra :])


def swap(values, stat=None, after=()):
    out_shape = [jax.ShapeDtypeStruct((RANKS,) + values.shape[-2:], values.dtype)]
    scratch = [pltpu.SemaphoreType.DMA((RANKS - 1,)), pltpu.SemaphoreType.DMA((RANKS - 1,))]
    args = [values]
    if stat is not None:
        out_shape.append(jax.ShapeDtypeStruct((RANKS,) + stat.shape, stat.dtype))
        scratch += scratch
        args.append(stat)
    out = pl.pallas_call(
        ignoring(functools.partial(swap_kernel, stat is not None), len(args), len(after)),
        out_shape=out_shape,
        in_specs=[VMEM_SPEC] * len(args) + [pl.BlockSpec(memory_space=pl.ANY)] * len(after),
        out_specs=[VMEM_SPEC] * len(out_shape),
        scratch_shapes=scratch,
        cost_estimate=lasting(9),
        compiler_params=pltpu.CompilerParams(
            collective_id=channel("swap", *args, *after),
            has_side_effects=True,
            vmem_limit_bytes=32 * 2**20,
        ),
    )(*args, *after)
    return out if stat is not None else out[0]


def scatter_sum(me, rows, part_ref, slots, send_sem, recv_sem):
    copies = []
    for step in range(1, RANKS):
        other = lax.rem(me + step, RANKS)
        copies.append(
            pltpu.make_async_remote_copy(
                src_ref=part_ref.at[pl.ds(pl.multiple_of(other * rows, rows), rows)],
                dst_ref=slots.at[step - 1],
                send_sem=send_sem.at[step - 1],
                recv_sem=recv_sem.at[step - 1],
                device_id=rank_id(other),
                device_id_type=MESH,
            )
        )
    for copy in copies:
        copy.start()
    total = part_ref[pl.ds(pl.multiple_of(me * rows, rows), rows), :].astype(F32)
    for step, copy in enumerate(copies):
        copy.wait()
        total = total + slots[step].astype(F32)
    return total


def spread(me, rows, out_ref, send_sem, recv_sem):
    here = pl.ds(pl.multiple_of(me * rows, rows), rows)
    copies = []
    for step in range(1, RANKS):
        copies.append(
            pltpu.make_async_remote_copy(
                src_ref=out_ref.at[here],
                dst_ref=out_ref.at[here],
                send_sem=send_sem.at[step - 1],
                recv_sem=recv_sem.at[step - 1],
                device_id=rank_id(lax.rem(me + step, RANKS)),
                device_id_type=MESH,
            )
        )
    for copy in copies:
        copy.start()
    for copy in copies:
        copy.wait()


def mid_kernel(part_ref, resid_ref, gain_ref, mid_ref, out_ref, slots, s1, r1, s2, r2):
    rows = resid_ref.shape[0]
    me = rank_place()
    greet(me)
    mid = scatter_sum(me, rows, part_ref, slots, s1, r1) + resid_ref[...].astype(F32)
    mid_ref[...] = mid
    scale = lax.rsqrt(jnp.mean(mid * mid, axis=-1, keepdims=True) + EPSILON)
    out_ref[pl.ds(pl.multiple_of(me * rows, rows), rows), :] = (
        mid * scale * gain_ref[...].astype(F32)
    ).astype(BF)
    spread(me, rows, out_ref, s2, r2)


def end_kernel(part_ref, resid_ref, out_ref, slots, s1, r1, s2, r2):
    rows = resid_ref.shape[0]
    me = rank_place()
    greet(me)
    total = scatter_sum(me, rows, part_ref, slots, s1, r1) + resid_ref[...]
    out_ref[pl.ds(pl.multiple_of(me * rows, rows), rows), :] = total.astype(BF)
    spread(me, rows, out_ref, s2, r2)


def back_kernel(
    part_ref, given_ref, value_ref, gain_ref, wide_ref, out_ref, gain_grad_ref, slots, s1, r1, s2, r2
):
    rows = given_ref.shape[0]
    me = rank_place()
    greet(me)
    grad = scatter_sum(me, rows, part_ref, slots, s1, r1)
    value = value_ref[...]
    scale = lax.rsqrt(jnp.mean(value * value, axis=-1, keepdims=True) + EPSILON)
    unit = value * scale
    gain_grad_ref[...] = jnp.sum(grad * unit, axis=0, keepdims=True)
    scaled = grad * gain_ref[...].astype(F32)
    total = given_ref[...] + scale * (
        scaled - unit * jnp.mean(scaled * unit, axis=-1, keepdims=True)
    )
    wide_ref[...] = total
    out_ref[pl.ds(pl.multiple_of(me * rows, rows), rows), :] = total.astype(BF)
    spread(me, rows, out_ref, s2, r2)


def rank_call(kernel, out_shape, rows, *args, after=()):
    return pl.pallas_call(
        ignoring(kernel, len(args), len(after)),
        out_shape=out_shape,
        in_specs=[VMEM_SPEC] * len(args) + [pl.BlockSpec(memory_space=pl.ANY)] * len(after),
        out_specs=[VMEM_SPEC] * len(out_shape),
        scratch_shapes=[pltpu.VMEM((RANKS - 1, rows, D), BF)]
        + [pltpu.SemaphoreType.DMA((RANKS - 1,))] * 4,
        cost_estimate=lasting(27),
        compiler_params=pltpu.CompilerParams(
            collective_id=channel(kernel.__name__, *args, *after),
            has_side_effects=True,
            vmem_limit_bytes=32 * 2**20,
        ),
    )(*args, *after)


def mid_step(part, resid, gain):
    rows = resid.shape[0]
    return rank_call(
        mid_kernel,
        [jax.ShapeDtypeStruct((rows, D), F32), jax.ShapeDtypeStruct(part.shape, BF)],
        rows,
        part,
        resid,
        gain[None],
    )


def end_step(part, resid):
    rows = resid.shape[0]
    return rank_call(end_kernel, [jax.ShapeDtypeStruct(part.shape, BF)], rows, part, resid)[0]


def back_step(part, given, value, gain, after=()):
    rows = given.shape[0]
    return rank_call(
        back_kernel,
        [
            jax.ShapeDtypeStruct((rows, D), F32),
            jax.ShapeDtypeStruct(part.shape, BF),
            jax.ShapeDtypeStruct((1, D), F32),
        ],
        rows,
        part,
        given,
        value,
        gain[None],
        after=after,
    )


def copy_kernel(value_ref, out_ref):
    out_ref[...] = value_ref[...]


def copy_after(value, *tokens):
    rows, width = value.shape
    tile = min(rows, 128)
    block = pl.BlockSpec((tile, width), lambda i: (i, 0))
    return pl.pallas_call(
        ignoring(copy_kernel, 1, len(tokens)),
        grid=(rows // tile,),
        out_shape=jax.ShapeDtypeStruct(value.shape, value.dtype),
        in_specs=[block] + [ANY_SPEC] * len(tokens),
        out_specs=block,
    )(value, *tokens)


def product_kernel(left_a, left_b, right_a, right_b, out_ref):
    turned = lambda left, right: lax.dot_general(
        left[...], right[...], (((0,), (0,)), ((), ())), preferred_element_type=F32
    )
    out_ref[...] = (turned(left_a, right_a) + turned(left_b, right_b)).astype(BF)


def outer_sum(left, right, tokens):
    rows, width = left[0].shape
    columns_right = right[0].shape[1]
    tile = 256
    left_block = pl.BlockSpec((rows, tile), lambda i: (0, i))
    right_block = pl.BlockSpec((rows, columns_right), lambda i: (0, 0))
    return pl.pallas_call(
        ignoring(product_kernel, 4, len(tokens)),
        grid=(width // tile,),
        out_shape=jax.ShapeDtypeStruct((width, columns_right), BF),
        in_specs=[left_block] * 2 + [right_block] * 2 + [ANY_SPEC] * len(tokens),
        out_specs=pl.BlockSpec((tile, columns_right), lambda i: (i, 0)),
        cost_estimate=lasting(3),
        compiler_params=pltpu.CompilerParams(vmem_limit_bytes=56 * 2**20),
    )(*left, *right, *tokens)


def share_kernel(one_ref, zero_ref, *refs):
    own, own_c, across, across_c, local_sem, send_sem, recv_sem = refs[-7:]
    s, y, core = (lax.axis_index(name) for name in ("section", "y", "core"))
    rows = one_ref.shape[0]
    half = rows // 2
    barrier = pltpu.get_barrier_semaphore()
    ids = {"section": {"section": 1 - s}, "y": {"y": 1 - y}, "core": {"core": 1 - core}}
    for who in ids.values():
        pl.semaphore_signal(barrier, inc=1, device_id=who, device_id_type=MESH)
    pl.semaphore_wait(barrier, 3)

    def remote(k, src, dst, axis):
        return pltpu.make_async_remote_copy(
            src_ref=src, dst_ref=dst, send_sem=send_sem.at[k], recv_sem=recv_sem.at[k],
            device_id=ids[axis], device_id_type=MESH,
        )

    part = lambda ref, k: ref.at[pl.ds(half * k, half)]
    slot = lambda ref, place, k: ref.at[place, pl.ds(half * k, half)]
    for section, mine, sent in ((0, zero_ref, one_ref), (1, one_ref, zero_ref)):

        @pl.when(s == section)
        def _():
            for k in range(2):
                remote(k, part(sent, k), slot(own, section, k), "section").start()
            for k in range(2):
                remote(2 + k, part(mine, k), slot(across, section, k), "y").start()
            remote(6, mine, own_c.at[section], "core").start()
            keep = pltpu.make_async_copy(mine, own.at[section], local_sem)
            keep.start()
            for k in range(2):
                remote(k, part(sent, k), slot(own, 1 - section, k), "section").wait_recv()
                remote(4 + k, slot(own, 1 - section, k), slot(across, 1 - section, k), "y").start()
                remote(
                    7 + k, slot(own, 1 - section, k), slot(own_c, 1 - section, k), "core"
                ).start()
            for k in range(2):
                remote(2 + k, part(mine, k), slot(across, section, k), "y").wait_recv()
                remote(
                    9 + k, slot(across, section, k), slot(across_c, section, k), "core"
                ).start()
            for k in range(2):
                there = slot(across, 1 - section, k)
                remote(4 + k, slot(own, 1 - section, k), there, "y").wait_recv()
                remote(11 + k, there, slot(across_c, 1 - section, k), "core").start()
            remote(6, mine, own_c.at[section], "core").wait_recv()
            for k in range(2):
                there = slot(own_c, 1 - section, k)
                remote(7 + k, slot(own, 1 - section, k), there, "core").wait_recv()
                there = slot(across_c, section, k)
                remote(9 + k, slot(across, section, k), there, "core").wait_recv()
                there = slot(across_c, 1 - section, k)
                remote(11 + k, slot(across, 1 - section, k), there, "core").wait_recv()
            for k in range(2):
                remote(k, part(sent, k), slot(own, section, k), "section").wait_send()
                remote(2 + k, part(mine, k), slot(across, section, k), "y").wait_send()
                there = slot(across, 1 - section, k)
                remote(4 + k, slot(own, 1 - section, k), there, "y").wait_send()
                there = slot(own_c, 1 - section, k)
                remote(7 + k, slot(own, 1 - section, k), there, "core").wait_send()
                there = slot(across_c, section, k)
                remote(9 + k, slot(across, section, k), there, "core").wait_send()
                there = slot(across_c, 1 - section, k)
                remote(11 + k, slot(across, 1 - section, k), there, "core").wait_send()
            remote(6, mine, own_c.at[section], "core").wait_send()
            keep.wait()


def share(one, zero, us, after=()):
    shape = jax.ShapeDtypeStruct((2,) + one.shape, one.dtype)
    return pl.pallas_call(
        ignoring(share_kernel, 2, len(after)),
        out_shape=[shape] * 4,
        in_specs=[ANY_SPEC] * (2 + len(after)),
        out_specs=[ANY_SPEC] * 4,
        scratch_shapes=[
            pltpu.SemaphoreType.DMA,
            pltpu.SemaphoreType.DMA((13,)),
            pltpu.SemaphoreType.DMA((13,)),
        ],
        cost_estimate=lasting(us),
        compiler_params=pltpu.CompilerParams(
            collective_id=channel("share", one, zero, *after), has_side_effects=True
        ),
    )(one, zero, *after)


def chosen(place_ref, refs):
    y, core = place_ref[0], place_ref[1]
    values = [ref[...] for ref in refs]
    found = [[None, None], [None, None]]
    for side in range(2):
        flat = [jnp.where(core == side, values[2 * k], values[2 * k + 1]) for k in range(2)]
        for row in range(2):
            found[row][side] = jnp.where(y == row, flat[0], flat[1])
    return found


def rows_kernel(place_ref, a, b, c, d, out_ref):
    found = chosen(place_ref, (a, b, c, d))
    row = lax.rem(pl.program_id(0), 2)
    for side in range(2):
        value = jnp.where(row == 0, found[0][side][0], found[1][side][0])
        out_ref[:, HALF * side : HALF * (side + 1)] = value.astype(F32)


PLACE_SPEC = pl.BlockSpec(memory_space=pltpu.SMEM)


def spread_rows(place, pieces, first, count, tile):
    steps = count // tile
    block = pl.BlockSpec((1, tile, HALF), lambda r, i: (r // 2, first // tile + i, 0))
    return pl.pallas_call(
        rows_kernel,
        grid=(RANKS, steps),
        out_shape=jax.ShapeDtypeStruct((RANKS * count, D), F32),
        in_specs=[PLACE_SPEC] + [block] * 4,
        out_specs=pl.BlockSpec((tile, D), lambda r, i: (r * steps + i, 0)),
        compiler_params=pltpu.CompilerParams(vmem_limit_bytes=56 * 2**20),
    )(place, *pieces)


def gate_up_kernel(nz, place_ref, a, b, c, d, out_ref):
    found = chosen(place_ref, (a, b, c, d))
    width = R_FF // nz
    for side in range(2):
        for shard in range(nz):
            for rank in range(RANKS):
                start = FF * side + (FF // nz) * shard + width * rank
                out_ref[:, start : start + width] = found[rank % 2][side][
                    rank // 2, :, width * shard : width * (shard + 1)
                ].astype(F32)


def spread_gate_up(place, pieces, nz):
    rows = pieces[0].shape[1]
    tile = min(rows, 64)
    block = pl.BlockSpec((2, tile, HALF), lambda i: (0, i, 0))
    return pl.pallas_call(
        functools.partial(gate_up_kernel, nz),
        grid=(rows // tile,),
        out_shape=jax.ShapeDtypeStruct((rows, 2 * FF), F32),
        in_specs=[PLACE_SPEC] + [block] * 4,
        out_specs=pl.BlockSpec((tile, 2 * FF), lambda i: (i, 0)),
        compiler_params=pltpu.CompilerParams(vmem_limit_bytes=56 * 2**20),
    )(place, *pieces)


def in_kernel(place_ref, a, b, c, d, in_ref, qkv_ref):
    found = chosen(place_ref, (a, b, c, d))
    for rank in range(RANKS):
        left, right = (found[rank % 2][side][rank // 2].astype(F32) for side in range(2))
        in_ref[R_SSM * rank : R_SSM * (rank + 1)] = right[:, :R_SSM].T
        start = D_SSM + R_SSM * rank
        in_ref[start : start + R_SSM] = left[:, :R_SSM].T
        start = 2 * D_SSM + R_BC * rank
        in_ref[start : start + R_BC] = left[:, R_SSM:R_CONV].T
        qkv_ref[:, R_ATT * rank : R_ATT * (rank + 1)] = right[:, R_SSM:]
        start = ATT + KV * (rank % 2) + HEAD_DIM * (rank // 2)
        qkv_ref[:, start : start + HEAD_DIM] = left[:, R_CONV:]


def dt_kernel(whole_ref, dt_ref, out_ref):
    out_ref[...] = dt_ref[...]


def with_dt(whole, dt):
    rows, width = dt.shape
    tile = 16
    first = (whole.shape[0] - rows) // tile
    return pl.pallas_call(
        dt_kernel,
        grid=(rows // tile,),
        out_shape=jax.ShapeDtypeStruct(whole.shape, whole.dtype),
        in_specs=[ANY_SPEC, pl.BlockSpec((tile, width), lambda i: (i, 0))],
        out_specs=pl.BlockSpec((tile, width), lambda i: (first + i, 0)),
        input_output_aliases={0: 0},
    )(whole, dt)


def spread_in(place, pieces):
    rows = pieces[0].shape[1]
    tile = min(rows, 128)
    block = pl.BlockSpec((2, tile, HALF), lambda i: (0, i, 0))
    return pl.pallas_call(
        in_kernel,
        grid=(rows // tile,),
        out_shape=[
            jax.ShapeDtypeStruct((D_IN, rows), F32),
            jax.ShapeDtypeStruct((rows, ATT + 2 * KV), F32),
        ],
        in_specs=[PLACE_SPEC] + [block] * 4,
        out_specs=[
            pl.BlockSpec((D_IN, tile), lambda i: (0, i)),
            pl.BlockSpec((tile, ATT + 2 * KV), lambda i: (i, 0)),
        ],
        compiler_params=pltpu.CompilerParams(vmem_limit_bytes=56 * 2**20),
    )(place, *pieces)


LANES = 128


def turned_lanes(values, cosine, sine):
    parts = []
    for start in range(0, values.shape[1], HEAD_DIM):
        head = values[:, start : start + HEAD_DIM]
        parts.append(head * cosine + pltpu.roll(head, HEAD_DIM // 2, 1) * sine)
    return parts[0] if len(parts) == 1 else jnp.concatenate(parts, axis=1)


def exact(left, right, contract):
    return lax.dot_general(
        left, right, (contract, ((), ())), precision=HIGHEST, preferred_element_type=F32
    )


def mixer_back_kernel(
    nz, got_ref, scan_ref, z_ref, norm_ref, gain_ref, x_ref, b_ref, c_ref, raw_ref, heads_ref,
    run_ref, dt_ref, q_ref, k_ref, v_ref, probs_ref, cos_ref, sin_ref,
    message_ref, right_ref, dx_ref, draw_ref, heads_out_ref, lanes_out_ref,
):
    length = scan_ref.shape[0]
    inner = nz // RANKS
    wide, narrow_w = R_OUT // nz, R_SSM // nz
    d_norm = jnp.concatenate(
        [
            got_ref[r][:, wide * i : wide * i + narrow_w].astype(F32)
            for i in range(inner)
            for r in range(RANKS)
        ],
        axis=1,
    )
    d_o = jnp.concatenate(
        [
            got_ref[r][:, wide * i + narrow_w : wide * (i + 1)].astype(F32)
            for i in range(inner)
            for r in range(RANKS)
        ],
        axis=1,
    ).astype(BF)
    spread_of, overlap = norm_ref[:, 0:1], norm_ref[:, 1:2]
    scan, z = scan_ref[...], z_ref[...]
    sig = jax.nn.sigmoid(z)
    silu = z * sig
    gated = scan * silu
    lanes_out_ref[0:1, :] = jnp.sum(d_norm * gated * spread_of, axis=0, keepdims=True)
    d_gated = spread_of * d_norm * gain_ref[...] - gated * (
        spread_of * spread_of * overlap * (1.0 / D_SSM)
    )
    d_scan = d_gated * silu
    right_ref[:, :R_SSM] = (d_gated * scan * (sig * (1.0 + z * (1.0 - sig)))).astype(BF)

    row = lax.broadcasted_iota(jnp.int32, (length, length), 0)
    column = lax.broadcasted_iota(jnp.int32, (length, length), 1)
    allowed = row >= column

    scale = HEAD_DIM**-0.5
    key, value = k_ref[...], v_ref[...]
    d_key = jnp.zeros((length, HEAD_DIM), F32)
    d_value = jnp.zeros((length, HEAD_DIM), F32)
    for head in range(R_ATT // HEAD_DIM):
        cut = slice(HEAD_DIM * head, HEAD_DIM * (head + 1))
        query, grad, probs = q_ref[:, cut], d_o[:, cut], probs_ref[head]
        d_probs = dot_t(grad, value)
        d_scores = (
            probs * (d_probs - jnp.sum(probs * d_probs, axis=1, keepdims=True))
        ).astype(BF)
        d_query = dot(d_scores, key) * scale
        right_ref[:, R_SSM + HEAD_DIM * head : R_SSM + HEAD_DIM * (head + 1)] = turned_lanes(
            d_query, cos_ref[...], -sin_ref[...]
        ).astype(BF)
        d_key = d_key + t_dot(d_scores, query) * scale
        d_value = d_value + t_dot(probs.astype(BF), grad)

    b_rows, c_rows = b_ref[...], c_ref[...]
    mixing = dot_t(c_rows, b_rows)
    x = x_ref[...]
    lanes_out_ref[1:2, :] = jnp.sum(d_scan * x.astype(F32), axis=0, keepdims=True)
    grad_b = d_scan.astype(BF)
    run_t, dt_t = run_ref[...].T, dt_ref[...].T
    d_mixing = jnp.zeros((length, length), F32)
    lane = lax.broadcasted_iota(jnp.int32, (length, LANES), 1)
    head_row = lax.broadcasted_iota(jnp.int32, (LANES, length), 0)
    by_row = jnp.zeros((length, LANES), F32)
    direct = jnp.zeros((LANES, length), F32)
    for pair in range(R_HEADS // 2):
        cut = slice(LANES * pair, LANES * (pair + 1))
        x_pair, g_pair = x[:, cut], grad_b[:, cut]
        d_pair = []
        for side in range(2):
            head = 2 * pair + side
            mine = (lane < SSM_HEAD) if side == 0 else (lane >= SSM_HEAD)
            d_weights = dot_t(jnp.where(mine, g_pair, jnp.zeros_like(g_pair)), x_pair)
            gap = run_ref[:, head : head + 1] - run_t[head : head + 1, :]
            table = jnp.exp(jnp.where(allowed, gap, NEGATIVE))
            dt_row = dt_t[head : head + 1, :]
            faded = d_weights * table
            faded_dt = faded * dt_row
            d_mixing = d_mixing + faded_dt
            plain = faded * mixing
            direct = jnp.where(head_row == head, jnp.sum(plain, axis=0, keepdims=True), direct)
            by_row = jnp.where(
                lane == head, jnp.sum(faded_dt * mixing, axis=1, keepdims=True), by_row
            )
            weights = (table * mixing * dt_row).astype(BF)
            d_pair.append(t_dot(weights, g_pair))
        skip = jnp.where(
            lane[:1] < SSM_HEAD,
            heads_ref[2:3, 2 * pair : 2 * pair + 1],
            heads_ref[2:3, 2 * pair + 1 : 2 * pair + 2],
        )
        dx_ref[:, cut] = jnp.where(lane < SSM_HEAD, d_pair[0], d_pair[1]) + skip * d_scan[:, cut]
    d_mixing = d_mixing.astype(BF)
    d_c = dot(d_mixing, b_rows)
    d_b = t_dot(d_mixing, c_rows)
    for r in range(RANKS):
        source = d_b if r < 2 else d_c
        start = R_BC * (r % 2)
        message_ref[r, :, :R_BC] = source[:, start : start + R_BC].astype(BF)
        message_ref[r, :, R_BC:] = (d_key if r % 2 == 0 else d_value).astype(BF)

    later = (column >= row).astype(F32)
    from_rows_sum = exact(later, by_row, ((1,), (0,)))
    grad_step = from_rows_sum - exact(later, direct * dt_t, ((1,), (1,)))
    grad_dt = direct.T
    bias, log = heads_ref[0:1, :], heads_ref[1:2, :]
    raw = raw_ref[...] + bias
    rate = jnp.exp(log)
    step = -jax.nn.softplus(raw) * rate
    valid = lane < R_HEADS
    grad_dt = grad_dt - grad_step * rate
    grad_raw = jnp.where(valid, grad_dt * jax.nn.sigmoid(raw), 0.0)
    draw_ref[...] = grad_raw.astype(BF)
    heads_out_ref[0:1, :] = jnp.sum(grad_raw, axis=0, keepdims=True)
    heads_out_ref[1:2, :] = jnp.sum(grad_step * step, axis=0, keepdims=True)


def whole_block(array):
    shape = array.shape
    return pl.BlockSpec(shape, lambda i: (0,) * len(shape), pipeline_mode=pl.Buffered(1))


def mixer_back(got, kept, small, overlap, tables):
    length = got.shape[1]
    nz = lax.axis_size("fsdp")
    norm = jnp.stack([kept["spread"], overlap], axis=1)
    shape = jax.ShapeDtypeStruct
    out_shape = [
        shape((RANKS, length, 2 * R_BC), BF),
        shape((length, HALF), BF),
        shape((length, R_SSM), F32),
        shape((length, LANES), BF),
        shape((8, LANES), F32),
        shape((8, R_SSM), F32),
    ]
    args = (
        got, kept["scan"], kept["z"], norm, small["ssm_gain"][None], kept["u"][:, :R_SSM],
        kept["b"], kept["c"], kept["dt_raw"], small["heads"], kept["running"], kept["dt"],
        kept["query"], kept["key"], kept["value"],
        kept["probs"], *tables,
    )
    return pl.pallas_call(
        functools.partial(mixer_back_kernel, nz),
        grid=(1,),
        out_shape=out_shape,
        in_specs=[whole_block(arg) for arg in args],
        out_specs=[whole_block(out) for out in out_shape],
        cost_estimate=lasting(16),
        compiler_params=pltpu.CompilerParams(vmem_limit_bytes=56 * 2**20),
    )(*args)


def conv_back_kernel(
    place_ref, back_ref, dx_ref, xbc_ref, table_ref, cos_ref, sin_ref, left_ref, conv_ref
):
    y, s = place_ref[0], place_ref[1]
    length = dx_ref.shape[0]
    back = [back_ref[r].astype(F32) for r in range(RANKS)]
    d_bc = (back[0] + back[1] + back[2] + back[3])[:, :R_BC]
    d_kv = jnp.where(s == 0, back[0] + back[1], back[2] + back[3])[:, R_BC:]
    d_kv = jnp.where(y == 0, turned_lanes(d_kv, cos_ref[...], -sin_ref[...]), d_kv)
    left_ref[:, R_CONV:] = d_kv.astype(BF)
    d_u = jnp.concatenate([dx_ref[...], d_bc], axis=1)
    wide = xbc_ref[...].astype(F32)
    place = lax.broadcasted_iota(jnp.int32, (length, R_CONV), 0)
    moved = []
    before = table_ref[CONV_K : CONV_K + 1, :] + jnp.zeros_like(wide)
    for tap in range(CONV_K):
        steps = CONV_K - 1 - tap
        value = wide
        if steps:
            value = jnp.where(place >= steps, pltpu.roll(wide, steps, 0), 0.0)
        moved.append(value)
        before = before + table_ref[tap : tap + 1, :] * value
    sig = jax.nn.sigmoid(before)
    d_before = d_u * (sig * (1.0 + before * (1.0 - sig)))
    d_xbc = jnp.zeros_like(wide)
    for tap in range(CONV_K):
        conv_ref[tap : tap + 1, :] = jnp.sum(d_before * moved[tap], axis=0, keepdims=True)
        steps = CONV_K - 1 - tap
        value = d_before
        if steps:
            value = jnp.where(
                place < length - steps, pltpu.roll(d_before, length - steps, 0), 0.0
            )
        d_xbc = d_xbc + table_ref[tap : tap + 1, :] * value
    conv_ref[CONV_K : CONV_K + 1, :] = jnp.sum(d_before, axis=0, keepdims=True)
    left_ref[:, :R_CONV] = d_xbc.astype(BF)


def conv_back(back, d_x, xbc, table, tables):
    length = d_x.shape[0]
    place = jnp.stack([lax.axis_index("y"), lax.axis_index("section")]).astype(jnp.int32)
    args = (back, d_x, xbc, table, *tables)
    out_shape = [
        jax.ShapeDtypeStruct((length, HALF), BF),
        jax.ShapeDtypeStruct((8, R_CONV), F32),
    ]
    return pl.pallas_call(
        conv_back_kernel,
        grid=(1,),
        out_shape=out_shape,
        in_specs=[PLACE_SPEC] + [whole_block(arg) for arg in args],
        out_specs=[whole_block(out) for out in out_shape],
        cost_estimate=lasting(7),
        compiler_params=pltpu.CompilerParams(vmem_limit_bytes=56 * 2**20),
    )(place, *args)


def rotation_tables(length):
    half = HEAD_DIM // 2
    frequency = ROPE_BASE ** (-jnp.arange(half, dtype=F32) / half)
    angles = jnp.arange(length, dtype=F32)[:, None] * frequency[None, :]
    cosine, sine = jnp.cos(angles), jnp.sin(angles)
    return jnp.concatenate([cosine, cosine], 1), jnp.concatenate([-sine, sine], 1)


def narrow(values):
    return values.astype(BF)


def dot(left, right):
    return jnp.dot(left, right, preferred_element_type=F32)


def dot_t(left, right):
    return lax.dot_general(left, right, (((1,), (1,)), ((), ())), preferred_element_type=F32)


def t_dot(left, right):
    return lax.dot_general(left, right, (((0,), (0,)), ((), ())), preferred_element_type=F32)


def columns(array, start, width):
    return lax.dynamic_slice_in_dim(array, start, width, axis=1)


def cut_rows(array, start, width):
    return lax.dynamic_slice_in_dim(array, start, width, axis=0)


def rms(values, gain):
    return values * lax.rsqrt(jnp.mean(values * values, axis=-1, keepdims=True) + EPSILON) * gain


def rotary(values, turning):
    length, width = values.shape
    half = HEAD_DIM // 2
    frequency = ROPE_BASE ** (-jnp.arange(half, dtype=F32) / half)
    angles = jnp.arange(length, dtype=F32)[:, None] * frequency[None, :]
    cosine = jnp.cos(angles)[:, None, :]
    sine = turning * jnp.sin(angles)[:, None, :]
    halves = values.reshape(length, width // HEAD_DIM, 2, half)
    first, second = halves[:, :, 0], halves[:, :, 1]
    return jnp.stack(
        [first * cosine - second * sine, second * cosine + first * sine], axis=2
    ).reshape(length, width)


def causal(length):
    position = jnp.arange(length)
    return position[:, None] >= position[None, :]


def shifted(values, steps):
    if steps == 0:
        return values
    blank = jnp.zeros((abs(steps), values.shape[1]), values.dtype)
    if steps > 0:
        return jnp.concatenate([blank, values[:-steps]], axis=0)
    return jnp.concatenate([values[-steps:], blank], axis=0)


def conv_sum(rows, table):
    wide = rows.astype(F32)
    total = table[CONV_K][None, :]
    for tap in range(CONV_K):
        total = total + table[tap][None, :] * shifted(wide, CONV_K - 1 - tap)
    return total


def decays(dt_raw, heads):
    dt = jax.nn.softplus(dt_raw + heads[0][None, :])
    step = -dt * jnp.exp(heads[1])[None, :]
    length = dt.shape[0]
    running = jnp.dot(causal(length).astype(F32), step, precision=HIGHEST)
    return dt, step, running


def decay_table(running):
    length = running.shape[0]
    turned = running.T
    gap = turned[:, :, None] - turned[:, None, :]
    return jnp.exp(jnp.where(causal(length)[None], gap, NEGATIVE))


def by_head(values):
    return values.reshape(values.shape[0], R_HEADS, SSM_HEAD)


def scan_forward(x, b_rows, c_rows, dt_raw, heads):
    dt, _, running = decays(dt_raw, heads)
    mixing = dot_t(c_rows, b_rows)
    weights = narrow(decay_table(running[:, :R_HEADS]) * mixing[None] * dt.T[:R_HEADS, None, :])
    x_heads = by_head(x)
    result = jnp.einsum("hts,shp->thp", weights, x_heads, preferred_element_type=F32)
    result = result + heads[2][None, :R_HEADS, None] * x_heads.astype(F32)
    return result.reshape(x.shape), running, dt


def scan_backward(x, b_rows, c_rows, dt_raw, heads, grad_y):
    dt, step, running = decays(dt_raw, heads)
    length = x.shape[0]
    mixing = dot_t(c_rows, b_rows)
    table = decay_table(running)
    dt_t = dt.T
    x_heads = by_head(x)
    grad_heads = by_head(narrow(grad_y))
    grad_weights = jnp.einsum("thp,shp->hts", grad_heads, x_heads, preferred_element_type=F32)
    faded = grad_weights * table
    weights = table * mixing[None] * dt_t[:, None, :]
    grad_x = jnp.einsum("hts,thp->shp", narrow(weights), grad_heads, preferred_element_type=F32)
    grad_y_heads = by_head(grad_y)
    grad_x = grad_x + heads[2][None, :, None] * grad_y_heads
    grad_skip = jnp.sum(grad_y_heads * x_heads.astype(F32), axis=(0, 2))
    grad_mixing = narrow(jnp.sum(faded * dt_t[:, None, :], axis=0))
    grad_c = dot(grad_mixing, b_rows)
    grad_b = t_dot(grad_mixing, c_rows)
    plain = faded * mixing[None]
    grad_dt = jnp.sum(plain, axis=1)
    grad_gap = plain * dt_t[:, None, :]
    grad_running = jnp.sum(grad_gap, axis=2) - jnp.sum(grad_gap, axis=1)
    grad_step = jnp.dot(grad_running, causal(length).astype(F32), precision=HIGHEST).T
    grad_dt = grad_dt.T - grad_step * jnp.exp(heads[1])[None, :]
    grad_log = jnp.sum(grad_step * step, axis=0)
    grad_raw = grad_dt * jax.nn.sigmoid(dt_raw + heads[0][None, :])
    grad_table = jnp.stack([jnp.sum(grad_raw, axis=0), grad_log, grad_skip])
    return grad_x.reshape(x.shape), grad_b, grad_c, grad_raw, grad_table


def attend(query, key, value):
    length = query.shape[0]
    heads = query.reshape(length, -1, HEAD_DIM)
    scores = jnp.einsum("qhd,sd->hqs", heads, key, preferred_element_type=F32) * HEAD_DIM**-0.5
    scores = jnp.where(causal(length)[None], scores, NEGATIVE)
    weights = jnp.exp(scores - jnp.max(scores, axis=-1, keepdims=True))
    probs = weights / jnp.sum(weights, axis=-1, keepdims=True)
    mixed = jnp.einsum("hqs,sd->qhd", narrow(probs), value, preferred_element_type=F32)
    return narrow(mixed.reshape(query.shape)), probs


def attend_back(query, key, value, probs, grad_out):
    length = query.shape[0]
    heads = query.reshape(length, -1, HEAD_DIM)
    grad_heads = grad_out.reshape(length, -1, HEAD_DIM)
    grad_probs = jnp.einsum("qhd,sd->hqs", grad_heads, value, preferred_element_type=F32)
    grad_scores = narrow(
        probs * (grad_probs - jnp.sum(probs * grad_probs, axis=-1, keepdims=True))
    )
    scale = HEAD_DIM**-0.5
    grad_query = jnp.einsum("hqs,sd->qhd", grad_scores, key, preferred_element_type=F32) * scale
    grad_key = jnp.einsum("hqs,qhd->sd", grad_scores, heads, preferred_element_type=F32) * scale
    grad_value = jnp.einsum("hqs,qhd->sd", narrow(probs), grad_heads, preferred_element_type=F32)
    return grad_query.reshape(query.shape), grad_key, grad_value


def flip(value, axis):
    return lax.ppermute(value, axis, [(0, 1), (1, 0)])


def layer_forward(entering, resid, weights, small, first):
    s, y = lax.axis_index("section"), lax.axis_index("y")
    length = entering.shape[0]
    x1 = narrow(rms(entering.astype(F32), small["gain0"][None, :]))
    left = dot(x1, weights["in"][0])
    right = dot(x1, weights["in"][1])
    dt_raw = dot(x1, weights["dt"])
    xbc = narrow(left[:, :R_CONV])
    u = narrow(jax.nn.silu(conv_sum(xbc, small["conv"])))
    kv_raw = left[:, R_CONV:]
    kv = narrow(jnp.where(y == 0, rotary(kv_raw, 1.0), kv_raw))
    shared = swap(jnp.concatenate([u[:, R_SSM:], kv], axis=1))
    b_rows = jnp.concatenate([shared[0, :, :R_BC], shared[1, :, :R_BC]], axis=1)
    c_rows = jnp.concatenate([shared[2, :, :R_BC], shared[3, :, :R_BC]], axis=1)
    pair = lax.dynamic_slice_in_dim(shared, 2 * s, 2, axis=0)[:, :, R_BC:]
    key, value = pair[0], pair[1]
    z = right[:, :R_SSM]
    query = narrow(rotary(right[:, R_SSM:], 1.0))
    o, probs = attend(query, key, value)
    x = u[:, :R_SSM]
    scan, running, dt = scan_forward(x, b_rows, c_rows, dt_raw, small["heads"])
    gated = scan * jax.nn.silu(z)
    squares = jnp.sum(gated * gated, axis=1)
    scaled = narrow(gated * small["ssm_gain"][None, :])
    message = to_rows(scaled, o)
    stat = jnp.broadcast_to(squares[None, :], (8, length))
    got, stats = swap(message, stat)
    spread_of = lax.rsqrt(jnp.sum(stats[:, 0, :], axis=0) / D_SSM + EPSILON)
    wide = jnp.transpose(got, (1, 0, 2)).reshape(length, R_OUT)
    is_ssm = small["is_ssm"][None, :]
    mo = narrow(jnp.where(is_ssm, wide.astype(F32) * spread_of[:, None], wide.astype(F32)))
    part = jnp.concatenate([dot(mo, weights["out"][0]), dot(mo, weights["out"][1])], axis=1)
    mid, x2 = mid_step(narrow(part), resid, small["gain1"])
    gate = dot(x2, weights["gu"][0])
    up = dot(x2, weights["gu"][1])
    act = narrow(jax.nn.silu(gate) * up)
    part2 = jnp.concatenate([dot(act, weights["down"][0]), dot(act, weights["down"][1])], axis=1)
    leaving = end_step(narrow(part2), mid)
    kept = dict(
        resid=resid, x1=x1, xbc=xbc, u=u, b=b_rows, c=c_rows, key=key, value=value, query=query,
        probs=probs, z=z, dt_raw=dt_raw, scan=scan, spread=spread_of, mo=mo, mid=mid, x2=x2,
        gate=gate, up=up, act=act, running=running, dt=dt,
    )
    return leaving, kept


def to_rows(ssm_part, att_part):
    length = ssm_part.shape[0]
    nz = lax.axis_size("fsdp")
    inner = nz // RANKS
    a = ssm_part.reshape(length, inner, RANKS, R_SSM // nz)
    b = att_part.reshape(length, inner, RANKS, R_ATT // nz)
    both = jnp.concatenate([a, b], axis=3)
    return jnp.transpose(both, (2, 0, 1, 3)).reshape(RANKS, length, R_OUT // RANKS)


def from_rows(got):
    length = got.shape[1]
    nz = lax.axis_size("fsdp")
    inner = nz // RANKS
    both = jnp.transpose(got.reshape(RANKS, length, inner, R_OUT // nz), (1, 2, 0, 3))
    a = both[..., : R_SSM // nz].reshape(length, R_SSM)
    b = both[..., R_SSM // nz :].reshape(length, R_ATT)
    return a, b


def layer_backward(grad, given, kept, weights, small, queue, layer, tables, first=()):
    s, y = lax.axis_index("section"), lax.axis_index("y")
    core = lax.axis_index("core")
    length = grad.shape[0]
    down, gu, out, win = weights["down"], weights["gu"], weights["out"], weights["in"]

    def product(left, right, *tokens):
        mine = jnp.where(core == 0, right[0], right[1])
        theirs = jnp.where(core == 0, right[1], right[0])
        return outer_sum((left, flip(left, "core")), (mine, flip(theirs, "core")), tokens)

    def reduce(name, block):
        nonlocal queue
        if queue:
            block, queue["last"] = lax.optimization_barrier((block, queue["last"]))
        queue[name] = queue["last"] = lax.psum_scatter(
            block, "fsdp", scatter_dimension=0, tiled=True
        )

    def due(point):
        return [queue[k] for k in WAITS[layer].get(point, ())]

    halves = lambda v: (v[:, :HALF], v[:, HALF:])
    g0, g1 = halves(grad)
    down_block = functools.partial(product, kept["act"], (g0, g1))
    if layer == 1:
        reduce("down1", down_block())
    grad_act = dot_t(g0, down[0]) + dot_t(g1, down[1])
    gate, up = kept["gate"], kept["up"]
    sig = jax.nn.sigmoid(gate)
    d_gate = narrow(grad_act * up * (sig * (1.0 + gate * (1.0 - sig))))
    d_up = narrow(grad_act * gate * sig)
    if layer == 1:
        reduce("gu1", product(kept["x2"], (d_gate, d_up), *first))
    part = dot_t(d_gate, gu[0]) + dot_t(d_up, gu[1])
    d_mid, db, grad_gain1 = back_step(
        narrow(part), given, kept["mid"], small["gain1"], due("mlp") + list(first)
    )
    if layer == 0:
        reduce("gu0", product(kept["x2"], (d_gate, d_up), db))
    b0, b1 = halves(db)
    d_mo = dot_t(b0, out[0]) + dot_t(b1, out[1])
    mo = kept["mo"]
    is_ssm = small["is_ssm"][None, :]
    stat_row = jnp.sum(jnp.where(is_ssm, d_mo * mo.astype(F32), 0.0), axis=1)
    stat = jnp.broadcast_to(stat_row[None, :], (8, length))
    blocks = jnp.transpose(narrow(d_mo).reshape(length, RANKS, R_OUT // RANKS), (1, 0, 2))
    got, stats = swap(blocks, stat, due("norm"))
    overlap = jnp.sum(stats[:, 0, :], axis=0)
    message, d_right, d_x, d_raw, head_sums, lane_sums = mixer_back(
        got, kept, small, overlap, tables
    )
    skip = jnp.sum(lane_sums[1].reshape(R_HEADS, SSM_HEAD), axis=1)
    grad_heads = jnp.concatenate([head_sums[:2, :R_HEADS], skip[None]], axis=0)
    grad_ssm_gain = lane_sums[0]
    if layer == 1:
        reduce("out1", product(kept["mo"], (b0, b1), message))
    back = swap(message, None, due("scan"))
    d_left, grad_conv = conv_back(back, d_x, kept["xbc"], small["conv"], tables)
    grad_conv = grad_conv[: CONV_K + 1]
    part = dot_t(d_left, win[0]) + dot_t(d_right, win[1]) + dot_t(d_raw, weights["dt"])
    part = narrow(part)
    reduce(f"in{layer}", product(kept["x1"], (d_left, d_right), part))
    _, entering_grad, grad_gain0 = back_step(
        part,
        d_mid,
        kept["resid"].astype(F32),
        small["gain0"],
        due("in"),
    )
    got_gu = None
    if layer == 0:
        got_gu = share(queue["gu1"], queue["gu0"], 50, (entering_grad,))
        reduce("out0", product(kept["mo"], (b0, b1), got_gu[0]))
    two = lambda v: jnp.concatenate([v, flip(v, "core")], axis=0)
    grad_dt_w = t_dot(two(d_raw[:, :16]), two(kept["x1"]))
    smalls_grad = dict(
        heads=grad_heads, conv=grad_conv, ssm=grad_ssm_gain[None], dt=grad_dt_w,
        gains=jnp.concatenate([grad_gain0, grad_gain1], axis=0),
    )
    return entering_grad, smalls_grad, (down_block, reduce, got_gu)


WAITS = (
    {"mlp": ("out1",), "scan": ("in1",)},
    {"norm": ("down1",), "in": ("gu1",)},
)


def body(
    inputs, cotangent, norm_gains, head_params, conv_params, ssm_gain,
    w_in, w_out, w_qkv, w_o, w_gu, w_down,
):
    s, y = lax.axis_index("section"), lax.axis_index("y")
    core = lax.axis_index("core")
    nz = lax.axis_size("fsdp")
    z_place = lax.axis_index("fsdp")
    rank = 2 * s + y
    rows = inputs.shape[2]
    length = RANKS * rows
    w_in, w_out, w_qkv, w_o, w_gu, w_down = (
        w[0] for w in (w_in, w_out, w_qkv, w_o, w_gu, w_down)
    )

    flat = jnp.concatenate(
        [
            norm_gains[0].reshape(-1),
            head_params[0].reshape(-1),
            conv_params[0].reshape(-1),
            ssm_gain[0],
            w_in[:, D_SSM + CONV_W :].reshape(-1),
        ]
    )
    count = flat.shape[0]
    flat = jnp.pad(flat, (0, -count % 2048)).reshape(-1, 128)
    everything = lax.all_gather(flat, ("section", "fsdp"), axis=0).reshape(2, nz, -1)[..., :count]

    def unpack(layer):
        part = everything[layer]
        sizes = [2 * D // nz, 3 * SSM_HEADS // nz, 5 * CONV_W // nz, D_SSM // nz]
        starts = [0]
        for size in sizes:
            starts.append(starts[-1] + size)
        join = lambda k, lead: jnp.transpose(
            part[:, starts[k] : starts[k + 1]].reshape(nz, lead, -1), (1, 0, 2)
        ).reshape(lead, -1).astype(F32)
        gains, heads, conv, gain = join(0, 2), join(1, 3), join(2, 5), join(3, 1)[0]
        conv_own = jnp.concatenate(
            [columns(conv, R_SSM * rank, R_SSM), columns(conv, D_SSM + R_BC * rank, R_BC)], axis=1
        )
        channel = jnp.arange(R_OUT) % (R_OUT // nz)
        small = dict(
            gain0=gains[0],
            gain1=gains[1],
            heads=jnp.pad(
                columns(heads, R_HEADS * rank, R_HEADS), ((0, 0), (0, LANES - R_HEADS))
            ),
            conv=conv_own,
            ssm_gain=lax.dynamic_slice_in_dim(gain, R_SSM * rank, R_SSM),
            is_ssm=channel < R_SSM // nz,
        )
        dt_w = columns(part[:, starts[4] :].reshape(D, SSM_HEADS), R_HEADS * rank, R_HEADS)
        return small, jnp.pad(dt_w, ((0, 0), (0, LANES - R_HEADS)))

    def pieces(section):
        rk = 2 * section + y
        first = columns(w_in, jnp.where(core == 0, D_SSM, 0) + R_SSM * rk, R_SSM)
        second = jnp.where(
            core == 0,
            columns(w_in, 2 * D_SSM + R_BC * rk, R_BC),
            columns(w_qkv, R_ATT * rk, HEAD_DIM),
        )
        third = columns(
            w_qkv,
            jnp.where(core == 0, ATT + KV * y + HEAD_DIM * section, R_ATT * rk + HEAD_DIM),
            HEAD_DIM,
        )
        side = HALF * core
        out_rows, o_rows, down_rows = R_SSM // nz, R_ATT // nz, R_FF // nz
        ff = R_FF // nz
        return {
            "in": jnp.concatenate([first, second, third], axis=1),
            "out": jnp.concatenate(
                [
                    lax.dynamic_slice(w_out, (out_rows * rk, side), (out_rows, HALF)),
                    lax.dynamic_slice(w_o, (o_rows * rk, side), (o_rows, HALF)),
                ],
                axis=0,
            ),
            "gu": jnp.concatenate(
                [
                    columns(w_gu, FF * core + (FF // nz) * k + ff * rk, ff) for k in range(nz)
                ],
                axis=1,
            ),
            "down": lax.dynamic_slice(w_down, (down_rows * rk, side), (down_rows, HALF)),
        }

    order = []

    def in_turn(value):
        if order:
            value, order[-1] = lax.optimization_barrier((value, order[-1]))
        return value

    def gather(piece):
        order.append(lax.all_gather(in_turn(piece), ("core", "fsdp"), axis=0))
        return order[-1]

    own, other = pieces(s), pieces(1 - s)
    out_own = gather(own["out"])
    mlp = lambda found: jnp.concatenate([found["gu"], found["down"]], axis=0)
    in_arrived = flip(other["in"], "section")
    out_sent, in_arrived = lax.optimization_barrier((other["out"], in_arrived))
    out_arrived = flip(out_sent, "section")
    mlp_own = mlp(own)
    mlp_sent, out_arrived = lax.optimization_barrier((mlp(other), out_arrived))
    mlp_arrived = flip(mlp_sent, "section")
    of_layer = lambda layer, mine, theirs: jnp.where(s == layer, mine, theirs)
    flat_rows = lambda whole: whole.reshape(2, -1, HALF)
    in0 = gather(copy_after(of_layer(0, own["in"], in_arrived), everything))
    out_other = gather(copy_after(out_arrived, in0))
    wide = own["gu"].shape[0]
    mlp0, mlp1 = (of_layer(layer, mlp_own, mlp_arrived) for layer in range(2))
    gu0 = gather(mlp0[:wide])
    down0 = gather(mlp0[wide:])
    in1 = gather(of_layer(1, own["in"], in_arrived))
    gu1 = gather(mlp1[:wide])
    down1 = gather(mlp1[wide:])
    weights = [
        dict(
            out=flat_rows(of_layer(layer, out_own, out_other)),
            **{"in": flat_rows((in0, in1)[layer])},
        )
        for layer in range(2)
    ]
    weights[0]["gu"] = flat_rows(gu0)
    weights[0]["down"] = flat_rows(down0)
    weights[1]["gu"] = flat_rows(gu1)
    weights[1]["down"] = flat_rows(down1)

    def whole_sequence(own_rows):
        place = 2 * y + core
        result = jnp.zeros((RANKS, rows, D), BF)
        result = lax.dynamic_update_index_in_dim(
            result, lax.dynamic_index_in_dim(own_rows, core, 0, False), place, 0
        )
        for dy, dc in ((0, 1), (1, 0), (1, 1)):
            sent = lax.dynamic_index_in_dim(own_rows, core ^ dc, 0, False)
            pairs = [
                (2 * a + b, 2 * (a ^ dy) + (b ^ dc)) for a in range(2) for b in range(2)
            ]
            here = lax.ppermute(sent, ("y", "core"), pairs)
            result = lax.dynamic_update_index_in_dim(
                result, here, 2 * (y ^ dy) + (core ^ dc), 0
            )
        return result.reshape(length, D)

    def rank_rows(whole):
        return cut_rows(whole, rows * rank, rows)

    smalls = []
    for layer in range(2):
        small, weights[layer]["dt"] = unpack(layer)
        smalls.append(small)
    hidden = whole_sequence(inputs[:, 0])
    grad = whole_sequence(cotangent[:, 0])
    outs, kept = [], []
    for layer in range(2):
        hidden, keep = layer_forward(
            hidden, rank_rows(hidden), weights[layer], smalls[layer], layer == 0
        )
        outs.append(hidden)
        kept.append(keep)
    tables = rotation_tables(length)
    grads = [None, None]
    smalls_grad, queue = [None, None], {}
    for layer in (1, 0):
        grad, smalls_grad[layer], blocks = layer_backward(
            grad,
            rank_rows(grad).astype(F32),
            kept[layer],
            weights[layer],
            smalls[layer],
            queue,
            layer,
            tables,
            (outs[1],) if layer == 1 else (),
        )
        grads[layer] = grad

    def block_rows(pair):
        chosen = jnp.where(s == 0, pair[0], pair[1]).reshape(RANKS, rows, D)
        mine = lax.dynamic_index_in_dim(chosen, 2 * y + core, 0, False)
        sent = lax.dynamic_index_in_dim(chosen, 2 * y + (1 - core), 0, False)
        theirs = flip(sent, "core")
        both = jnp.where(core == 0, jnp.stack([mine, theirs]), jnp.stack([theirs, mine]))
        return both[None, :, None]

    down_block, reduce, got_gu = blocks
    fan = lambda array, axis: jnp.moveaxis(
        array.reshape(array.shape[:axis] + (nz, -1) + array.shape[axis + 1 :]), axis, 0
    )
    dt_rows = jnp.concatenate([fan(g["dt"], 1) for g in smalls_grad], axis=2)
    dt_rows = jnp.pad(dt_rows, ((0, 0), (0, 0), (0, HALF - dt_rows.shape[2])))

    def placed(array, total, starts):
        whole = jnp.zeros((array.shape[0], total), F32)
        at = 0
        for start, width in starts:
            whole = lax.dynamic_update_slice(whole, array[:, at : at + width], (0, start))
            at += width
        return fan(whole, 1).reshape(nz, -1)

    listed = []
    for g in smalls_grad:
        listed.append(fan(g["gains"], 1).reshape(nz, -1))
        listed.append(placed(g["heads"], SSM_HEADS, [(R_HEADS * rank, R_HEADS)]))
        listed.append(
            placed(g["conv"], CONV_W, [(R_SSM * rank, R_SSM), (D_SSM + R_BC * rank, R_BC)])
        )
        listed.append(placed(g["ssm"], D_SSM, [(R_SSM * rank, R_SSM)]))
    packed = jnp.concatenate(listed, axis=1)
    packed = packed + flip(packed, "core")
    amount = packed.shape[1]
    packed = jnp.pad(packed, ((0, 0), (0, -amount % (16 * HALF)))).reshape(nz, -1, HALF)
    down_rows = R_FF // nz
    extra = jnp.concatenate([dt_rows, packed], axis=1)
    extra_count = extra.shape[1]
    got_in = share(queue["in1"], queue["in0"], 50)
    down_block = down_block(got_in[0])
    last = jnp.concatenate([down_block.reshape(nz, down_rows, HALF), narrow(extra)], axis=1)
    reduce("down0", last.reshape(-1, HALF))
    down0, extra = queue["down0"][:down_rows], queue["down0"][down_rows:]

    place = jnp.stack([y, core]).astype(jnp.int32)
    grad_w_gu = spread_gate_up(place, got_gu, nz)
    got_out = share(queue["out1"], queue["out0"], 30, (got_in[0],))
    shared = swap(extra).astype(F32)
    grad_w_in, grad_w_qkv = spread_in(place, got_in)
    got_down = share(queue["down1"], down0, 30, (grad_w_in,))
    out_rows, o_rows = R_SSM // nz, R_ATT // nz
    grad_w_out = spread_rows(place, got_out, 0, out_rows, o_rows)
    grad_w_o = spread_rows(place, got_out, out_rows, o_rows, o_rows)
    grad_w_down = spread_rows(place, got_down, 0, down_rows, min(down_rows, 128))

    width = D // nz
    dt_all = jnp.where(s == 0, shared[:, :12, :width], shared[:, :12, width : 2 * width])
    grad_w_in = with_dt(grad_w_in, dt_all.reshape(SSM_HEADS, width)).T
    small_sum = jnp.sum(shared[:, 16:], axis=0).reshape(-1)[:amount].reshape(2, -1)
    small_sum = jnp.where(s == 0, small_sum[0], small_sum[1])
    cuts, at = [], 0
    for lead, total in ((2, D), (3, SSM_HEADS), (5, CONV_W), (1, D_SSM)):
        size = lead * total // nz
        cuts.append(small_sum[at : at + size].reshape(lead, total // nz))
        at += size
    return (
        block_rows(outs),
        block_rows(grads),
        cuts[0][None],
        cuts[1][None],
        cuts[2][None],
        cuts[3],
        grad_w_in[None],
        grad_w_out[None],
        grad_w_qkv[None],
        grad_w_o[None],
        grad_w_gu[None],
        grad_w_down[None],
    )


def solution(mesh):
    CHANNELS.clear()
    sections, ctx, fsdp = mesh.devices.shape
    fine = Mesh(
        mesh.devices.reshape(sections, ctx // 2, 2, fsdp), ("section", "y", "core", "fsdp")
    )
    tokens = ("y", "core")
    in_specs = (
        P(None, "fsdp", tokens, None),
        P(None, "fsdp", tokens, None),
        P("section", None, "fsdp"),
        P("section", None, "fsdp"),
        P("section", None, "fsdp"),
        P("section", "fsdp"),
    ) + (P("section", "fsdp", None),) * 6
    out_specs = (
        P("section", None, "fsdp", tokens, None),
        P("section", None, "fsdp", tokens, None),
        P("section", None, "fsdp"),
        P("section", None, "fsdp"),
        P("section", None, "fsdp"),
        P("section", "fsdp"),
    ) + (P("section", "fsdp", None),) * 6
    return jax.shard_map(body, mesh=fine, in_specs=in_specs, out_specs=out_specs, check_vma=False)
```

```python
import functools

import jax
import jax.numpy as jnp
from jax import lax
from jax.experimental import pallas as pl
from jax.experimental.pallas import tpu as pltpu
from jax.sharding import Mesh
from jax.sharding import PartitionSpec as P

D = 2048
FF = 4096
SSM_HEADS = 48
SSM_HEAD = 64
STATE = 256
Q_HEADS = 8
KV_HEADS = 2
HEAD_DIM = 128
CONV_K = 4
D_SSM = 3072
CONV_W = 3584
D_IN = 6704
ATT = 1024
KV = 256
EPSILON = 1e-05
ROPE_BASE = 10000.0
NEGATIVE = -1e30
HIGHEST = lax.Precision.HIGHEST

RANKS = 4
R_HEADS = SSM_HEADS // RANKS
R_SSM = D_SSM // RANKS
R_BC = 2 * STATE // RANKS
R_CONV = R_SSM + R_BC
R_ATT = ATT // RANKS
R_FF = FF // RANKS
R_OUT = R_SSM + R_ATT
HALF = 1024
PART = HALF // 2
MESH = pl.DeviceIdType.MESH
BF = jnp.bfloat16
F32 = jnp.float32


def rank_place():
    return 2 * lax.axis_index("section") + lax.axis_index("y")


def rank_id(rank):
    return {"section": rank // 2, "y": lax.rem(rank, 2)}


def greet(me):
    barrier = pltpu.get_barrier_semaphore()
    for step in range(1, RANKS):
        pl.semaphore_signal(
            barrier, inc=1, device_id=rank_id(lax.rem(me + step, RANKS)), device_id_type=MESH
        )
    pl.semaphore_wait(barrier, RANKS - 1)


def swap_kernel(with_stat, *refs):
    if with_stat:
        send_ref, stat_ref, out_ref, all_stat_ref, send_sem, recv_sem, stat_send, stat_recv = refs
    else:
        send_ref, out_ref, send_sem, recv_sem = refs
    me = rank_place()
    greet(me)
    copies = []
    for step in range(1, RANKS):
        other = lax.rem(me + step, RANKS)
        copies.append(
            pltpu.make_async_remote_copy(
                src_ref=send_ref.at[other] if len(send_ref.shape) == 3 else send_ref,
                dst_ref=out_ref.at[me],
                send_sem=send_sem.at[step - 1],
                recv_sem=recv_sem.at[step - 1],
                device_id=rank_id(other),
                device_id_type=MESH,
            )
        )
        if with_stat:
            copies.append(
                pltpu.make_async_remote_copy(
                    src_ref=stat_ref,
                    dst_ref=all_stat_ref.at[me],
                    send_sem=stat_send.at[step - 1],
                    recv_sem=stat_recv.at[step - 1],
                    device_id=rank_id(other),
                    device_id_type=MESH,
                )
            )
    for copy in copies:
        copy.start()
    if len(send_ref.shape) == 3:
        out_ref[me] = send_ref[me]
    else:
        out_ref[me] = send_ref[...]
    if with_stat:
        all_stat_ref[me] = stat_ref[...]
    for copy in copies:
        copy.wait()


CHANNELS = {}


def channel(name, *operands):
    key = (name,) + tuple((o.shape, str(o.dtype)) for o in operands)
    return CHANNELS.setdefault(key, len(CHANNELS))


def lasting(us):
    return pl.CostEstimate(flops=0, transcendentals=0, bytes_accessed=int(us * 850000))


VMEM_SPEC = pl.BlockSpec(memory_space=pltpu.VMEM)
ANY_SPEC = pl.BlockSpec(memory_space=pl.ANY)


def ignoring(kernel, used, extra):
    if not extra:
        return kernel
    return lambda *refs: kernel(*refs[:used], *refs[used + extra :])


def swap(values, stat=None, after=()):
    out_shape = [jax.ShapeDtypeStruct((RANKS,) + values.shape[-2:], values.dtype)]
    scratch = [pltpu.SemaphoreType.DMA((RANKS - 1,)), pltpu.SemaphoreType.DMA((RANKS - 1,))]
    args = [values]
    if stat is not None:
        out_shape.append(jax.ShapeDtypeStruct((RANKS,) + stat.shape, stat.dtype))
        scratch += scratch
        args.append(stat)
    out = pl.pallas_call(
        ignoring(functools.partial(swap_kernel, stat is not None), len(args), len(after)),
        out_shape=out_shape,
        in_specs=[VMEM_SPEC] * len(args) + [pl.BlockSpec(memory_space=pl.ANY)] * len(after),
        out_specs=[VMEM_SPEC] * len(out_shape),
        scratch_shapes=scratch,
        cost_estimate=lasting(9),
        compiler_params=pltpu.CompilerParams(
            collective_id=channel("swap", *args, *after),
            has_side_effects=True,
            vmem_limit_bytes=32 * 2**20,
        ),
    )(*args, *after)
    return out if stat is not None else out[0]


def scatter_sum(me, rows, part_ref, slots, send_sem, recv_sem):
    copies = []
    for step in range(1, RANKS):
        other = lax.rem(me + step, RANKS)
        copies.append(
            pltpu.make_async_remote_copy(
                src_ref=part_ref.at[pl.ds(pl.multiple_of(other * rows, rows), rows)],
                dst_ref=slots.at[step - 1],
                send_sem=send_sem.at[step - 1],
                recv_sem=recv_sem.at[step - 1],
                device_id=rank_id(other),
                device_id_type=MESH,
            )
        )
    for copy in copies:
        copy.start()
    total = part_ref[pl.ds(pl.multiple_of(me * rows, rows), rows), :].astype(F32)
    for step, copy in enumerate(copies):
        copy.wait()
        total = total + slots[step].astype(F32)
    return total


def spread(me, rows, out_ref, send_sem, recv_sem):
    here = pl.ds(pl.multiple_of(me * rows, rows), rows)
    copies = []
    for step in range(1, RANKS):
        copies.append(
            pltpu.make_async_remote_copy(
                src_ref=out_ref.at[here],
                dst_ref=out_ref.at[here],
                send_sem=send_sem.at[step - 1],
                recv_sem=recv_sem.at[step - 1],
                device_id=rank_id(lax.rem(me + step, RANKS)),
                device_id_type=MESH,
            )
        )
    for copy in copies:
        copy.start()
    for copy in copies:
        copy.wait()


def mid_kernel(part_ref, resid_ref, gain_ref, mid_ref, out_ref, slots, s1, r1, s2, r2):
    rows = resid_ref.shape[0]
    me = rank_place()
    greet(me)
    mid = scatter_sum(me, rows, part_ref, slots, s1, r1) + resid_ref[...].astype(F32)
    mid_ref[...] = mid
    scale = lax.rsqrt(jnp.mean(mid * mid, axis=-1, keepdims=True) + EPSILON)
    out_ref[pl.ds(pl.multiple_of(me * rows, rows), rows), :] = (
        mid * scale * gain_ref[...].astype(F32)
    ).astype(BF)
    spread(me, rows, out_ref, s2, r2)


def end_rows_kernel(part_ref, resid_ref, out_ref, slots, s1, r1, s2, r2):
    me = rank_place()
    greet(me)
    total = scatter_sum(me, resid_ref.shape[0], part_ref, slots, s1, r1) + resid_ref[...]
    out_ref[...] = total.astype(BF)


def back_rows_kernel(
    part_ref, given_ref, value_ref, gain_ref, out_ref, gain_grad_ref, slots, s1, r1, s2, r2
):
    me = rank_place()
    greet(me)
    grad = scatter_sum(me, given_ref.shape[0], part_ref, slots, s1, r1)
    total, gain_grad_ref[...] = norm_back(grad, value_ref[...], gain_ref[...].astype(F32))
    out_ref[...] = (given_ref[...] + total).astype(BF)


def norm_back(grad, value, gain):
    scale = lax.rsqrt(jnp.mean(value * value, axis=-1, keepdims=True) + EPSILON)
    unit = value * scale
    scaled = grad * gain
    total = scale * (scaled - unit * jnp.mean(scaled * unit, axis=-1, keepdims=True))
    return total, jnp.sum(grad * unit, axis=0, keepdims=True)


def end_kernel(part_ref, resid_ref, out_ref, slots, s1, r1, s2, r2):
    rows = resid_ref.shape[0]
    me = rank_place()
    greet(me)
    total = scatter_sum(me, rows, part_ref, slots, s1, r1) + resid_ref[...]
    out_ref[pl.ds(pl.multiple_of(me * rows, rows), rows), :] = total.astype(BF)
    spread(me, rows, out_ref, s2, r2)


def back_kernel(
    part_ref, given_ref, value_ref, gain_ref, wide_ref, out_ref, gain_grad_ref, slots, s1, r1, s2, r2
):
    rows = given_ref.shape[0]
    me = rank_place()
    greet(me)
    grad = scatter_sum(me, rows, part_ref, slots, s1, r1)
    total, gain_grad_ref[...] = norm_back(grad, value_ref[...], gain_ref[...].astype(F32))
    total = given_ref[...] + total
    wide_ref[...] = total
    out_ref[pl.ds(pl.multiple_of(me * rows, rows), rows), :] = total.astype(BF)
    spread(me, rows, out_ref, s2, r2)


def rank_call(kernel, out_shape, rows, *args, after=()):
    return pl.pallas_call(
        ignoring(kernel, len(args), len(after)),
        out_shape=out_shape,
        in_specs=[VMEM_SPEC] * len(args) + [pl.BlockSpec(memory_space=pl.ANY)] * len(after),
        out_specs=[VMEM_SPEC] * len(out_shape),
        scratch_shapes=[pltpu.VMEM((RANKS - 1, rows, D), BF)]
        + [pltpu.SemaphoreType.DMA((RANKS - 1,))] * 4,
        cost_estimate=lasting(27),
        compiler_params=pltpu.CompilerParams(
            collective_id=channel(kernel.__name__, *args, *after),
            has_side_effects=True,
            vmem_limit_bytes=32 * 2**20,
        ),
    )(*args, *after)


def mid_step(part, resid, gain):
    rows = resid.shape[0]
    return rank_call(
        mid_kernel,
        [jax.ShapeDtypeStruct((rows, D), F32), jax.ShapeDtypeStruct(part.shape, BF)],
        rows,
        part,
        resid,
        gain[None],
    )


def end_step(part, resid):
    rows = resid.shape[0]
    return rank_call(end_kernel, [jax.ShapeDtypeStruct(part.shape, BF)], rows, part, resid)[0]


def end_rows(part, resid):
    shape = jax.ShapeDtypeStruct(resid.shape, BF)
    return rank_call(end_rows_kernel, [shape], resid.shape[0], part, resid)[0]


def back_rows(part, given, value, gain):
    shapes = [jax.ShapeDtypeStruct(given.shape, BF), jax.ShapeDtypeStruct((1, D), F32)]
    return rank_call(back_rows_kernel, shapes, given.shape[0], part, given, value, gain[None])


def back_step(part, given, value, gain, after=()):
    rows = given.shape[0]
    return rank_call(
        back_kernel,
        [
            jax.ShapeDtypeStruct((rows, D), F32),
            jax.ShapeDtypeStruct(part.shape, BF),
            jax.ShapeDtypeStruct((1, D), F32),
        ],
        rows,
        part,
        given,
        value,
        gain[None],
        after=after,
    )


def copy_kernel(value_ref, out_ref):
    out_ref[...] = value_ref[...]


def copy_after(value, *tokens):
    rows, width = value.shape
    tile = min(rows, 128)
    block = pl.BlockSpec((tile, width), lambda i: (i, 0))
    return pl.pallas_call(
        ignoring(copy_kernel, 1, len(tokens)),
        grid=(rows // tile,),
        out_shape=jax.ShapeDtypeStruct(value.shape, value.dtype),
        in_specs=[block] + [ANY_SPEC] * len(tokens),
        out_specs=block,
    )(value, *tokens)


def product_kernel(left_a, left_b, right_a, right_b, out_ref):
    turned = lambda left, right: lax.dot_general(
        left[...], right[...], (((0,), (0,)), ((), ())), preferred_element_type=F32
    )
    out_ref[...] = (turned(left_a, right_a) + turned(left_b, right_b)).astype(BF)


def outer_sum(left, right, tokens):
    rows, width = left[0].shape
    columns_right = right[0].shape[1]
    tile = 256
    left_block = pl.BlockSpec((rows, tile), lambda i: (0, i))
    right_block = pl.BlockSpec((rows, columns_right), lambda i: (0, 0))
    return pl.pallas_call(
        ignoring(product_kernel, 4, len(tokens)),
        grid=(width // tile,),
        out_shape=jax.ShapeDtypeStruct((width, columns_right), BF),
        in_specs=[left_block] * 2 + [right_block] * 2 + [ANY_SPEC] * len(tokens),
        out_specs=pl.BlockSpec((tile, columns_right), lambda i: (i, 0)),
        cost_estimate=lasting(3),
        compiler_params=pltpu.CompilerParams(vmem_limit_bytes=56 * 2**20),
    )(*left, *right, *tokens)


def share_kernel(one_ref, zero_ref, *refs):
    own, own_c, across, across_c, local_sem, send_sem, recv_sem = refs[-7:]
    s, y, core = (lax.axis_index(name) for name in ("section", "y", "core"))
    rows = one_ref.shape[0]
    half = rows // 2
    barrier = pltpu.get_barrier_semaphore()
    ids = {"section": {"section": 1 - s}, "y": {"y": 1 - y}, "core": {"core": 1 - core}}
    for who in ids.values():
        pl.semaphore_signal(barrier, inc=1, device_id=who, device_id_type=MESH)
    pl.semaphore_wait(barrier, 3)

    def remote(k, src, dst, axis):
        return pltpu.make_async_remote_copy(
            src_ref=src, dst_ref=dst, send_sem=send_sem.at[k], recv_sem=recv_sem.at[k],
            device_id=ids[axis], device_id_type=MESH,
        )

    part = lambda ref, k: ref.at[pl.ds(half * k, half)]
    slot = lambda ref, place, k: ref.at[place, pl.ds(half * k, half)]
    for section, mine, sent in ((0, zero_ref, one_ref), (1, one_ref, zero_ref)):

        @pl.when(s == section)
        def _():
            for k in range(2):
                remote(k, part(sent, k), slot(own, section, k), "section").start()
            for k in range(2):
                remote(2 + k, part(mine, k), slot(across, section, k), "y").start()
            remote(6, mine, own_c.at[section], "core").start()
            keep = pltpu.make_async_copy(mine, own.at[section], local_sem)
            keep.start()
            for k in range(2):
                remote(k, part(sent, k), slot(own, 1 - section, k), "section").wait_recv()
                remote(4 + k, slot(own, 1 - section, k), slot(across, 1 - section, k), "y").start()
                remote(
                    7 + k, slot(own, 1 - section, k), slot(own_c, 1 - section, k), "core"
                ).start()
            for k in range(2):
                remote(2 + k, part(mine, k), slot(across, section, k), "y").wait_recv()
                remote(
                    9 + k, slot(across, section, k), slot(across_c, section, k), "core"
                ).start()
            for k in range(2):
                there = slot(across, 1 - section, k)
                remote(4 + k, slot(own, 1 - section, k), there, "y").wait_recv()
                remote(11 + k, there, slot(across_c, 1 - section, k), "core").start()
            remote(6, mine, own_c.at[section], "core").wait_recv()
            for k in range(2):
                there = slot(own_c, 1 - section, k)
                remote(7 + k, slot(own, 1 - section, k), there, "core").wait_recv()
                there = slot(across_c, section, k)
                remote(9 + k, slot(across, section, k), there, "core").wait_recv()
                there = slot(across_c, 1 - section, k)
                remote(11 + k, slot(across, 1 - section, k), there, "core").wait_recv()
            for k in range(2):
                remote(k, part(sent, k), slot(own, section, k), "section").wait_send()
                remote(2 + k, part(mine, k), slot(across, section, k), "y").wait_send()
                there = slot(across, 1 - section, k)
                remote(4 + k, slot(own, 1 - section, k), there, "y").wait_send()
                there = slot(own_c, 1 - section, k)
                remote(7 + k, slot(own, 1 - section, k), there, "core").wait_send()
                there = slot(across_c, section, k)
                remote(9 + k, slot(across, section, k), there, "core").wait_send()
                there = slot(across_c, 1 - section, k)
                remote(11 + k, slot(across, 1 - section, k), there, "core").wait_send()
            remote(6, mine, own_c.at[section], "core").wait_send()
            keep.wait()


def share(one, zero, us, after=()):
    shape = jax.ShapeDtypeStruct((2,) + one.shape, one.dtype)
    return pl.pallas_call(
        ignoring(share_kernel, 2, len(after)),
        out_shape=[shape] * 4,
        in_specs=[ANY_SPEC] * (2 + len(after)),
        out_specs=[ANY_SPEC] * 4,
        scratch_shapes=[
            pltpu.SemaphoreType.DMA,
            pltpu.SemaphoreType.DMA((13,)),
            pltpu.SemaphoreType.DMA((13,)),
        ],
        cost_estimate=lasting(us),
        compiler_params=pltpu.CompilerParams(
            collective_id=channel("share", one, zero, *after), has_side_effects=True
        ),
    )(one, zero, *after)


def chosen(place_ref, refs):
    y, core = place_ref[0], place_ref[1]
    values = [ref[...] for ref in refs]
    found = [[None, None], [None, None]]
    for side in range(2):
        flat = [jnp.where(core == side, values[2 * k], values[2 * k + 1]) for k in range(2)]
        for row in range(2):
            found[row][side] = jnp.where(y == row, flat[0], flat[1])
    return found


def rows_kernel(place_ref, a, b, c, d, out_ref):
    found = chosen(place_ref, (a, b, c, d))
    row = lax.rem(pl.program_id(0), 2)
    for side in range(2):
        value = jnp.where(row == 0, found[0][side][0], found[1][side][0])
        out_ref[:, HALF * side : HALF * (side + 1)] = value.astype(F32)


PLACE_SPEC = pl.BlockSpec(memory_space=pltpu.SMEM)


def spread_rows(place, pieces, first, count, tile):
    steps = count // tile
    block = pl.BlockSpec((1, tile, HALF), lambda r, i: (r // 2, first // tile + i, 0))
    return pl.pallas_call(
        rows_kernel,
        grid=(RANKS, steps),
        out_shape=jax.ShapeDtypeStruct((RANKS * count, D), F32),
        in_specs=[PLACE_SPEC] + [block] * 4,
        out_specs=pl.BlockSpec((tile, D), lambda r, i: (r * steps + i, 0)),
        compiler_params=pltpu.CompilerParams(vmem_limit_bytes=56 * 2**20),
    )(place, *pieces)


def gate_up_kernel(nz, place_ref, a, b, c, d, out_ref):
    found = chosen(place_ref, (a, b, c, d))
    width = R_FF // nz
    for side in range(2):
        for shard in range(nz):
            for rank in range(RANKS):
                start = FF * side + (FF // nz) * shard + width * rank
                out_ref[:, start : start + width] = found[rank % 2][side][
                    rank // 2, :, width * shard : width * (shard + 1)
                ].astype(F32)


def spread_gate_up(place, pieces, nz):
    rows = pieces[0].shape[1]
    tile = min(rows, 128)
    block = pl.BlockSpec((2, tile, HALF), lambda i: (0, i, 0))
    return pl.pallas_call(
        functools.partial(gate_up_kernel, nz),
        grid=(rows // tile,),
        out_shape=jax.ShapeDtypeStruct((rows, 2 * FF), F32),
        in_specs=[PLACE_SPEC] + [block] * 4,
        out_specs=pl.BlockSpec((tile, 2 * FF), lambda i: (i, 0)),
        compiler_params=pltpu.CompilerParams(vmem_limit_bytes=56 * 2**20),
    )(place, *pieces)


def in_kernel(place_ref, a, b, c, d, in_ref, qkv_ref):
    found = chosen(place_ref, (a, b, c, d))
    for rank in range(RANKS):
        left, right = (found[rank % 2][side][rank // 2].astype(F32) for side in range(2))
        in_ref[R_SSM * rank : R_SSM * (rank + 1)] = right[:, :R_SSM].T
        start = D_SSM + R_SSM * rank
        in_ref[start : start + R_SSM] = left[:, :R_SSM].T
        start = 2 * D_SSM + R_BC * rank
        in_ref[start : start + R_BC] = left[:, R_SSM:R_CONV].T
        qkv_ref[:, R_ATT * rank : R_ATT * (rank + 1)] = right[:, R_SSM:]
        start = ATT + KV * (rank % 2) + HEAD_DIM * (rank // 2)
        qkv_ref[:, start : start + HEAD_DIM] = left[:, R_CONV:]


def dt_kernel(whole_ref, dt_ref, out_ref):
    out_ref[...] = dt_ref[...]


def with_dt(whole, dt):
    rows, width = dt.shape
    tile = 16
    first = (whole.shape[0] - rows) // tile
    return pl.pallas_call(
        dt_kernel,
        grid=(rows // tile,),
        out_shape=jax.ShapeDtypeStruct(whole.shape, whole.dtype),
        in_specs=[ANY_SPEC, pl.BlockSpec((tile, width), lambda i: (i, 0))],
        out_specs=pl.BlockSpec((tile, width), lambda i: (first + i, 0)),
        input_output_aliases={0: 0},
    )(whole, dt)


def spread_in(place, pieces):
    rows = pieces[0].shape[1]
    tile = min(rows, 128)
    block = pl.BlockSpec((2, tile, HALF), lambda i: (0, i, 0))
    return pl.pallas_call(
        in_kernel,
        grid=(rows // tile,),
        out_shape=[
            jax.ShapeDtypeStruct((D_IN, rows), F32),
            jax.ShapeDtypeStruct((rows, ATT + 2 * KV), F32),
        ],
        in_specs=[PLACE_SPEC] + [block] * 4,
        out_specs=[
            pl.BlockSpec((D_IN, tile), lambda i: (0, i)),
            pl.BlockSpec((tile, ATT + 2 * KV), lambda i: (i, 0)),
        ],
        compiler_params=pltpu.CompilerParams(vmem_limit_bytes=56 * 2**20),
    )(place, *pieces)


LANES = 128


def turned_lanes(values, cosine, sine):
    parts = []
    for start in range(0, values.shape[1], HEAD_DIM):
        head = values[:, start : start + HEAD_DIM]
        parts.append(head * cosine + pltpu.roll(head, HEAD_DIM // 2, 1) * sine)
    return parts[0] if len(parts) == 1 else jnp.concatenate(parts, axis=1)


def exact(left, right, contract):
    return lax.dot_general(
        left, right, (contract, ((), ())), precision=HIGHEST, preferred_element_type=F32
    )


def mixer_back_kernel(
    nz, got_ref, scan_ref, z_ref, norm_ref, gain_ref, x_ref, b_ref, c_ref, raw_ref, heads_ref,
    run_ref, dt_ref, q_ref, k_ref, v_ref, probs_ref, cos_ref, sin_ref,
    message_ref, right_ref, dx_ref, draw_ref, heads_out_ref, lanes_out_ref,
):
    length = scan_ref.shape[0]
    inner = nz // RANKS
    wide, narrow_w = R_OUT // nz, R_SSM // nz
    d_norm = jnp.concatenate(
        [
            got_ref[r][:, wide * i : wide * i + narrow_w].astype(F32)
            for i in range(inner)
            for r in range(RANKS)
        ],
        axis=1,
    )
    d_o = jnp.concatenate(
        [
            got_ref[r][:, wide * i + narrow_w : wide * (i + 1)].astype(F32)
            for i in range(inner)
            for r in range(RANKS)
        ],
        axis=1,
    ).astype(BF)
    spread_of, overlap = norm_ref[:, 0:1], norm_ref[:, 1:2]
    scan, z = scan_ref[...], z_ref[...]
    sig = jax.nn.sigmoid(z)
    silu = z * sig
    gated = scan * silu
    lanes_out_ref[0:1, :] = jnp.sum(d_norm * gated * spread_of, axis=0, keepdims=True)
    d_gated = spread_of * d_norm * gain_ref[...] - gated * (
        spread_of * spread_of * overlap * (1.0 / D_SSM)
    )
    d_scan = d_gated * silu
    right_ref[:, :R_SSM] = (d_gated * scan * (sig * (1.0 + z * (1.0 - sig)))).astype(BF)

    row = lax.broadcasted_iota(jnp.int32, (length, length), 0)
    column = lax.broadcasted_iota(jnp.int32, (length, length), 1)
    allowed = row >= column

    scale = HEAD_DIM**-0.5
    key, value = k_ref[...], v_ref[...]
    d_key = jnp.zeros((length, HEAD_DIM), F32)
    d_value = jnp.zeros((length, HEAD_DIM), F32)
    for head in range(R_ATT // HEAD_DIM):
        cut = slice(HEAD_DIM * head, HEAD_DIM * (head + 1))
        query, grad, probs = q_ref[:, cut], d_o[:, cut], probs_ref[head]
        d_probs = dot_t(grad, value)
        d_scores = (
            probs * (d_probs - jnp.sum(probs * d_probs, axis=1, keepdims=True))
        ).astype(BF)
        d_query = dot(d_scores, key) * scale
        right_ref[:, R_SSM + HEAD_DIM * head : R_SSM + HEAD_DIM * (head + 1)] = turned_lanes(
            d_query, cos_ref[...], -sin_ref[...]
        ).astype(BF)
        d_key = d_key + t_dot(d_scores, query) * scale
        d_value = d_value + t_dot(probs.astype(BF), grad)

    b_rows, c_rows = b_ref[...], c_ref[...]
    mixing = dot_t(c_rows, b_rows)
    x = x_ref[...]
    lanes_out_ref[1:2, :] = jnp.sum(d_scan * x.astype(F32), axis=0, keepdims=True)
    grad_b = d_scan.astype(BF)
    run_t, dt_t = run_ref[...].T, dt_ref[...].T
    d_mixing = jnp.zeros((length, length), F32)
    lane = lax.broadcasted_iota(jnp.int32, (length, LANES), 1)
    head_row = lax.broadcasted_iota(jnp.int32, (LANES, length), 0)
    by_row = jnp.zeros((length, LANES), F32)
    direct = jnp.zeros((LANES, length), F32)
    for pair in range(R_HEADS // 2):
        cut = slice(LANES * pair, LANES * (pair + 1))
        x_pair, g_pair = x[:, cut], grad_b[:, cut]
        d_pair = []
        for side in range(2):
            head = 2 * pair + side
            mine = (lane < SSM_HEAD) if side == 0 else (lane >= SSM_HEAD)
            d_weights = dot_t(jnp.where(mine, g_pair, jnp.zeros_like(g_pair)), x_pair)
            gap = run_ref[:, head : head + 1] - run_t[head : head + 1, :]
            table = jnp.exp(jnp.where(allowed, gap, NEGATIVE))
            dt_row = dt_t[head : head + 1, :]
            faded = d_weights * table
            faded_dt = faded * dt_row
            d_mixing = d_mixing + faded_dt
            plain = faded * mixing
            direct = jnp.where(head_row == head, jnp.sum(plain, axis=0, keepdims=True), direct)
            by_row = jnp.where(
                lane == head, jnp.sum(faded_dt * mixing, axis=1, keepdims=True), by_row
            )
            weights = (table * mixing * dt_row).astype(BF)
            d_pair.append(t_dot(weights, g_pair))
        skip = jnp.where(
            lane[:1] < SSM_HEAD,
            heads_ref[2:3, 2 * pair : 2 * pair + 1],
            heads_ref[2:3, 2 * pair + 1 : 2 * pair + 2],
        )
        dx_ref[:, cut] = jnp.where(lane < SSM_HEAD, d_pair[0], d_pair[1]) + skip * d_scan[:, cut]
    d_mixing = d_mixing.astype(BF)
    d_c = dot(d_mixing, b_rows)
    d_b = t_dot(d_mixing, c_rows)
    for r in range(RANKS):
        source = d_b if r < 2 else d_c
        start = R_BC * (r % 2)
        message_ref[r, :, :R_BC] = source[:, start : start + R_BC].astype(BF)
        message_ref[r, :, R_BC:] = (d_key if r % 2 == 0 else d_value).astype(BF)

    later = (column >= row).astype(F32)
    from_rows_sum = exact(later, by_row, ((1,), (0,)))
    grad_step = from_rows_sum - exact(later, direct * dt_t, ((1,), (1,)))
    grad_dt = direct.T
    bias, log = heads_ref[0:1, :], heads_ref[1:2, :]
    raw = raw_ref[...] + bias
    rate = jnp.exp(log)
    step = -jax.nn.softplus(raw) * rate
    valid = lane < R_HEADS
    grad_dt = grad_dt - grad_step * rate
    grad_raw = jnp.where(valid, grad_dt * jax.nn.sigmoid(raw), 0.0)
    draw_ref[...] = grad_raw.astype(BF)
    heads_out_ref[0:1, :] = jnp.sum(grad_raw, axis=0, keepdims=True)
    heads_out_ref[1:2, :] = jnp.sum(grad_step * step, axis=0, keepdims=True)


def whole_block(array):
    shape = array.shape
    return pl.BlockSpec(shape, lambda i: (0,) * len(shape), pipeline_mode=pl.Buffered(1))


def mixer_back(got, kept, small, overlap, tables):
    length = got.shape[1]
    nz = lax.axis_size("fsdp")
    norm = jnp.stack([kept["spread"], overlap], axis=1)
    shape = jax.ShapeDtypeStruct
    out_shape = [
        shape((RANKS, length, 2 * R_BC), BF),
        shape((length, HALF), BF),
        shape((length, R_SSM), F32),
        shape((length, LANES), BF),
        shape((8, LANES), F32),
        shape((8, R_SSM), F32),
    ]
    args = (
        got, kept["scan"], kept["z"], norm, small["ssm_gain"][None], kept["u"][:, :R_SSM],
        kept["b"], kept["c"], kept["dt_raw"], small["heads"], kept["running"], kept["dt"],
        kept["query"], kept["key"], kept["value"],
        kept["probs"], *tables,
    )
    return pl.pallas_call(
        functools.partial(mixer_back_kernel, nz),
        grid=(1,),
        out_shape=out_shape,
        in_specs=[whole_block(arg) for arg in args],
        out_specs=[whole_block(out) for out in out_shape],
        cost_estimate=lasting(16),
        compiler_params=pltpu.CompilerParams(vmem_limit_bytes=56 * 2**20),
    )(*args)


def conv_back_kernel(
    place_ref, back_ref, dx_ref, xbc_ref, table_ref, cos_ref, sin_ref, left_ref, conv_ref
):
    y, s = place_ref[0], place_ref[1]
    length = dx_ref.shape[0]
    back = [back_ref[r].astype(F32) for r in range(RANKS)]
    d_bc = (back[0] + back[1] + back[2] + back[3])[:, :R_BC]
    d_kv = jnp.where(s == 0, back[0] + back[1], back[2] + back[3])[:, R_BC:]
    d_kv = jnp.where(y == 0, turned_lanes(d_kv, cos_ref[...], -sin_ref[...]), d_kv)
    left_ref[:, R_CONV:] = d_kv.astype(BF)
    d_u = jnp.concatenate([dx_ref[...], d_bc], axis=1)
    wide = xbc_ref[...].astype(F32)
    place = lax.broadcasted_iota(jnp.int32, (length, R_CONV), 0)
    moved = []
    before = table_ref[CONV_K : CONV_K + 1, :] + jnp.zeros_like(wide)
    for tap in range(CONV_K):
        steps = CONV_K - 1 - tap
        value = wide
        if steps:
            value = jnp.where(place >= steps, pltpu.roll(wide, steps, 0), 0.0)
        moved.append(value)
        before = before + table_ref[tap : tap + 1, :] * value
    sig = jax.nn.sigmoid(before)
    d_before = d_u * (sig * (1.0 + before * (1.0 - sig)))
    d_xbc = jnp.zeros_like(wide)
    for tap in range(CONV_K):
        conv_ref[tap : tap + 1, :] = jnp.sum(d_before * moved[tap], axis=0, keepdims=True)
        steps = CONV_K - 1 - tap
        value = d_before
        if steps:
            value = jnp.where(
                place < length - steps, pltpu.roll(d_before, length - steps, 0), 0.0
            )
        d_xbc = d_xbc + table_ref[tap : tap + 1, :] * value
    conv_ref[CONV_K : CONV_K + 1, :] = jnp.sum(d_before, axis=0, keepdims=True)
    left_ref[:, :R_CONV] = d_xbc.astype(BF)


def conv_back(back, d_x, xbc, table, tables):
    length = d_x.shape[0]
    place = jnp.stack([lax.axis_index("y"), lax.axis_index("section")]).astype(jnp.int32)
    args = (back, d_x, xbc, table, *tables)
    out_shape = [
        jax.ShapeDtypeStruct((length, HALF), BF),
        jax.ShapeDtypeStruct((8, R_CONV), F32),
    ]
    return pl.pallas_call(
        conv_back_kernel,
        grid=(1,),
        out_shape=out_shape,
        in_specs=[PLACE_SPEC] + [whole_block(arg) for arg in args],
        out_specs=[whole_block(out) for out in out_shape],
        cost_estimate=lasting(7),
        compiler_params=pltpu.CompilerParams(vmem_limit_bytes=56 * 2**20),
    )(place, *args)


EXTRA = 32


def pack_kernel(nz, *refs):
    out_ref, conv_full, ssm_full = refs[-3:]
    rank = rank_place()
    out_ref[...] = jnp.zeros_like(out_ref)
    width, conv_width, ssm_width = D // nz, CONV_W // nz, D_SSM // nz
    heads_width, inner = SSM_HEADS // nz, nz // RANKS
    head_of = lax.broadcasted_iota(jnp.int32, (R_SSM, LANES), 0) // SSM_HEAD
    lane = lax.broadcasted_iota(jnp.int32, (R_SSM, LANES), 1)
    to_heads = (head_of == lane).astype(F32)
    for layer in range(2):
        heads_ref, lanes_ref, conv_ref, gain0_ref, gain1_ref, dt_ref = refs[6 * layer : 6 * layer + 6]
        conv_full[...] = jnp.zeros_like(conv_full)
        ssm_full[...] = jnp.zeros_like(ssm_full)
        at = lambda start, size: pl.ds(pl.multiple_of(start, LANES), size)
        conv_full[:, at(R_SSM * rank, R_SSM)] = conv_ref[:, :R_SSM]
        conv_full[:, at(D_SSM + R_BC * rank, R_BC)] = conv_ref[:, R_SSM:]
        ssm_full[:, at(R_SSM * rank, R_SSM)] = lanes_ref[...]
        skip = exact(lanes_ref[...], to_heads, ((1,), (0,)))[1:2]
        heads = (heads_ref[0:1], heads_ref[1:2], skip)
        row = 16 + 8 * layer
        for z in range(nz):
            cut = slice(width * z, width * (z + 1))
            out_ref[z, 0:16, PART * layer : PART * layer + width] = dt_ref[:, cut]
            out_ref[z, row : row + 1, 0:width] = gain0_ref[:, cut]
            out_ref[z, row : row + 1, PART : PART + width] = gain1_ref[:, cut]
            out_ref[z, row + 1 : row + 6, 0:conv_width] = conv_full[
                0 : CONV_K + 1, conv_width * z : conv_width * (z + 1)
            ]
            out_ref[z, row + 6 : row + 7, 0:ssm_width] = ssm_full[
                0:1, ssm_width * z : ssm_width * (z + 1)
            ]
            start = heads_width * (z % inner)
            for k in range(3):
                value = jnp.where(rank == z // inner, heads[k], 0.0)
                out_ref[z, row + 7 : row + 8, LANES * k : LANES * k + heads_width] = value[
                    :, start : start + heads_width
                ]


def pack(layers, nz):
    args = [array for layer in layers for array in layer]
    out = jax.ShapeDtypeStruct((nz, EXTRA, HALF), F32)
    return pl.pallas_call(
        functools.partial(pack_kernel, nz),
        grid=(1,),
        out_shape=out,
        in_specs=[whole_block(arg) for arg in args],
        out_specs=whole_block(out),
        scratch_shapes=[pltpu.VMEM((8, CONV_W), F32), pltpu.VMEM((8, D_SSM), F32)],
        cost_estimate=lasting(4),
        compiler_params=pltpu.CompilerParams(vmem_limit_bytes=40 * 2**20),
    )(*args)


def rotation_tables(length):
    half = HEAD_DIM // 2
    frequency = ROPE_BASE ** (-jnp.arange(half, dtype=F32) / half)
    angles = jnp.arange(length, dtype=F32)[:, None] * frequency[None, :]
    cosine, sine = jnp.cos(angles), jnp.sin(angles)
    return jnp.concatenate([cosine, cosine], 1), jnp.concatenate([-sine, sine], 1)


def narrow(values):
    return values.astype(BF)


def dot(left, right):
    return jnp.dot(left, right, preferred_element_type=F32)


def dot_t(left, right):
    return lax.dot_general(left, right, (((1,), (1,)), ((), ())), preferred_element_type=F32)


def t_dot(left, right):
    return lax.dot_general(left, right, (((0,), (0,)), ((), ())), preferred_element_type=F32)


def columns(array, start, width):
    return lax.dynamic_slice_in_dim(array, start, width, axis=1)


def cut_rows(array, start, width):
    return lax.dynamic_slice_in_dim(array, start, width, axis=0)


def rms(values, gain):
    return values * lax.rsqrt(jnp.mean(values * values, axis=-1, keepdims=True) + EPSILON) * gain


def rotary(values, turning):
    length, width = values.shape
    half = HEAD_DIM // 2
    frequency = ROPE_BASE ** (-jnp.arange(half, dtype=F32) / half)
    angles = jnp.arange(length, dtype=F32)[:, None] * frequency[None, :]
    cosine = jnp.cos(angles)[:, None, :]
    sine = turning * jnp.sin(angles)[:, None, :]
    halves = values.reshape(length, width // HEAD_DIM, 2, half)
    first, second = halves[:, :, 0], halves[:, :, 1]
    return jnp.stack(
        [first * cosine - second * sine, second * cosine + first * sine], axis=2
    ).reshape(length, width)


def causal(length):
    position = jnp.arange(length)
    return position[:, None] >= position[None, :]


def shifted(values, steps):
    if steps == 0:
        return values
    blank = jnp.zeros((abs(steps), values.shape[1]), values.dtype)
    if steps > 0:
        return jnp.concatenate([blank, values[:-steps]], axis=0)
    return jnp.concatenate([values[-steps:], blank], axis=0)


def conv_sum(rows, table):
    wide = rows.astype(F32)
    total = table[CONV_K][None, :]
    for tap in range(CONV_K):
        total = total + table[tap][None, :] * shifted(wide, CONV_K - 1 - tap)
    return total


def decays(dt_raw, heads):
    dt = jax.nn.softplus(dt_raw + heads[0][None, :])
    step = -dt * jnp.exp(heads[1])[None, :]
    length = dt.shape[0]
    running = jnp.dot(causal(length).astype(F32), step, precision=HIGHEST)
    return dt, step, running


def decay_table(running):
    length = running.shape[0]
    turned = running.T
    gap = turned[:, :, None] - turned[:, None, :]
    return jnp.exp(jnp.where(causal(length)[None], gap, NEGATIVE))


def by_head(values):
    return values.reshape(values.shape[0], R_HEADS, SSM_HEAD)


def scan_forward(x, b_rows, c_rows, dt_raw, heads):
    dt, _, running = decays(dt_raw, heads)
    mixing = dot_t(c_rows, b_rows)
    weights = narrow(decay_table(running[:, :R_HEADS]) * mixing[None] * dt.T[:R_HEADS, None, :])
    x_heads = by_head(x)
    result = jnp.einsum("hts,shp->thp", weights, x_heads, preferred_element_type=F32)
    result = result + heads[2][None, :R_HEADS, None] * x_heads.astype(F32)
    return result.reshape(x.shape), running, dt


def scan_backward(x, b_rows, c_rows, dt_raw, heads, grad_y):
    dt, step, running = decays(dt_raw, heads)
    length = x.shape[0]
    mixing = dot_t(c_rows, b_rows)
    table = decay_table(running)
    dt_t = dt.T
    x_heads = by_head(x)
    grad_heads = by_head(narrow(grad_y))
    grad_weights = jnp.einsum("thp,shp->hts", grad_heads, x_heads, preferred_element_type=F32)
    faded = grad_weights * table
    weights = table * mixing[None] * dt_t[:, None, :]
    grad_x = jnp.einsum("hts,thp->shp", narrow(weights), grad_heads, preferred_element_type=F32)
    grad_y_heads = by_head(grad_y)
    grad_x = grad_x + heads[2][None, :, None] * grad_y_heads
    grad_skip = jnp.sum(grad_y_heads * x_heads.astype(F32), axis=(0, 2))
    grad_mixing = narrow(jnp.sum(faded * dt_t[:, None, :], axis=0))
    grad_c = dot(grad_mixing, b_rows)
    grad_b = t_dot(grad_mixing, c_rows)
    plain = faded * mixing[None]
    grad_dt = jnp.sum(plain, axis=1)
    grad_gap = plain * dt_t[:, None, :]
    grad_running = jnp.sum(grad_gap, axis=2) - jnp.sum(grad_gap, axis=1)
    grad_step = jnp.dot(grad_running, causal(length).astype(F32), precision=HIGHEST).T
    grad_dt = grad_dt.T - grad_step * jnp.exp(heads[1])[None, :]
    grad_log = jnp.sum(grad_step * step, axis=0)
    grad_raw = grad_dt * jax.nn.sigmoid(dt_raw + heads[0][None, :])
    grad_table = jnp.stack([jnp.sum(grad_raw, axis=0), grad_log, grad_skip])
    return grad_x.reshape(x.shape), grad_b, grad_c, grad_raw, grad_table


def attend(query, key, value):
    length = query.shape[0]
    heads = query.reshape(length, -1, HEAD_DIM)
    scores = jnp.einsum("qhd,sd->hqs", heads, key, preferred_element_type=F32) * HEAD_DIM**-0.5
    scores = jnp.where(causal(length)[None], scores, NEGATIVE)
    weights = jnp.exp(scores - jnp.max(scores, axis=-1, keepdims=True))
    probs = weights / jnp.sum(weights, axis=-1, keepdims=True)
    mixed = jnp.einsum("hqs,sd->qhd", narrow(probs), value, preferred_element_type=F32)
    return narrow(mixed.reshape(query.shape)), probs


def attend_back(query, key, value, probs, grad_out):
    length = query.shape[0]
    heads = query.reshape(length, -1, HEAD_DIM)
    grad_heads = grad_out.reshape(length, -1, HEAD_DIM)
    grad_probs = jnp.einsum("qhd,sd->hqs", grad_heads, value, preferred_element_type=F32)
    grad_scores = narrow(
        probs * (grad_probs - jnp.sum(probs * grad_probs, axis=-1, keepdims=True))
    )
    scale = HEAD_DIM**-0.5
    grad_query = jnp.einsum("hqs,sd->qhd", grad_scores, key, preferred_element_type=F32) * scale
    grad_key = jnp.einsum("hqs,qhd->sd", grad_scores, heads, preferred_element_type=F32) * scale
    grad_value = jnp.einsum("hqs,qhd->sd", narrow(probs), grad_heads, preferred_element_type=F32)
    return grad_query.reshape(query.shape), grad_key, grad_value


def flip(value, axis):
    return lax.ppermute(value, axis, [(0, 1), (1, 0)])


def layer_forward(entering, resid, weights, small, then, last):
    s, y = lax.axis_index("section"), lax.axis_index("y")
    length = entering.shape[0]
    x1 = narrow(rms(entering.astype(F32), small["gain0"][None, :]))
    left = dot(x1, weights["in"][0])
    right = dot(x1, weights["in"][1])
    dt_raw = dot(x1, weights["dt"])
    xbc = narrow(left[:, :R_CONV])
    u = narrow(jax.nn.silu(conv_sum(xbc, small["conv"])))
    kv_raw = left[:, R_CONV:]
    kv = narrow(jnp.where(y == 0, rotary(kv_raw, 1.0), kv_raw))
    shared = swap(jnp.concatenate([u[:, R_SSM:], kv], axis=1))
    then("swap", shared)
    b_rows = jnp.concatenate([shared[0, :, :R_BC], shared[1, :, :R_BC]], axis=1)
    c_rows = jnp.concatenate([shared[2, :, :R_BC], shared[3, :, :R_BC]], axis=1)
    pair = lax.dynamic_slice_in_dim(shared, 2 * s, 2, axis=0)[:, :, R_BC:]
    key, value = pair[0], pair[1]
    z = right[:, :R_SSM]
    query = narrow(rotary(right[:, R_SSM:], 1.0))
    o, probs = attend(query, key, value)
    x = u[:, :R_SSM]
    scan, running, dt = scan_forward(x, b_rows, c_rows, dt_raw, small["heads"])
    gated = scan * jax.nn.silu(z)
    squares = jnp.sum(gated * gated, axis=1)
    scaled = narrow(gated * small["ssm_gain"][None, :])
    message = to_rows(scaled, o)
    stat = jnp.broadcast_to(squares[None, :], (8, length))
    got, stats = swap(message, stat)
    spread_of = lax.rsqrt(jnp.sum(stats[:, 0, :], axis=0) / D_SSM + EPSILON)
    wide = jnp.transpose(got, (1, 0, 2)).reshape(length, R_OUT)
    is_ssm = small["is_ssm"][None, :]
    mo = narrow(jnp.where(is_ssm, wide.astype(F32) * spread_of[:, None], wide.astype(F32)))
    part = jnp.concatenate([dot(mo, weights["out"][0]), dot(mo, weights["out"][1])], axis=1)
    mid, x2 = mid_step(narrow(part), resid, small["gain1"])
    then("mid", mid)
    gate = dot(x2, weights["gu"][0])
    up = dot(x2, weights["gu"][1])
    act = narrow(jax.nn.silu(gate) * up)
    part2 = jnp.concatenate([dot(act, weights["down"][0]), dot(act, weights["down"][1])], axis=1)
    leaving = (end_rows if last else end_step)(narrow(part2), mid)
    kept = dict(
        resid=resid, x1=x1, xbc=xbc, u=u, b=b_rows, c=c_rows, key=key, value=value, query=query,
        probs=probs, z=z, dt_raw=dt_raw, scan=scan, spread=spread_of, mo=mo, mid=mid, x2=x2,
        gate=gate, up=up, act=act, running=running, dt=dt,
    )
    return leaving, kept


def to_rows(ssm_part, att_part):
    length = ssm_part.shape[0]
    nz = lax.axis_size("fsdp")
    inner = nz // RANKS
    a = ssm_part.reshape(length, inner, RANKS, R_SSM // nz)
    b = att_part.reshape(length, inner, RANKS, R_ATT // nz)
    both = jnp.concatenate([a, b], axis=3)
    return jnp.transpose(both, (2, 0, 1, 3)).reshape(RANKS, length, R_OUT // RANKS)


def from_rows(got):
    length = got.shape[1]
    nz = lax.axis_size("fsdp")
    inner = nz // RANKS
    both = jnp.transpose(got.reshape(RANKS, length, inner, R_OUT // nz), (1, 2, 0, 3))
    a = both[..., : R_SSM // nz].reshape(length, R_SSM)
    b = both[..., R_SSM // nz :].reshape(length, R_ATT)
    return a, b


def layer_backward(grad, given, kept, weights, small, queue, layer, tables, first=()):
    s, y = lax.axis_index("section"), lax.axis_index("y")
    core = lax.axis_index("core")
    length = grad.shape[0]
    down, gu, out, win = weights["down"], weights["gu"], weights["out"], weights["in"]

    def product(left, right, *tokens):
        mine = jnp.where(core == 0, right[0], right[1])
        theirs = jnp.where(core == 0, right[1], right[0])
        return outer_sum((left, flip(left, "core")), (mine, flip(theirs, "core")), tokens)

    def reduce(name, block):
        nonlocal queue
        if queue:
            block, queue["last"] = lax.optimization_barrier((block, queue["last"]))
        queue[name] = queue["last"] = lax.psum_scatter(
            block, "fsdp", scatter_dimension=0, tiled=True
        )

    def due(point):
        return [queue[k] for k in WAITS[layer].get(point, ())]

    halves = lambda v: (v[:, :HALF], v[:, HALF:])
    g0, g1 = halves(grad)
    down_block = None
    if layer == 1:
        reduce("down1", product(kept["act"], (g0, g1)))
    grad_act = dot_t(g0, down[0]) + dot_t(g1, down[1])
    gate, up = kept["gate"], kept["up"]
    sig = jax.nn.sigmoid(gate)
    d_gate = narrow(grad_act * up * (sig * (1.0 + gate * (1.0 - sig))))
    d_up = narrow(grad_act * gate * sig)
    part = dot_t(d_gate, gu[0]) + dot_t(d_up, gu[1])
    if layer == 1:
        reduce("gu1", product(kept["x2"], (d_gate, d_up), *first))
    d_mid, db, grad_gain1 = back_step(
        narrow(part), given, kept["mid"], small["gain1"], due("mlp") + list(first)
    )
    if layer == 0:
        reduce("gu0", product(kept["x2"], (d_gate, d_up), db))
    b0, b1 = halves(db)
    if layer == 0:
        down_block = product(kept["act"], (g0, g1), db)
    d_mo = dot_t(b0, out[0]) + dot_t(b1, out[1])
    mo = kept["mo"]
    is_ssm = small["is_ssm"][None, :]
    stat_row = jnp.sum(jnp.where(is_ssm, d_mo * mo.astype(F32), 0.0), axis=1)
    stat = jnp.broadcast_to(stat_row[None, :], (8, length))
    blocks = jnp.transpose(narrow(d_mo).reshape(length, RANKS, R_OUT // RANKS), (1, 0, 2))
    got, stats = swap(blocks, stat, due("norm"))
    overlap = jnp.sum(stats[:, 0, :], axis=0)
    message, d_right, d_x, d_raw, head_sums, lane_sums = mixer_back(
        got, kept, small, overlap, tables
    )
    if layer == 1:
        reduce("out1", product(kept["mo"], (b0, b1), message))
    back = swap(message, None, due("scan"))
    d_left, grad_conv = conv_back(back, d_x, kept["xbc"], small["conv"], tables)
    part = dot_t(d_left, win[0]) + dot_t(d_right, win[1]) + dot_t(d_raw, weights["dt"])
    part = narrow(part)
    if layer == 1:
        reduce("in1", product(kept["x1"], (d_left, d_right), part))
    enter = (part, d_mid, kept["resid"].astype(F32), small["gain0"])
    if layer == 0:
        entering_grad, grad_gain0 = back_rows(*enter)
        reduce("in0", product(kept["x1"], (d_left, d_right), entering_grad))
    else:
        _, entering_grad, grad_gain0 = back_step(*enter, due("in"))
    got_gu = None
    if layer == 0:
        got_gu = share(queue["gu1"], queue["gu0"], 50, (entering_grad,))
        place = jnp.stack([y, core]).astype(jnp.int32)
        got_gu = spread_gate_up(place, got_gu, lax.axis_size("fsdp"))
        reduce("out0", product(kept["mo"], (b0, b1), got_gu, down_block))
    grad_dt_w = t_dot(d_raw[:, :16], kept["x1"])
    smalls_grad = (head_sums, lane_sums, grad_conv, grad_gain0, grad_gain1, grad_dt_w)
    return entering_grad, smalls_grad, (down_block, reduce, got_gu)


WAITS = (
    {"mlp": ("out1",), "scan": ("in1",)},
    {"norm": ("down1",), "in": ("gu1",)},
)


def body(
    inputs, cotangent, norm_gains, head_params, conv_params, ssm_gain,
    w_in, w_out, w_qkv, w_o, w_gu, w_down,
):
    s, y = lax.axis_index("section"), lax.axis_index("y")
    core = lax.axis_index("core")
    nz = lax.axis_size("fsdp")
    z_place = lax.axis_index("fsdp")
    rank = 2 * s + y
    rows = inputs.shape[2]
    length = RANKS * rows
    w_in, w_out, w_qkv, w_o, w_gu, w_down = (
        w[0] for w in (w_in, w_out, w_qkv, w_o, w_gu, w_down)
    )

    flat = jnp.concatenate(
        [
            norm_gains[0].reshape(-1),
            head_params[0].reshape(-1),
            conv_params[0].reshape(-1),
            ssm_gain[0],
            w_in[:, D_SSM + CONV_W :].reshape(-1),
        ]
    )
    count = flat.shape[0]
    flat = jnp.pad(flat, (0, -count % 2048)).reshape(-1, 128)
    everything = lax.all_gather(flat, ("section", "fsdp"), axis=0).reshape(2, nz, -1)[..., :count]

    def unpack(layer):
        part = everything[layer]
        sizes = [2 * D // nz, 3 * SSM_HEADS // nz, 5 * CONV_W // nz, D_SSM // nz]
        starts = [0]
        for size in sizes:
            starts.append(starts[-1] + size)
        join = lambda k, lead: jnp.transpose(
            part[:, starts[k] : starts[k + 1]].reshape(nz, lead, -1), (1, 0, 2)
        ).reshape(lead, -1).astype(F32)
        gains, heads, conv, gain = join(0, 2), join(1, 3), join(2, 5), join(3, 1)[0]
        conv_own = jnp.concatenate(
            [columns(conv, R_SSM * rank, R_SSM), columns(conv, D_SSM + R_BC * rank, R_BC)], axis=1
        )
        channel = jnp.arange(R_OUT) % (R_OUT // nz)
        small = dict(
            gain0=gains[0],
            gain1=gains[1],
            heads=jnp.pad(
                columns(heads, R_HEADS * rank, R_HEADS), ((0, 0), (0, LANES - R_HEADS))
            ),
            conv=conv_own,
            ssm_gain=lax.dynamic_slice_in_dim(gain, R_SSM * rank, R_SSM),
            is_ssm=channel < R_SSM // nz,
        )
        dt_w = columns(part[:, starts[4] :].reshape(D, SSM_HEADS), R_HEADS * rank, R_HEADS)
        return small, jnp.pad(dt_w, ((0, 0), (0, LANES - R_HEADS)))

    def pieces(section):
        rk = 2 * section + y
        first = columns(w_in, jnp.where(core == 0, D_SSM, 0) + R_SSM * rk, R_SSM)
        second = jnp.where(
            core == 0,
            columns(w_in, 2 * D_SSM + R_BC * rk, R_BC),
            columns(w_qkv, R_ATT * rk, HEAD_DIM),
        )
        third = columns(
            w_qkv,
            jnp.where(core == 0, ATT + KV * y + HEAD_DIM * section, R_ATT * rk + HEAD_DIM),
            HEAD_DIM,
        )
        side = HALF * core
        out_rows, o_rows, down_rows = R_SSM // nz, R_ATT // nz, R_FF // nz
        ff = R_FF // nz
        return {
            "in": jnp.concatenate([first, second, third], axis=1),
            "out": jnp.concatenate(
                [
                    lax.dynamic_slice(w_out, (out_rows * rk, side), (out_rows, HALF)),
                    lax.dynamic_slice(w_o, (o_rows * rk, side), (o_rows, HALF)),
                ],
                axis=0,
            ),
            "gu": jnp.concatenate(
                [
                    columns(w_gu, FF * core + (FF // nz) * k + ff * rk, ff) for k in range(nz)
                ],
                axis=1,
            ),
            "down": lax.dynamic_slice(w_down, (down_rows * rk, side), (down_rows, HALF)),
        }

    order = []

    def in_turn(value):
        if order:
            value, order[-1] = lax.optimization_barrier((value, order[-1]))
        return value

    def gather(piece):
        order.append(lax.all_gather(in_turn(piece), ("core", "fsdp"), axis=0))
        return order[-1]

    own, other = pieces(s), pieces(1 - s)
    out_own = gather(own["out"])
    mlp = lambda found: jnp.concatenate([found["gu"], found["down"]], axis=0)
    in_arrived = flip(other["in"], "section")
    out_sent, in_arrived = lax.optimization_barrier((other["out"], in_arrived))
    out_arrived = flip(out_sent, "section")
    mlp_own = mlp(own)
    mlp_sent, out_arrived = lax.optimization_barrier((mlp(other), out_arrived))
    mlp_arrived = flip(mlp_sent, "section")
    of_layer = lambda layer, mine, theirs: jnp.where(s == layer, mine, theirs)
    flat_rows = lambda whole: whole.reshape(2, -1, HALF)
    in0 = gather(copy_after(of_layer(0, own["in"], in_arrived), everything, out_own))
    wide = own["gu"].shape[0]
    mlp0, mlp1 = (of_layer(layer, mlp_own, mlp_arrived) for layer in range(2))

    def together(token, *parts):
        whole = gather(copy_after(jnp.concatenate(parts, axis=0), token))
        whole = whole.reshape(2, nz, -1, HALF)
        found, at = [], 0
        for part in parts:
            found.append(flat_rows(whole[:, :, at : at + part.shape[0]]))
            at += part.shape[0]
        return found

    out_other, gu0, down0 = together(in0, out_arrived, mlp0[:wide], mlp0[wide:])
    weights = [
        dict(out=of_layer(layer, flat_rows(out_own), out_other)) for layer in range(2)
    ]
    weights[0].update({"in": flat_rows(in0), "gu": gu0, "down": down0})

    def then(point, token):
        if point == "swap":
            piece = of_layer(1, own["in"], in_arrived)
            weights[1]["in"] = flat_rows(gather(copy_after(piece, token)))
        elif point == "mid":
            weights[1]["gu"], weights[1]["down"] = together(token, mlp1[:wide], mlp1[wide:])

    def whole_sequence(own_rows):
        place = 2 * y + core
        result = jnp.zeros((RANKS, rows, D), BF)
        result = lax.dynamic_update_index_in_dim(
            result, lax.dynamic_index_in_dim(own_rows, core, 0, False), place, 0
        )
        for dy, dc in ((0, 1), (1, 0), (1, 1)):
            sent = lax.dynamic_index_in_dim(own_rows, core ^ dc, 0, False)
            pairs = [
                (2 * a + b, 2 * (a ^ dy) + (b ^ dc)) for a in range(2) for b in range(2)
            ]
            here = lax.ppermute(sent, ("y", "core"), pairs)
            result = lax.dynamic_update_index_in_dim(
                result, here, 2 * (y ^ dy) + (core ^ dc), 0
            )
        return result.reshape(length, D)

    def rank_rows(whole):
        return cut_rows(whole, rows * rank, rows)

    smalls = []
    for layer in range(2):
        small, weights[layer]["dt"] = unpack(layer)
        smalls.append(small)
    hidden = whole_sequence(inputs[:, 0])
    grad = whole_sequence(cotangent[:, 0])
    outs, kept = [], []
    for layer in range(2):
        hidden, keep = layer_forward(
            hidden,
            rank_rows(hidden),
            weights[layer],
            smalls[layer],
            then if layer == 0 else lambda *_: None,
            layer == 1,
        )
        outs.append(hidden)
        kept.append(keep)
    tables = rotation_tables(length)
    grads = [None, None]
    smalls_grad, queue = [None, None], {}
    for layer in (1, 0):
        grad, smalls_grad[layer], blocks = layer_backward(
            grad,
            rank_rows(grad).astype(F32),
            kept[layer],
            weights[layer],
            smalls[layer],
            queue,
            layer,
            tables,
            (outs[1],) if layer == 1 else (),
        )
        grads[layer] = grad

    def block_rows(whole):
        blocks = whole.reshape(RANKS, rows, D)
        mine = lax.dynamic_index_in_dim(blocks, 2 * y + core, 0, False)
        sent = lax.dynamic_index_in_dim(blocks, 2 * y + (1 - core), 0, False)
        theirs = flip(sent, "core")
        return jnp.where(core == 0, jnp.stack([mine, theirs]), jnp.stack([theirs, mine]))

    def block_from_ranks(part, section):
        moved = []
        for micro in range(2):
            pairs = [
                (4 * a + 2 * b + micro, 4 * section + 2 * a + b)
                for a in range(2)
                for b in range(2)
            ]
            moved.append(lax.ppermute(part, ("section", "y", "core"), pairs))
        return jnp.stack(moved)

    layer_outputs = jnp.where(s == 0, block_rows(outs[0]), block_from_ranks(outs[1], 1))
    grad_inputs = jnp.where(s == 1, block_rows(grads[1]), block_from_ranks(grads[0], 0))

    down_block, reduce, got_gu = blocks
    extra = pack(smalls_grad, nz)
    extra = extra + flip(extra, "core")
    down_rows = R_FF // nz
    extra_count = extra.shape[1]
    got_in = share(queue["in1"], queue["in0"], 50, (grad_inputs, layer_outputs))
    extra = copy_after(narrow(extra).reshape(-1, HALF), got_in[0]).reshape(extra.shape)
    last = jnp.concatenate([down_block.reshape(nz, down_rows, HALF), extra], axis=1)
    reduce("down0", last.reshape(-1, HALF))
    down0, extra = queue["down0"][:down_rows], queue["down0"][down_rows:]

    place = jnp.stack([y, core]).astype(jnp.int32)
    grad_w_gu = got_gu
    got_out = share(queue["out1"], queue["out0"], 30, (got_in[0],))
    shared = swap(extra).astype(F32)
    grad_w_in, grad_w_qkv = spread_in(place, got_in)
    got_down = share(queue["down1"], down0, 30, (grad_w_in,))
    out_rows, o_rows = R_SSM // nz, R_ATT // nz
    grad_w_out = spread_rows(place, got_out, 0, out_rows, out_rows)
    grad_w_o = spread_rows(place, got_out, out_rows, o_rows, o_rows)
    grad_w_down = spread_rows(place, got_down, 0, down_rows, down_rows)

    width, conv_width, ssm_width = D // nz, CONV_W // nz, D_SSM // nz
    heads_width = SSM_HEADS // nz
    dt_all = jnp.where(s == 0, shared[:, :R_HEADS, :width], shared[:, :R_HEADS, PART : PART + width])
    grad_w_in = with_dt(grad_w_in, dt_all.reshape(SSM_HEADS, width)).T
    small_sum = jnp.sum(shared[:, 16:], axis=0)
    small_sum = jnp.where(s == 0, small_sum[:8], small_sum[8:])
    head_row = small_sum[7, : 3 * LANES].reshape(3, LANES)
    cuts = (
        jnp.stack([small_sum[0, :width], small_sum[0, PART : PART + width]]),
        head_row[:, :heads_width],
        small_sum[1:6, :conv_width],
        small_sum[6:7, :ssm_width],
    )
    return (
        layer_outputs[None, :, None],
        grad_inputs[None, :, None],
        cuts[0][None],
        cuts[1][None],
        cuts[2][None],
        cuts[3],
        grad_w_in[None],
        grad_w_out[None],
        grad_w_qkv[None],
        grad_w_o[None],
        grad_w_gu[None],
        grad_w_down[None],
    )


def solution(mesh):
    CHANNELS.clear()
    sections, ctx, fsdp = mesh.devices.shape
    fine = Mesh(
        mesh.devices.reshape(sections, ctx // 2, 2, fsdp), ("section", "y", "core", "fsdp")
    )
    tokens = ("y", "core")
    in_specs = (
        P(None, "fsdp", tokens, None),
        P(None, "fsdp", tokens, None),
        P("section", None, "fsdp"),
        P("section", None, "fsdp"),
        P("section", None, "fsdp"),
        P("section", "fsdp"),
    ) + (P("section", "fsdp", None),) * 6
    out_specs = (
        P("section", None, "fsdp", tokens, None),
        P("section", None, "fsdp", tokens, None),
        P("section", None, "fsdp"),
        P("section", None, "fsdp"),
        P("section", None, "fsdp"),
        P("section", "fsdp"),
    ) + (P("section", "fsdp", None),) * 6
    return jax.shard_map(body, mesh=fine, in_specs=in_specs, out_specs=out_specs, check_vma=False)
```

```python
import functools

import jax
import jax.numpy as jnp
from jax import lax
from jax.experimental import pallas as pl
from jax.experimental.pallas import tpu as pltpu
from jax.sharding import Mesh
from jax.sharding import PartitionSpec as P

D = 2048
FF = 4096
SSM_HEADS = 48
SSM_HEAD = 64
STATE = 256
Q_HEADS = 8
KV_HEADS = 2
HEAD_DIM = 128
CONV_K = 4
D_SSM = 3072
CONV_W = 3584
D_IN = 6704
ATT = 1024
KV = 256
EPSILON = 1e-05
ROPE_BASE = 10000.0
NEGATIVE = -1e30
HIGHEST = lax.Precision.HIGHEST

RANKS = 4
R_HEADS = SSM_HEADS // RANKS
R_SSM = D_SSM // RANKS
R_BC = 2 * STATE // RANKS
R_CONV = R_SSM + R_BC
R_ATT = ATT // RANKS
R_FF = FF // RANKS
R_OUT = R_SSM + R_ATT
HALF = 1024
PART = HALF // 2
MESH = pl.DeviceIdType.MESH
BF = jnp.bfloat16
F32 = jnp.float32


def rank_place():
    return 2 * lax.axis_index("section") + lax.axis_index("y")


def rank_id(rank):
    return {"section": rank // 2, "y": lax.rem(rank, 2)}


def greet(me):
    barrier = pltpu.get_barrier_semaphore()
    for step in range(1, RANKS):
        pl.semaphore_signal(
            barrier, inc=1, device_id=rank_id(lax.rem(me + step, RANKS)), device_id_type=MESH
        )
    pl.semaphore_wait(barrier, RANKS - 1)


def swap_kernel(with_stat, *refs):
    if with_stat:
        send_ref, stat_ref, out_ref, all_stat_ref, send_sem, recv_sem, stat_send, stat_recv = refs
    else:
        send_ref, out_ref, send_sem, recv_sem = refs
    me = rank_place()
    greet(me)
    copies = []
    for step in range(1, RANKS):
        other = lax.rem(me + step, RANKS)
        copies.append(
            pltpu.make_async_remote_copy(
                src_ref=send_ref.at[other] if len(send_ref.shape) == 3 else send_ref,
                dst_ref=out_ref.at[me],
                send_sem=send_sem.at[step - 1],
                recv_sem=recv_sem.at[step - 1],
                device_id=rank_id(other),
                device_id_type=MESH,
            )
        )
        if with_stat:
            copies.append(
                pltpu.make_async_remote_copy(
                    src_ref=stat_ref,
                    dst_ref=all_stat_ref.at[me],
                    send_sem=stat_send.at[step - 1],
                    recv_sem=stat_recv.at[step - 1],
                    device_id=rank_id(other),
                    device_id_type=MESH,
                )
            )
    for copy in copies:
        copy.start()
    if len(send_ref.shape) == 3:
        out_ref[me] = send_ref[me]
    else:
        out_ref[me] = send_ref[...]
    if with_stat:
        all_stat_ref[me] = stat_ref[...]
    for copy in copies:
        copy.wait()


CHANNELS = {}


def channel(name, *operands):
    key = (name,) + tuple((o.shape, str(o.dtype)) for o in operands)
    return CHANNELS.setdefault(key, len(CHANNELS))


def lasting(us):
    return pl.CostEstimate(flops=0, transcendentals=0, bytes_accessed=int(us * 850000))


VMEM_SPEC = pl.BlockSpec(memory_space=pltpu.VMEM)
ANY_SPEC = pl.BlockSpec(memory_space=pl.ANY)


def ignoring(kernel, used, extra):
    if not extra:
        return kernel
    return lambda *refs: kernel(*refs[:used], *refs[used + extra :])


def swap(values, stat=None, after=()):
    out_shape = [jax.ShapeDtypeStruct((RANKS,) + values.shape[-2:], values.dtype)]
    scratch = [pltpu.SemaphoreType.DMA((RANKS - 1,)), pltpu.SemaphoreType.DMA((RANKS - 1,))]
    args = [values]
    if stat is not None:
        out_shape.append(jax.ShapeDtypeStruct((RANKS,) + stat.shape, stat.dtype))
        scratch += scratch
        args.append(stat)
    out = pl.pallas_call(
        ignoring(functools.partial(swap_kernel, stat is not None), len(args), len(after)),
        out_shape=out_shape,
        in_specs=[VMEM_SPEC] * len(args) + [pl.BlockSpec(memory_space=pl.ANY)] * len(after),
        out_specs=[VMEM_SPEC] * len(out_shape),
        scratch_shapes=scratch,
        cost_estimate=lasting(9),
        compiler_params=pltpu.CompilerParams(
            collective_id=channel("swap", *args, *after),
            has_side_effects=True,
            vmem_limit_bytes=32 * 2**20,
        ),
    )(*args, *after)
    return out if stat is not None else out[0]


def scatter_sum(me, rows, part_ref, slots, send_sem, recv_sem):
    copies = []
    for step in range(1, RANKS):
        other = lax.rem(me + step, RANKS)
        copies.append(
            pltpu.make_async_remote_copy(
                src_ref=part_ref.at[pl.ds(pl.multiple_of(other * rows, rows), rows)],
                dst_ref=slots.at[step - 1],
                send_sem=send_sem.at[step - 1],
                recv_sem=recv_sem.at[step - 1],
                device_id=rank_id(other),
                device_id_type=MESH,
            )
        )
    for copy in copies:
        copy.start()
    total = part_ref[pl.ds(pl.multiple_of(me * rows, rows), rows), :].astype(F32)
    for step, copy in enumerate(copies):
        copy.wait()
        total = total + slots[step].astype(F32)
    return total


def spread(me, rows, out_ref, send_sem, recv_sem):
    here = pl.ds(pl.multiple_of(me * rows, rows), rows)
    copies = []
    for step in range(1, RANKS):
        copies.append(
            pltpu.make_async_remote_copy(
                src_ref=out_ref.at[here],
                dst_ref=out_ref.at[here],
                send_sem=send_sem.at[step - 1],
                recv_sem=recv_sem.at[step - 1],
                device_id=rank_id(lax.rem(me + step, RANKS)),
                device_id_type=MESH,
            )
        )
    for copy in copies:
        copy.start()
    for copy in copies:
        copy.wait()


def mid_kernel(part_ref, resid_ref, gain_ref, mid_ref, out_ref, slots, s1, r1, s2, r2):
    rows = resid_ref.shape[0]
    me = rank_place()
    greet(me)
    mid = scatter_sum(me, rows, part_ref, slots, s1, r1) + resid_ref[...].astype(F32)
    mid_ref[...] = mid
    scale = lax.rsqrt(jnp.mean(mid * mid, axis=-1, keepdims=True) + EPSILON)
    out_ref[pl.ds(pl.multiple_of(me * rows, rows), rows), :] = (
        mid * scale * gain_ref[...].astype(F32)
    ).astype(BF)
    spread(me, rows, out_ref, s2, r2)


def end_rows_kernel(part_ref, resid_ref, out_ref, slots, s1, r1, s2, r2):
    me = rank_place()
    greet(me)
    total = scatter_sum(me, resid_ref.shape[0], part_ref, slots, s1, r1) + resid_ref[...]
    out_ref[...] = total.astype(BF)


def back_rows_kernel(
    part_ref, given_ref, value_ref, gain_ref, out_ref, gain_grad_ref, slots, s1, r1, s2, r2
):
    me = rank_place()
    greet(me)
    grad = scatter_sum(me, given_ref.shape[0], part_ref, slots, s1, r1)
    total, gain_grad_ref[...] = norm_back(grad, value_ref[...], gain_ref[...].astype(F32))
    out_ref[...] = (given_ref[...] + total).astype(BF)


def norm_back(grad, value, gain):
    scale = lax.rsqrt(jnp.mean(value * value, axis=-1, keepdims=True) + EPSILON)
    unit = value * scale
    scaled = grad * gain
    total = scale * (scaled - unit * jnp.mean(scaled * unit, axis=-1, keepdims=True))
    return total, jnp.sum(grad * unit, axis=0, keepdims=True)


def end_kernel(part_ref, resid_ref, out_ref, slots, s1, r1, s2, r2):
    rows = resid_ref.shape[0]
    me = rank_place()
    greet(me)
    total = scatter_sum(me, rows, part_ref, slots, s1, r1) + resid_ref[...]
    out_ref[pl.ds(pl.multiple_of(me * rows, rows), rows), :] = total.astype(BF)
    spread(me, rows, out_ref, s2, r2)


def back_kernel(
    part_ref, given_ref, value_ref, gain_ref, wide_ref, out_ref, gain_grad_ref, slots, s1, r1, s2, r2
):
    rows = given_ref.shape[0]
    me = rank_place()
    greet(me)
    grad = scatter_sum(me, rows, part_ref, slots, s1, r1)
    total, gain_grad_ref[...] = norm_back(grad, value_ref[...], gain_ref[...].astype(F32))
    total = given_ref[...] + total
    wide_ref[...] = total
    out_ref[pl.ds(pl.multiple_of(me * rows, rows), rows), :] = total.astype(BF)
    spread(me, rows, out_ref, s2, r2)


def rank_call(kernel, out_shape, rows, *args, after=()):
    return pl.pallas_call(
        ignoring(kernel, len(args), len(after)),
        out_shape=out_shape,
        in_specs=[VMEM_SPEC] * len(args) + [pl.BlockSpec(memory_space=pl.ANY)] * len(after),
        out_specs=[VMEM_SPEC] * len(out_shape),
        scratch_shapes=[pltpu.VMEM((RANKS - 1, rows, D), BF)]
        + [pltpu.SemaphoreType.DMA((RANKS - 1,))] * 4,
        cost_estimate=lasting(27),
        compiler_params=pltpu.CompilerParams(
            collective_id=channel(kernel.__name__, *args, *after),
            has_side_effects=True,
            vmem_limit_bytes=32 * 2**20,
        ),
    )(*args, *after)


def mid_step(part, resid, gain):
    rows = resid.shape[0]
    return rank_call(
        mid_kernel,
        [jax.ShapeDtypeStruct((rows, D), F32), jax.ShapeDtypeStruct(part.shape, BF)],
        rows,
        part,
        resid,
        gain[None],
    )


def end_step(part, resid):
    rows = resid.shape[0]
    return rank_call(end_kernel, [jax.ShapeDtypeStruct(part.shape, BF)], rows, part, resid)[0]


def end_rows(part, resid):
    shape = jax.ShapeDtypeStruct(resid.shape, BF)
    return rank_call(end_rows_kernel, [shape], resid.shape[0], part, resid)[0]


def back_rows(part, given, value, gain):
    shapes = [jax.ShapeDtypeStruct(given.shape, BF), jax.ShapeDtypeStruct((1, D), F32)]
    return rank_call(back_rows_kernel, shapes, given.shape[0], part, given, value, gain[None])


def back_step(part, given, value, gain, after=()):
    rows = given.shape[0]
    return rank_call(
        back_kernel,
        [
            jax.ShapeDtypeStruct((rows, D), F32),
            jax.ShapeDtypeStruct(part.shape, BF),
            jax.ShapeDtypeStruct((1, D), F32),
        ],
        rows,
        part,
        given,
        value,
        gain[None],
        after=after,
    )


def copy_kernel(value_ref, out_ref):
    out_ref[...] = value_ref[...]


def copy_after(value, *tokens):
    rows, width = value.shape
    tile = min(rows, 128)
    block = pl.BlockSpec((tile, width), lambda i: (i, 0))
    return pl.pallas_call(
        ignoring(copy_kernel, 1, len(tokens)),
        grid=(rows // tile,),
        out_shape=jax.ShapeDtypeStruct(value.shape, value.dtype),
        in_specs=[block] + [ANY_SPEC] * len(tokens),
        out_specs=block,
    )(value, *tokens)


def product_kernel(left_a, left_b, right_a, right_b, out_ref):
    turned = lambda left, right: lax.dot_general(
        left[...], right[...], (((0,), (0,)), ((), ())), preferred_element_type=F32
    )
    out_ref[...] = (turned(left_a, right_a) + turned(left_b, right_b)).astype(BF)


def outer_sum(left, right, tokens):
    rows, width = left[0].shape
    columns_right = right[0].shape[1]
    tile = 256
    left_block = pl.BlockSpec((rows, tile), lambda i: (0, i))
    right_block = pl.BlockSpec((rows, columns_right), lambda i: (0, 0))
    return pl.pallas_call(
        ignoring(product_kernel, 4, len(tokens)),
        grid=(width // tile,),
        out_shape=jax.ShapeDtypeStruct((width, columns_right), BF),
        in_specs=[left_block] * 2 + [right_block] * 2 + [ANY_SPEC] * len(tokens),
        out_specs=pl.BlockSpec((tile, columns_right), lambda i: (i, 0)),
        cost_estimate=lasting(3),
        compiler_params=pltpu.CompilerParams(vmem_limit_bytes=56 * 2**20),
    )(*left, *right, *tokens)


def share_kernel(one_ref, zero_ref, *refs):
    own, own_c, across, across_c, local_sem, send_sem, recv_sem = refs[-7:]
    s, y, core = (lax.axis_index(name) for name in ("section", "y", "core"))
    rows = one_ref.shape[0]
    half = rows // 2
    barrier = pltpu.get_barrier_semaphore()
    ids = {"section": {"section": 1 - s}, "y": {"y": 1 - y}, "core": {"core": 1 - core}}
    for who in ids.values():
        pl.semaphore_signal(barrier, inc=1, device_id=who, device_id_type=MESH)
    pl.semaphore_wait(barrier, 3)

    def remote(k, src, dst, axis):
        return pltpu.make_async_remote_copy(
            src_ref=src, dst_ref=dst, send_sem=send_sem.at[k], recv_sem=recv_sem.at[k],
            device_id=ids[axis], device_id_type=MESH,
        )

    part = lambda ref, k: ref.at[pl.ds(half * k, half)]
    slot = lambda ref, place, k: ref.at[place, pl.ds(half * k, half)]
    for section, mine, sent in ((0, zero_ref, one_ref), (1, one_ref, zero_ref)):

        @pl.when(s == section)
        def _():
            for k in range(2):
                remote(k, part(sent, k), slot(own, section, k), "section").start()
            for k in range(2):
                remote(2 + k, part(mine, k), slot(across, section, k), "y").start()
            remote(6, mine, own_c.at[section], "core").start()
            keep = pltpu.make_async_copy(mine, own.at[section], local_sem)
            keep.start()
            for k in range(2):
                remote(k, part(sent, k), slot(own, 1 - section, k), "section").wait_recv()
                remote(4 + k, slot(own, 1 - section, k), slot(across, 1 - section, k), "y").start()
                remote(
                    7 + k, slot(own, 1 - section, k), slot(own_c, 1 - section, k), "core"
                ).start()
            for k in range(2):
                remote(2 + k, part(mine, k), slot(across, section, k), "y").wait_recv()
                remote(
                    9 + k, slot(across, section, k), slot(across_c, section, k), "core"
                ).start()
            for k in range(2):
                there = slot(across, 1 - section, k)
                remote(4 + k, slot(own, 1 - section, k), there, "y").wait_recv()
                remote(11 + k, there, slot(across_c, 1 - section, k), "core").start()
            remote(6, mine, own_c.at[section], "core").wait_recv()
            for k in range(2):
                there = slot(own_c, 1 - section, k)
                remote(7 + k, slot(own, 1 - section, k), there, "core").wait_recv()
                there = slot(across_c, section, k)
                remote(9 + k, slot(across, section, k), there, "core").wait_recv()
                there = slot(across_c, 1 - section, k)
                remote(11 + k, slot(across, 1 - section, k), there, "core").wait_recv()
            for k in range(2):
                remote(k, part(sent, k), slot(own, section, k), "section").wait_send()
                remote(2 + k, part(mine, k), slot(across, section, k), "y").wait_send()
                there = slot(across, 1 - section, k)
                remote(4 + k, slot(own, 1 - section, k), there, "y").wait_send()
                there = slot(own_c, 1 - section, k)
                remote(7 + k, slot(own, 1 - section, k), there, "core").wait_send()
                there = slot(across_c, section, k)
                remote(9 + k, slot(across, section, k), there, "core").wait_send()
                there = slot(across_c, 1 - section, k)
                remote(11 + k, slot(across, 1 - section, k), there, "core").wait_send()
            remote(6, mine, own_c.at[section], "core").wait_send()
            keep.wait()


def share(one, zero, us, after=()):
    shape = jax.ShapeDtypeStruct((2,) + one.shape, one.dtype)
    return pl.pallas_call(
        ignoring(share_kernel, 2, len(after)),
        out_shape=[shape] * 4,
        in_specs=[ANY_SPEC] * (2 + len(after)),
        out_specs=[ANY_SPEC] * 4,
        scratch_shapes=[
            pltpu.SemaphoreType.DMA,
            pltpu.SemaphoreType.DMA((13,)),
            pltpu.SemaphoreType.DMA((13,)),
        ],
        cost_estimate=lasting(us),
        compiler_params=pltpu.CompilerParams(
            collective_id=channel("share", one, zero, *after), has_side_effects=True
        ),
    )(one, zero, *after)


def chosen(place_ref, refs):
    y, core = place_ref[0], place_ref[1]
    values = [ref[...] for ref in refs]
    found = [[None, None], [None, None]]
    for side in range(2):
        flat = [jnp.where(core == side, values[2 * k], values[2 * k + 1]) for k in range(2)]
        for row in range(2):
            found[row][side] = jnp.where(y == row, flat[0], flat[1])
    return found


def rows_kernel(place_ref, a, b, c, d, out_ref):
    found = chosen(place_ref, (a, b, c, d))
    row = lax.rem(pl.program_id(0), 2)
    for side in range(2):
        value = jnp.where(row == 0, found[0][side][0], found[1][side][0])
        out_ref[:, HALF * side : HALF * (side + 1)] = value.astype(F32)


PLACE_SPEC = pl.BlockSpec(memory_space=pltpu.SMEM)


def spread_rows(place, pieces, first, count, tile):
    steps = count // tile
    block = pl.BlockSpec((1, tile, HALF), lambda r, i: (r // 2, first // tile + i, 0))
    return pl.pallas_call(
        rows_kernel,
        grid=(RANKS, steps),
        out_shape=jax.ShapeDtypeStruct((RANKS * count, D), F32),
        in_specs=[PLACE_SPEC] + [block] * 4,
        out_specs=pl.BlockSpec((tile, D), lambda r, i: (r * steps + i, 0)),
        compiler_params=pltpu.CompilerParams(vmem_limit_bytes=56 * 2**20),
    )(place, *pieces)


def gate_up_kernel(nz, place_ref, a, b, c, d, out_ref):
    found = chosen(place_ref, (a, b, c, d))
    width = R_FF // nz
    for side in range(2):
        for shard in range(nz):
            for rank in range(RANKS):
                start = FF * side + (FF // nz) * shard + width * rank
                out_ref[:, start : start + width] = found[rank % 2][side][
                    rank // 2, :, width * shard : width * (shard + 1)
                ].astype(F32)


def spread_gate_up(place, pieces, nz):
    rows = pieces[0].shape[1]
    tile = min(rows, 128)
    block = pl.BlockSpec((2, tile, HALF), lambda i: (0, i, 0))
    return pl.pallas_call(
        functools.partial(gate_up_kernel, nz),
        grid=(rows // tile,),
        out_shape=jax.ShapeDtypeStruct((rows, 2 * FF), F32),
        in_specs=[PLACE_SPEC] + [block] * 4,
        out_specs=pl.BlockSpec((tile, 2 * FF), lambda i: (i, 0)),
        compiler_params=pltpu.CompilerParams(vmem_limit_bytes=56 * 2**20),
    )(place, *pieces)


def in_kernel(place_ref, a, b, c, d, in_ref, qkv_ref):
    found = chosen(place_ref, (a, b, c, d))
    for rank in range(RANKS):
        left, right = (found[rank % 2][side][rank // 2].astype(F32) for side in range(2))
        in_ref[R_SSM * rank : R_SSM * (rank + 1)] = right[:, :R_SSM].T
        start = D_SSM + R_SSM * rank
        in_ref[start : start + R_SSM] = left[:, :R_SSM].T
        start = 2 * D_SSM + R_BC * rank
        in_ref[start : start + R_BC] = left[:, R_SSM:R_CONV].T
        qkv_ref[:, R_ATT * rank : R_ATT * (rank + 1)] = right[:, R_SSM:]
        start = ATT + KV * (rank % 2) + HEAD_DIM * (rank // 2)
        qkv_ref[:, start : start + HEAD_DIM] = left[:, R_CONV:]


def dt_kernel(whole_ref, dt_ref, out_ref):
    out_ref[...] = dt_ref[...]


def with_dt(whole, dt):
    rows, width = dt.shape
    tile = 16
    first = (whole.shape[0] - rows) // tile
    return pl.pallas_call(
        dt_kernel,
        grid=(rows // tile,),
        out_shape=jax.ShapeDtypeStruct(whole.shape, whole.dtype),
        in_specs=[ANY_SPEC, pl.BlockSpec((tile, width), lambda i: (i, 0))],
        out_specs=pl.BlockSpec((tile, width), lambda i: (first + i, 0)),
        input_output_aliases={0: 0},
    )(whole, dt)


def spread_in(place, pieces):
    rows = pieces[0].shape[1]
    tile = min(rows, 128)
    block = pl.BlockSpec((2, tile, HALF), lambda i: (0, i, 0))
    return pl.pallas_call(
        in_kernel,
        grid=(rows // tile,),
        out_shape=[
            jax.ShapeDtypeStruct((D_IN, rows), F32),
            jax.ShapeDtypeStruct((rows, ATT + 2 * KV), F32),
        ],
        in_specs=[PLACE_SPEC] + [block] * 4,
        out_specs=[
            pl.BlockSpec((D_IN, tile), lambda i: (0, i)),
            pl.BlockSpec((tile, ATT + 2 * KV), lambda i: (i, 0)),
        ],
        compiler_params=pltpu.CompilerParams(vmem_limit_bytes=56 * 2**20),
    )(place, *pieces)


LANES = 128


def turned_lanes(values, cosine, sine):
    parts = []
    for start in range(0, values.shape[1], HEAD_DIM):
        head = values[:, start : start + HEAD_DIM]
        parts.append(head * cosine + pltpu.roll(head, HEAD_DIM // 2, 1) * sine)
    return parts[0] if len(parts) == 1 else jnp.concatenate(parts, axis=1)


def exact(left, right, contract):
    return lax.dot_general(
        left, right, (contract, ((), ())), precision=HIGHEST, preferred_element_type=F32
    )


def mixer_back_kernel(
    nz, got_ref, scan_ref, z_ref, norm_ref, gain_ref, x_ref, b_ref, c_ref, raw_ref, heads_ref,
    run_ref, dt_ref, q_ref, k_ref, v_ref, probs_ref, cos_ref, sin_ref,
    message_ref, right_ref, dx_ref, draw_ref, heads_out_ref, lanes_out_ref,
):
    length = scan_ref.shape[0]
    inner = nz // RANKS
    wide, narrow_w = R_OUT // nz, R_SSM // nz
    d_norm = jnp.concatenate(
        [
            got_ref[r][:, wide * i : wide * i + narrow_w].astype(F32)
            for i in range(inner)
            for r in range(RANKS)
        ],
        axis=1,
    )
    d_o = jnp.concatenate(
        [
            got_ref[r][:, wide * i + narrow_w : wide * (i + 1)].astype(F32)
            for i in range(inner)
            for r in range(RANKS)
        ],
        axis=1,
    ).astype(BF)
    spread_of, overlap = norm_ref[:, 0:1], norm_ref[:, 1:2]
    scan, z = scan_ref[...], z_ref[...]
    sig = jax.nn.sigmoid(z)
    silu = z * sig
    gated = scan * silu
    lanes_out_ref[0:1, :] = jnp.sum(d_norm * gated * spread_of, axis=0, keepdims=True)
    d_gated = spread_of * d_norm * gain_ref[...] - gated * (
        spread_of * spread_of * overlap * (1.0 / D_SSM)
    )
    d_scan = d_gated * silu
    right_ref[:, :R_SSM] = (d_gated * scan * (sig * (1.0 + z * (1.0 - sig)))).astype(BF)

    row = lax.broadcasted_iota(jnp.int32, (length, length), 0)
    column = lax.broadcasted_iota(jnp.int32, (length, length), 1)
    allowed = row >= column

    scale = HEAD_DIM**-0.5
    key, value = k_ref[...], v_ref[...]
    d_key = jnp.zeros((length, HEAD_DIM), F32)
    d_value = jnp.zeros((length, HEAD_DIM), F32)
    for head in range(R_ATT // HEAD_DIM):
        cut = slice(HEAD_DIM * head, HEAD_DIM * (head + 1))
        query, grad, probs = q_ref[:, cut], d_o[:, cut], probs_ref[head]
        d_probs = dot_t(grad, value)
        d_scores = (
            probs * (d_probs - jnp.sum(probs * d_probs, axis=1, keepdims=True))
        ).astype(BF)
        d_query = dot(d_scores, key) * scale
        right_ref[:, R_SSM + HEAD_DIM * head : R_SSM + HEAD_DIM * (head + 1)] = turned_lanes(
            d_query, cos_ref[...], -sin_ref[...]
        ).astype(BF)
        d_key = d_key + t_dot(d_scores, query) * scale
        d_value = d_value + t_dot(probs.astype(BF), grad)

    b_rows, c_rows = b_ref[...], c_ref[...]
    mixing = dot_t(c_rows, b_rows)
    x = x_ref[...]
    lanes_out_ref[1:2, :] = jnp.sum(d_scan * x.astype(F32), axis=0, keepdims=True)
    grad_b = d_scan.astype(BF)
    run_t, dt_t = run_ref[...].T, dt_ref[...].T
    d_mixing = jnp.zeros((length, length), F32)
    lane = lax.broadcasted_iota(jnp.int32, (length, LANES), 1)
    head_row = lax.broadcasted_iota(jnp.int32, (LANES, length), 0)
    by_row = jnp.zeros((length, LANES), F32)
    direct = jnp.zeros((LANES, length), F32)
    for pair in range(R_HEADS // 2):
        cut = slice(LANES * pair, LANES * (pair + 1))
        x_pair, g_pair = x[:, cut], grad_b[:, cut]
        d_pair = []
        for side in range(2):
            head = 2 * pair + side
            mine = (lane < SSM_HEAD) if side == 0 else (lane >= SSM_HEAD)
            d_weights = dot_t(jnp.where(mine, g_pair, jnp.zeros_like(g_pair)), x_pair)
            gap = run_ref[:, head : head + 1] - run_t[head : head + 1, :]
            table = jnp.exp(jnp.where(allowed, gap, NEGATIVE))
            dt_row = dt_t[head : head + 1, :]
            faded = d_weights * table
            faded_dt = faded * dt_row
            d_mixing = d_mixing + faded_dt
            plain = faded * mixing
            direct = jnp.where(head_row == head, jnp.sum(plain, axis=0, keepdims=True), direct)
            by_row = jnp.where(
                lane == head, jnp.sum(faded_dt * mixing, axis=1, keepdims=True), by_row
            )
            weights = (table * mixing * dt_row).astype(BF)
            d_pair.append(t_dot(weights, g_pair))
        skip = jnp.where(
            lane[:1] < SSM_HEAD,
            heads_ref[2:3, 2 * pair : 2 * pair + 1],
            heads_ref[2:3, 2 * pair + 1 : 2 * pair + 2],
        )
        dx_ref[:, cut] = jnp.where(lane < SSM_HEAD, d_pair[0], d_pair[1]) + skip * d_scan[:, cut]
    d_mixing = d_mixing.astype(BF)
    d_c = dot(d_mixing, b_rows)
    d_b = t_dot(d_mixing, c_rows)
    for r in range(RANKS):
        source = d_b if r < 2 else d_c
        start = R_BC * (r % 2)
        message_ref[r, :, :R_BC] = source[:, start : start + R_BC].astype(BF)
        message_ref[r, :, R_BC:] = (d_key if r % 2 == 0 else d_value).astype(BF)

    later = (column >= row).astype(F32)
    from_rows_sum = exact(later, by_row, ((1,), (0,)))
    grad_step = from_rows_sum - exact(later, direct * dt_t, ((1,), (1,)))
    grad_dt = direct.T
    bias, log = heads_ref[0:1, :], heads_ref[1:2, :]
    raw = raw_ref[...] + bias
    rate = jnp.exp(log)
    step = -jax.nn.softplus(raw) * rate
    valid = lane < R_HEADS
    grad_dt = grad_dt - grad_step * rate
    grad_raw = jnp.where(valid, grad_dt * jax.nn.sigmoid(raw), 0.0)
    draw_ref[...] = grad_raw.astype(BF)
    heads_out_ref[0:1, :] = jnp.sum(grad_raw, axis=0, keepdims=True)
    heads_out_ref[1:2, :] = jnp.sum(grad_step * step, axis=0, keepdims=True)


def whole_block(array):
    shape = array.shape
    return pl.BlockSpec(shape, lambda i: (0,) * len(shape), pipeline_mode=pl.Buffered(1))


def mixer_back(got, kept, small, overlap, tables):
    length = got.shape[1]
    nz = lax.axis_size("fsdp")
    norm = jnp.stack([kept["spread"], overlap], axis=1)
    shape = jax.ShapeDtypeStruct
    out_shape = [
        shape((RANKS, length, 2 * R_BC), BF),
        shape((length, HALF), BF),
        shape((length, R_SSM), F32),
        shape((length, LANES), BF),
        shape((8, LANES), F32),
        shape((8, R_SSM), F32),
    ]
    args = (
        got, kept["scan"], kept["z"], norm, small["ssm_gain"][None], kept["u"][:, :R_SSM],
        kept["b"], kept["c"], kept["dt_raw"], small["heads"], kept["running"], kept["dt"],
        kept["query"], kept["key"], kept["value"],
        kept["probs"], *tables,
    )
    return pl.pallas_call(
        functools.partial(mixer_back_kernel, nz),
        grid=(1,),
        out_shape=out_shape,
        in_specs=[whole_block(arg) for arg in args],
        out_specs=[whole_block(out) for out in out_shape],
        cost_estimate=lasting(16),
        compiler_params=pltpu.CompilerParams(vmem_limit_bytes=56 * 2**20),
    )(*args)


def conv_back_kernel(
    place_ref, back_ref, dx_ref, xbc_ref, table_ref, cos_ref, sin_ref, left_ref, conv_ref
):
    y, s = place_ref[0], place_ref[1]
    length = dx_ref.shape[0]
    back = [back_ref[r].astype(F32) for r in range(RANKS)]
    d_bc = (back[0] + back[1] + back[2] + back[3])[:, :R_BC]
    d_kv = jnp.where(s == 0, back[0] + back[1], back[2] + back[3])[:, R_BC:]
    d_kv = jnp.where(y == 0, turned_lanes(d_kv, cos_ref[...], -sin_ref[...]), d_kv)
    left_ref[:, R_CONV:] = d_kv.astype(BF)
    d_u = jnp.concatenate([dx_ref[...], d_bc], axis=1)
    wide = xbc_ref[...].astype(F32)
    place = lax.broadcasted_iota(jnp.int32, (length, R_CONV), 0)
    moved = []
    before = table_ref[CONV_K : CONV_K + 1, :] + jnp.zeros_like(wide)
    for tap in range(CONV_K):
        steps = CONV_K - 1 - tap
        value = wide
        if steps:
            value = jnp.where(place >= steps, pltpu.roll(wide, steps, 0), 0.0)
        moved.append(value)
        before = before + table_ref[tap : tap + 1, :] * value
    sig = jax.nn.sigmoid(before)
    d_before = d_u * (sig * (1.0 + before * (1.0 - sig)))
    d_xbc = jnp.zeros_like(wide)
    for tap in range(CONV_K):
        conv_ref[tap : tap + 1, :] = jnp.sum(d_before * moved[tap], axis=0, keepdims=True)
        steps = CONV_K - 1 - tap
        value = d_before
        if steps:
            value = jnp.where(
                place < length - steps, pltpu.roll(d_before, length - steps, 0), 0.0
            )
        d_xbc = d_xbc + table_ref[tap : tap + 1, :] * value
    conv_ref[CONV_K : CONV_K + 1, :] = jnp.sum(d_before, axis=0, keepdims=True)
    left_ref[:, :R_CONV] = d_xbc.astype(BF)


def conv_back(back, d_x, xbc, table, tables):
    length = d_x.shape[0]
    place = jnp.stack([lax.axis_index("y"), lax.axis_index("section")]).astype(jnp.int32)
    args = (back, d_x, xbc, table, *tables)
    out_shape = [
        jax.ShapeDtypeStruct((length, HALF), BF),
        jax.ShapeDtypeStruct((8, R_CONV), F32),
    ]
    return pl.pallas_call(
        conv_back_kernel,
        grid=(1,),
        out_shape=out_shape,
        in_specs=[PLACE_SPEC] + [whole_block(arg) for arg in args],
        out_specs=[whole_block(out) for out in out_shape],
        cost_estimate=lasting(7),
        compiler_params=pltpu.CompilerParams(vmem_limit_bytes=56 * 2**20),
    )(place, *args)


EXTRA = 32


def pack_kernel(nz, *refs):
    out_ref, conv_full, ssm_full = refs[-3:]
    rank = rank_place()
    out_ref[...] = jnp.zeros_like(out_ref)
    width, conv_width, ssm_width = D // nz, CONV_W // nz, D_SSM // nz
    heads_width, inner = SSM_HEADS // nz, nz // RANKS
    head_of = lax.broadcasted_iota(jnp.int32, (R_SSM, LANES), 0) // SSM_HEAD
    lane = lax.broadcasted_iota(jnp.int32, (R_SSM, LANES), 1)
    to_heads = (head_of == lane).astype(F32)
    for layer in range(2):
        heads_ref, lanes_ref, conv_ref, gain0_ref, gain1_ref, dt_ref = refs[6 * layer : 6 * layer + 6]
        conv_full[...] = jnp.zeros_like(conv_full)
        ssm_full[...] = jnp.zeros_like(ssm_full)
        at = lambda start, size: pl.ds(pl.multiple_of(start, LANES), size)
        conv_full[:, at(R_SSM * rank, R_SSM)] = conv_ref[:, :R_SSM]
        conv_full[:, at(D_SSM + R_BC * rank, R_BC)] = conv_ref[:, R_SSM:]
        ssm_full[:, at(R_SSM * rank, R_SSM)] = lanes_ref[...]
        skip = exact(lanes_ref[...], to_heads, ((1,), (0,)))[1:2]
        heads = (heads_ref[0:1], heads_ref[1:2], skip)
        row = 16 + 8 * layer
        for z in range(nz):
            cut = slice(width * z, width * (z + 1))
            out_ref[z, 0:16, PART * layer : PART * layer + width] = dt_ref[:, cut]
            out_ref[z, row : row + 1, 0:width] = gain0_ref[:, cut]
            out_ref[z, row : row + 1, PART : PART + width] = gain1_ref[:, cut]
            out_ref[z, row + 1 : row + 6, 0:conv_width] = conv_full[
                0 : CONV_K + 1, conv_width * z : conv_width * (z + 1)
            ]
            out_ref[z, row + 6 : row + 7, 0:ssm_width] = ssm_full[
                0:1, ssm_width * z : ssm_width * (z + 1)
            ]
            start = heads_width * (z % inner)
            for k in range(3):
                value = jnp.where(rank == z // inner, heads[k], 0.0)
                out_ref[z, row + 7 : row + 8, LANES * k : LANES * k + heads_width] = value[
                    :, start : start + heads_width
                ]


def pack(layers, nz):
    args = [array for layer in layers for array in layer]
    out = jax.ShapeDtypeStruct((nz, EXTRA, HALF), F32)
    return pl.pallas_call(
        functools.partial(pack_kernel, nz),
        grid=(1,),
        out_shape=out,
        in_specs=[whole_block(arg) for arg in args],
        out_specs=whole_block(out),
        scratch_shapes=[pltpu.VMEM((8, CONV_W), F32), pltpu.VMEM((8, D_SSM), F32)],
        cost_estimate=lasting(4),
        compiler_params=pltpu.CompilerParams(vmem_limit_bytes=40 * 2**20),
    )(*args)


def rotation_tables(length):
    half = HEAD_DIM // 2
    frequency = ROPE_BASE ** (-jnp.arange(half, dtype=F32) / half)
    angles = jnp.arange(length, dtype=F32)[:, None] * frequency[None, :]
    cosine, sine = jnp.cos(angles), jnp.sin(angles)
    return jnp.concatenate([cosine, cosine], 1), jnp.concatenate([-sine, sine], 1)


def narrow(values):
    return values.astype(BF)


def dot(left, right):
    return jnp.dot(left, right, preferred_element_type=F32)


def dot_t(left, right):
    return lax.dot_general(left, right, (((1,), (1,)), ((), ())), preferred_element_type=F32)


def t_dot(left, right):
    return lax.dot_general(left, right, (((0,), (0,)), ((), ())), preferred_element_type=F32)


def columns(array, start, width):
    return lax.dynamic_slice_in_dim(array, start, width, axis=1)


def cut_rows(array, start, width):
    return lax.dynamic_slice_in_dim(array, start, width, axis=0)


def rms(values, gain):
    return values * lax.rsqrt(jnp.mean(values * values, axis=-1, keepdims=True) + EPSILON) * gain


def rotary(values, turning):
    length, width = values.shape
    half = HEAD_DIM // 2
    frequency = ROPE_BASE ** (-jnp.arange(half, dtype=F32) / half)
    angles = jnp.arange(length, dtype=F32)[:, None] * frequency[None, :]
    cosine = jnp.cos(angles)[:, None, :]
    sine = turning * jnp.sin(angles)[:, None, :]
    halves = values.reshape(length, width // HEAD_DIM, 2, half)
    first, second = halves[:, :, 0], halves[:, :, 1]
    return jnp.stack(
        [first * cosine - second * sine, second * cosine + first * sine], axis=2
    ).reshape(length, width)


def causal(length):
    position = jnp.arange(length)
    return position[:, None] >= position[None, :]


def shifted(values, steps):
    if steps == 0:
        return values
    blank = jnp.zeros((abs(steps), values.shape[1]), values.dtype)
    if steps > 0:
        return jnp.concatenate([blank, values[:-steps]], axis=0)
    return jnp.concatenate([values[-steps:], blank], axis=0)


def conv_sum(rows, table):
    wide = rows.astype(F32)
    total = table[CONV_K][None, :]
    for tap in range(CONV_K):
        total = total + table[tap][None, :] * shifted(wide, CONV_K - 1 - tap)
    return total


def decays(dt_raw, heads):
    dt = jax.nn.softplus(dt_raw + heads[0][None, :])
    step = -dt * jnp.exp(heads[1])[None, :]
    length = dt.shape[0]
    running = jnp.dot(causal(length).astype(F32), step, precision=HIGHEST)
    return dt, step, running


def decay_table(running):
    length = running.shape[0]
    turned = running.T
    gap = turned[:, :, None] - turned[:, None, :]
    return jnp.exp(jnp.where(causal(length)[None], gap, NEGATIVE))


def by_head(values):
    return values.reshape(values.shape[0], R_HEADS, SSM_HEAD)


def scan_forward(x, b_rows, c_rows, dt_raw, heads):
    dt, _, running = decays(dt_raw, heads)
    mixing = dot_t(c_rows, b_rows)
    weights = narrow(decay_table(running[:, :R_HEADS]) * mixing[None] * dt.T[:R_HEADS, None, :])
    x_heads = by_head(x)
    result = jnp.einsum("hts,shp->thp", weights, x_heads, preferred_element_type=F32)
    result = result + heads[2][None, :R_HEADS, None] * x_heads.astype(F32)
    return result.reshape(x.shape), running, dt


def scan_backward(x, b_rows, c_rows, dt_raw, heads, grad_y):
    dt, step, running = decays(dt_raw, heads)
    length = x.shape[0]
    mixing = dot_t(c_rows, b_rows)
    table = decay_table(running)
    dt_t = dt.T
    x_heads = by_head(x)
    grad_heads = by_head(narrow(grad_y))
    grad_weights = jnp.einsum("thp,shp->hts", grad_heads, x_heads, preferred_element_type=F32)
    faded = grad_weights * table
    weights = table * mixing[None] * dt_t[:, None, :]
    grad_x = jnp.einsum("hts,thp->shp", narrow(weights), grad_heads, preferred_element_type=F32)
    grad_y_heads = by_head(grad_y)
    grad_x = grad_x + heads[2][None, :, None] * grad_y_heads
    grad_skip = jnp.sum(grad_y_heads * x_heads.astype(F32), axis=(0, 2))
    grad_mixing = narrow(jnp.sum(faded * dt_t[:, None, :], axis=0))
    grad_c = dot(grad_mixing, b_rows)
    grad_b = t_dot(grad_mixing, c_rows)
    plain = faded * mixing[None]
    grad_dt = jnp.sum(plain, axis=1)
    grad_gap = plain * dt_t[:, None, :]
    grad_running = jnp.sum(grad_gap, axis=2) - jnp.sum(grad_gap, axis=1)
    grad_step = jnp.dot(grad_running, causal(length).astype(F32), precision=HIGHEST).T
    grad_dt = grad_dt.T - grad_step * jnp.exp(heads[1])[None, :]
    grad_log = jnp.sum(grad_step * step, axis=0)
    grad_raw = grad_dt * jax.nn.sigmoid(dt_raw + heads[0][None, :])
    grad_table = jnp.stack([jnp.sum(grad_raw, axis=0), grad_log, grad_skip])
    return grad_x.reshape(x.shape), grad_b, grad_c, grad_raw, grad_table


def attend(query, key, value):
    length = query.shape[0]
    heads = query.reshape(length, -1, HEAD_DIM)
    scores = jnp.einsum("qhd,sd->hqs", heads, key, preferred_element_type=F32) * HEAD_DIM**-0.5
    scores = jnp.where(causal(length)[None], scores, NEGATIVE)
    weights = jnp.exp(scores - jnp.max(scores, axis=-1, keepdims=True))
    probs = weights / jnp.sum(weights, axis=-1, keepdims=True)
    mixed = jnp.einsum("hqs,sd->qhd", narrow(probs), value, preferred_element_type=F32)
    return narrow(mixed.reshape(query.shape)), probs


def attend_back(query, key, value, probs, grad_out):
    length = query.shape[0]
    heads = query.reshape(length, -1, HEAD_DIM)
    grad_heads = grad_out.reshape(length, -1, HEAD_DIM)
    grad_probs = jnp.einsum("qhd,sd->hqs", grad_heads, value, preferred_element_type=F32)
    grad_scores = narrow(
        probs * (grad_probs - jnp.sum(probs * grad_probs, axis=-1, keepdims=True))
    )
    scale = HEAD_DIM**-0.5
    grad_query = jnp.einsum("hqs,sd->qhd", grad_scores, key, preferred_element_type=F32) * scale
    grad_key = jnp.einsum("hqs,qhd->sd", grad_scores, heads, preferred_element_type=F32) * scale
    grad_value = jnp.einsum("hqs,qhd->sd", narrow(probs), grad_heads, preferred_element_type=F32)
    return grad_query.reshape(query.shape), grad_key, grad_value


def flip(value, axis):
    return lax.ppermute(value, axis, [(0, 1), (1, 0)])


def layer_forward(entering, resid, weights, small, then, last):
    s, y = lax.axis_index("section"), lax.axis_index("y")
    length = entering.shape[0]
    x1 = narrow(rms(entering.astype(F32), small["gain0"][None, :]))
    left = dot(x1, weights["in"][0])
    right = dot(x1, weights["in"][1])
    dt_raw = dot(x1, weights["dt"])
    xbc = narrow(left[:, :R_CONV])
    u = narrow(jax.nn.silu(conv_sum(xbc, small["conv"])))
    kv_raw = left[:, R_CONV:]
    kv = narrow(jnp.where(y == 0, rotary(kv_raw, 1.0), kv_raw))
    shared = swap(jnp.concatenate([u[:, R_SSM:], kv], axis=1))
    then("swap", shared)
    b_rows = jnp.concatenate([shared[0, :, :R_BC], shared[1, :, :R_BC]], axis=1)
    c_rows = jnp.concatenate([shared[2, :, :R_BC], shared[3, :, :R_BC]], axis=1)
    pair = lax.dynamic_slice_in_dim(shared, 2 * s, 2, axis=0)[:, :, R_BC:]
    key, value = pair[0], pair[1]
    z = right[:, :R_SSM]
    query = narrow(rotary(right[:, R_SSM:], 1.0))
    o, probs = attend(query, key, value)
    x = u[:, :R_SSM]
    scan, running, dt = scan_forward(x, b_rows, c_rows, dt_raw, small["heads"])
    gated = scan * jax.nn.silu(z)
    squares = jnp.sum(gated * gated, axis=1)
    scaled = narrow(gated * small["ssm_gain"][None, :])
    message = to_rows(scaled, o)
    stat = jnp.broadcast_to(squares[None, :], (8, length))
    got, stats = swap(message, stat)
    spread_of = lax.rsqrt(jnp.sum(stats[:, 0, :], axis=0) / D_SSM + EPSILON)
    wide = jnp.transpose(got, (1, 0, 2)).reshape(length, R_OUT)
    is_ssm = small["is_ssm"][None, :]
    mo = narrow(jnp.where(is_ssm, wide.astype(F32) * spread_of[:, None], wide.astype(F32)))
    part = jnp.concatenate([dot(mo, weights["out"][0]), dot(mo, weights["out"][1])], axis=1)
    mid, x2 = mid_step(narrow(part), resid, small["gain1"])
    then("mid", mid)
    gate = dot(x2, weights["gu"][0])
    up = dot(x2, weights["gu"][1])
    act = narrow(jax.nn.silu(gate) * up)
    part2 = jnp.concatenate([dot(act, weights["down"][0]), dot(act, weights["down"][1])], axis=1)
    leaving = (end_rows if last else end_step)(narrow(part2), mid)
    kept = dict(
        resid=resid, x1=x1, xbc=xbc, u=u, b=b_rows, c=c_rows, key=key, value=value, query=query,
        probs=probs, z=z, dt_raw=dt_raw, scan=scan, spread=spread_of, mo=mo, mid=mid, x2=x2,
        gate=gate, up=up, act=act, running=running, dt=dt,
    )
    return leaving, kept


def to_rows(ssm_part, att_part):
    length = ssm_part.shape[0]
    nz = lax.axis_size("fsdp")
    inner = nz // RANKS
    a = ssm_part.reshape(length, inner, RANKS, R_SSM // nz)
    b = att_part.reshape(length, inner, RANKS, R_ATT // nz)
    both = jnp.concatenate([a, b], axis=3)
    return jnp.transpose(both, (2, 0, 1, 3)).reshape(RANKS, length, R_OUT // RANKS)


def from_rows(got):
    length = got.shape[1]
    nz = lax.axis_size("fsdp")
    inner = nz // RANKS
    both = jnp.transpose(got.reshape(RANKS, length, inner, R_OUT // nz), (1, 2, 0, 3))
    a = both[..., : R_SSM // nz].reshape(length, R_SSM)
    b = both[..., R_SSM // nz :].reshape(length, R_ATT)
    return a, b


def layer_backward(grad, given, kept, weights, small, queue, layer, tables, first=(), earlier=None):
    s, y = lax.axis_index("section"), lax.axis_index("y")
    core = lax.axis_index("core")
    length = grad.shape[0]
    down, gu, out, win = weights["down"], weights["gu"], weights["out"], weights["in"]

    def product(left, right, *tokens):
        mine = jnp.where(core == 0, right[0], right[1])
        theirs = jnp.where(core == 0, right[1], right[0])
        return outer_sum((left, flip(left, "core")), (mine, flip(theirs, "core")), tokens)

    def reduce(name, block):
        nonlocal queue
        if queue:
            block, queue["last"] = lax.optimization_barrier((block, queue["last"]))
        queue[name] = queue["last"] = lax.psum_scatter(
            block, "fsdp", scatter_dimension=0, tiled=True
        )

    def due(point):
        return [queue[k] for k in WAITS[layer].get(point, ())]

    halves = lambda v: (v[:, :HALF], v[:, HALF:])
    g0, g1 = halves(grad)
    down_block = None
    if layer == 1:
        reduce("down1", product(kept["act"], (g0, g1)))
    grad_act = dot_t(g0, down[0]) + dot_t(g1, down[1])
    gate, up = kept["gate"], kept["up"]
    sig = jax.nn.sigmoid(gate)
    d_gate = narrow(grad_act * up * (sig * (1.0 + gate * (1.0 - sig))))
    d_up = narrow(grad_act * gate * sig)
    part = dot_t(d_gate, gu[0]) + dot_t(d_up, gu[1])
    if layer == 1:
        reduce("gu1", product(kept["x2"], (d_gate, d_up), *first))
    d_mid, db, grad_gain1 = back_step(
        narrow(part), given, kept["mid"], small["gain1"], due("mlp") + list(first)
    )
    if layer == 0:
        reduce("gu0", product(kept["x2"], (d_gate, d_up), db))
    b0, b1 = halves(db)
    if layer == 0:
        down_block = product(kept["act"], (g0, g1), db)
    d_mo = dot_t(b0, out[0]) + dot_t(b1, out[1])
    mo = kept["mo"]
    is_ssm = small["is_ssm"][None, :]
    stat_row = jnp.sum(jnp.where(is_ssm, d_mo * mo.astype(F32), 0.0), axis=1)
    stat = jnp.broadcast_to(stat_row[None, :], (8, length))
    blocks = jnp.transpose(narrow(d_mo).reshape(length, RANKS, R_OUT // RANKS), (1, 0, 2))
    got, stats = swap(blocks, stat, due("norm"))
    overlap = jnp.sum(stats[:, 0, :], axis=0)
    message, d_right, d_x, d_raw, head_sums, lane_sums = mixer_back(
        got, kept, small, overlap, tables
    )
    out_block = product(kept["mo"], (b0, b1), message) if layer == 1 else None
    back = swap(message, None, due("scan"))
    d_left, grad_conv = conv_back(back, d_x, kept["xbc"], small["conv"], tables)
    part = dot_t(d_left, win[0]) + dot_t(d_right, win[1]) + dot_t(d_raw, weights["dt"])
    part = narrow(part)
    if layer == 1:
        reduce("in1", product(kept["x1"], (d_left, d_right), part))
    enter = (part, d_mid, kept["resid"].astype(F32), small["gain0"])
    if layer == 0:
        entering_grad, grad_gain0 = back_rows(*enter)
        reduce("in0", product(kept["x1"], (d_left, d_right), entering_grad))
    else:
        _, entering_grad, grad_gain0 = back_step(*enter, due("in"))
    got_gu = None
    if layer == 0:
        got_gu = share(queue["gu1"], queue["gu0"], 50, (entering_grad,))
        place = jnp.stack([y, core]).astype(jnp.int32)
        got_gu = spread_gate_up(place, got_gu, lax.axis_size("fsdp"))
        nz = lax.axis_size("fsdp")
        out_block = product(kept["mo"], (b0, b1), got_gu, down_block)
        both = [block.reshape(nz, -1, HALF) for block in (earlier, out_block)]
        reduce("outs", jnp.concatenate(both, axis=1).reshape(-1, HALF))
    grad_dt_w = t_dot(d_raw[:, :16], kept["x1"])
    smalls_grad = (head_sums, lane_sums, grad_conv, grad_gain0, grad_gain1, grad_dt_w)
    return entering_grad, smalls_grad, (
        out_block if layer == 1 else (down_block, reduce, got_gu)
    )


WAITS = (
    {"scan": ("in1",)},
    {"norm": ("down1",), "in": ("gu1",)},
)


def body(
    inputs, cotangent, norm_gains, head_params, conv_params, ssm_gain,
    w_in, w_out, w_qkv, w_o, w_gu, w_down,
):
    s, y = lax.axis_index("section"), lax.axis_index("y")
    core = lax.axis_index("core")
    nz = lax.axis_size("fsdp")
    z_place = lax.axis_index("fsdp")
    rank = 2 * s + y
    rows = inputs.shape[2]
    length = RANKS * rows
    w_in, w_out, w_qkv, w_o, w_gu, w_down = (
        w[0] for w in (w_in, w_out, w_qkv, w_o, w_gu, w_down)
    )

    flat = jnp.concatenate(
        [
            norm_gains[0].reshape(-1),
            head_params[0].reshape(-1),
            conv_params[0].reshape(-1),
            ssm_gain[0],
            w_in[:, D_SSM + CONV_W :].reshape(-1),
        ]
    )
    count = flat.shape[0]
    flat = jnp.pad(flat, (0, -count % 2048)).reshape(-1, 128)
    everything = lax.all_gather(flat, ("section", "fsdp"), axis=0).reshape(2, nz, -1)[..., :count]

    def unpack(layer):
        part = everything[layer]
        sizes = [2 * D // nz, 3 * SSM_HEADS // nz, 5 * CONV_W // nz, D_SSM // nz]
        starts = [0]
        for size in sizes:
            starts.append(starts[-1] + size)
        join = lambda k, lead: jnp.transpose(
            part[:, starts[k] : starts[k + 1]].reshape(nz, lead, -1), (1, 0, 2)
        ).reshape(lead, -1).astype(F32)
        gains, heads, conv, gain = join(0, 2), join(1, 3), join(2, 5), join(3, 1)[0]
        conv_own = jnp.concatenate(
            [columns(conv, R_SSM * rank, R_SSM), columns(conv, D_SSM + R_BC * rank, R_BC)], axis=1
        )
        channel = jnp.arange(R_OUT) % (R_OUT // nz)
        small = dict(
            gain0=gains[0],
            gain1=gains[1],
            heads=jnp.pad(
                columns(heads, R_HEADS * rank, R_HEADS), ((0, 0), (0, LANES - R_HEADS))
            ),
            conv=conv_own,
            ssm_gain=lax.dynamic_slice_in_dim(gain, R_SSM * rank, R_SSM),
            is_ssm=channel < R_SSM // nz,
        )
        dt_w = columns(part[:, starts[4] :].reshape(D, SSM_HEADS), R_HEADS * rank, R_HEADS)
        return small, jnp.pad(dt_w, ((0, 0), (0, LANES - R_HEADS)))

    def pieces(section):
        rk = 2 * section + y
        first = columns(w_in, jnp.where(core == 0, D_SSM, 0) + R_SSM * rk, R_SSM)
        second = jnp.where(
            core == 0,
            columns(w_in, 2 * D_SSM + R_BC * rk, R_BC),
            columns(w_qkv, R_ATT * rk, HEAD_DIM),
        )
        third = columns(
            w_qkv,
            jnp.where(core == 0, ATT + KV * y + HEAD_DIM * section, R_ATT * rk + HEAD_DIM),
            HEAD_DIM,
        )
        side = HALF * core
        out_rows, o_rows, down_rows = R_SSM // nz, R_ATT // nz, R_FF // nz
        ff = R_FF // nz
        return {
            "in": jnp.concatenate([first, second, third], axis=1),
            "out": jnp.concatenate(
                [
                    lax.dynamic_slice(w_out, (out_rows * rk, side), (out_rows, HALF)),
                    lax.dynamic_slice(w_o, (o_rows * rk, side), (o_rows, HALF)),
                ],
                axis=0,
            ),
            "gu": jnp.concatenate(
                [
                    columns(w_gu, FF * core + (FF // nz) * k + ff * rk, ff) for k in range(nz)
                ],
                axis=1,
            ),
            "down": lax.dynamic_slice(w_down, (down_rows * rk, side), (down_rows, HALF)),
        }

    order = []

    def in_turn(value):
        if order:
            value, order[-1] = lax.optimization_barrier((value, order[-1]))
        return value

    def gather(piece):
        order.append(lax.all_gather(in_turn(piece), ("core", "fsdp"), axis=0))
        return order[-1]

    own, other = pieces(s), pieces(1 - s)
    out_own = gather(own["out"])
    mlp = lambda found: jnp.concatenate([found["gu"], found["down"]], axis=0)
    in_arrived = flip(other["in"], "section")
    out_sent, in_arrived = lax.optimization_barrier((other["out"], in_arrived))
    out_arrived = flip(out_sent, "section")
    mlp_own = mlp(own)
    mlp_sent, out_arrived = lax.optimization_barrier((mlp(other), out_arrived))
    mlp_arrived = flip(mlp_sent, "section")
    of_layer = lambda layer, mine, theirs: jnp.where(s == layer, mine, theirs)
    flat_rows = lambda whole: whole.reshape(2, -1, HALF)
    in0 = gather(copy_after(of_layer(0, own["in"], in_arrived), everything, out_own))
    wide = own["gu"].shape[0]
    mlp0, mlp1 = (of_layer(layer, mlp_own, mlp_arrived) for layer in range(2))

    def together(token, *parts):
        whole = gather(copy_after(jnp.concatenate(parts, axis=0), token))
        whole = whole.reshape(2, nz, -1, HALF)
        found, at = [], 0
        for part in parts:
            found.append(flat_rows(whole[:, :, at : at + part.shape[0]]))
            at += part.shape[0]
        return found

    out_other, gu0, down0 = together(in0, out_arrived, mlp0[:wide], mlp0[wide:])
    weights = [
        dict(out=of_layer(layer, flat_rows(out_own), out_other)) for layer in range(2)
    ]
    weights[0].update({"in": flat_rows(in0), "gu": gu0, "down": down0})

    def then(point, token):
        if point == "swap":
            piece = of_layer(1, own["in"], in_arrived)
            weights[1]["in"] = flat_rows(gather(copy_after(piece, token)))
        elif point == "mid":
            weights[1]["gu"], weights[1]["down"] = together(token, mlp1[:wide], mlp1[wide:])

    def whole_sequence(own_rows):
        place = 2 * y + core
        result = jnp.zeros((RANKS, rows, D), BF)
        result = lax.dynamic_update_index_in_dim(
            result, lax.dynamic_index_in_dim(own_rows, core, 0, False), place, 0
        )
        for dy, dc in ((0, 1), (1, 0), (1, 1)):
            sent = lax.dynamic_index_in_dim(own_rows, core ^ dc, 0, False)
            pairs = [
                (2 * a + b, 2 * (a ^ dy) + (b ^ dc)) for a in range(2) for b in range(2)
            ]
            here = lax.ppermute(sent, ("y", "core"), pairs)
            result = lax.dynamic_update_index_in_dim(
                result, here, 2 * (y ^ dy) + (core ^ dc), 0
            )
        return result.reshape(length, D)

    def rank_rows(whole):
        return cut_rows(whole, rows * rank, rows)

    smalls = []
    for layer in range(2):
        small, weights[layer]["dt"] = unpack(layer)
        smalls.append(small)
    hidden = whole_sequence(inputs[:, 0])
    grad = whole_sequence(cotangent[:, 0])
    outs, kept = [], []
    for layer in range(2):
        hidden, keep = layer_forward(
            hidden,
            rank_rows(hidden),
            weights[layer],
            smalls[layer],
            then if layer == 0 else lambda *_: None,
            layer == 1,
        )
        outs.append(hidden)
        kept.append(keep)
    tables = rotation_tables(length)
    grads = [None, None]
    smalls_grad, queue, blocks = [None, None], {}, None
    for layer in (1, 0):
        grad, smalls_grad[layer], blocks = layer_backward(
            grad,
            rank_rows(grad).astype(F32),
            kept[layer],
            weights[layer],
            smalls[layer],
            queue,
            layer,
            tables,
            (outs[1],) if layer == 1 else (),
            blocks,
        )
        grads[layer] = grad

    def block_rows(whole):
        blocks = whole.reshape(RANKS, rows, D)
        mine = lax.dynamic_index_in_dim(blocks, 2 * y + core, 0, False)
        sent = lax.dynamic_index_in_dim(blocks, 2 * y + (1 - core), 0, False)
        theirs = flip(sent, "core")
        return jnp.where(core == 0, jnp.stack([mine, theirs]), jnp.stack([theirs, mine]))

    def block_from_ranks(part, section):
        moved = []
        for micro in range(2):
            pairs = [
                (4 * a + 2 * b + micro, 4 * section + 2 * a + b)
                for a in range(2)
                for b in range(2)
            ]
            moved.append(lax.ppermute(part, ("section", "y", "core"), pairs))
        return jnp.stack(moved)

    layer_outputs = jnp.where(s == 0, block_rows(outs[0]), block_from_ranks(outs[1], 1))
    grad_inputs = jnp.where(s == 1, block_rows(grads[1]), block_from_ranks(grads[0], 0))

    down_block, reduce, got_gu = blocks
    extra = pack(smalls_grad, nz)
    extra = extra + flip(extra, "core")
    down_rows = R_FF // nz
    extra_count = extra.shape[1]
    got_in = share(queue["in1"], queue["in0"], 50, (grad_inputs, layer_outputs))
    extra = copy_after(narrow(extra).reshape(-1, HALF), got_in[0]).reshape(extra.shape)
    last = jnp.concatenate([down_block.reshape(nz, down_rows, HALF), extra], axis=1)
    reduce("down0", last.reshape(-1, HALF))
    down0, extra = queue["down0"][:down_rows], queue["down0"][down_rows:]

    place = jnp.stack([y, core]).astype(jnp.int32)
    grad_w_gu = got_gu
    half_rows = queue["outs"].shape[0] // 2
    got_out = share(
        queue["outs"][:half_rows], queue["outs"][half_rows:], 30, (got_in[0],)
    )
    shared = swap(extra).astype(F32)
    grad_w_in, grad_w_qkv = spread_in(place, got_in)
    got_down = share(queue["down1"], down0, 30, (grad_w_in,))
    out_rows, o_rows = R_SSM // nz, R_ATT // nz
    grad_w_out = spread_rows(place, got_out, 0, out_rows, out_rows)
    grad_w_o = spread_rows(place, got_out, out_rows, o_rows, o_rows)
    grad_w_down = spread_rows(place, got_down, 0, down_rows, down_rows)

    width, conv_width, ssm_width = D // nz, CONV_W // nz, D_SSM // nz
    heads_width = SSM_HEADS // nz
    dt_all = jnp.where(s == 0, shared[:, :R_HEADS, :width], shared[:, :R_HEADS, PART : PART + width])
    grad_w_in = with_dt(grad_w_in, dt_all.reshape(SSM_HEADS, width)).T
    small_sum = jnp.sum(shared[:, 16:], axis=0)
    small_sum = jnp.where(s == 0, small_sum[:8], small_sum[8:])
    head_row = small_sum[7, : 3 * LANES].reshape(3, LANES)
    cuts = (
        jnp.stack([small_sum[0, :width], small_sum[0, PART : PART + width]]),
        head_row[:, :heads_width],
        small_sum[1:6, :conv_width],
        small_sum[6:7, :ssm_width],
    )
    return (
        layer_outputs[None, :, None],
        grad_inputs[None, :, None],
        cuts[0][None],
        cuts[1][None],
        cuts[2][None],
        cuts[3],
        grad_w_in[None],
        grad_w_out[None],
        grad_w_qkv[None],
        grad_w_o[None],
        grad_w_gu[None],
        grad_w_down[None],
    )


def solution(mesh):
    CHANNELS.clear()
    sections, ctx, fsdp = mesh.devices.shape
    fine = Mesh(
        mesh.devices.reshape(sections, ctx // 2, 2, fsdp), ("section", "y", "core", "fsdp")
    )
    tokens = ("y", "core")
    in_specs = (
        P(None, "fsdp", tokens, None),
        P(None, "fsdp", tokens, None),
        P("section", None, "fsdp"),
        P("section", None, "fsdp"),
        P("section", None, "fsdp"),
        P("section", "fsdp"),
    ) + (P("section", "fsdp", None),) * 6
    out_specs = (
        P("section", None, "fsdp", tokens, None),
        P("section", None, "fsdp", tokens, None),
        P("section", None, "fsdp"),
        P("section", None, "fsdp"),
        P("section", None, "fsdp"),
        P("section", "fsdp"),
    ) + (P("section", "fsdp", None),) * 6
    return jax.shard_map(body, mesh=fine, in_specs=in_specs, out_specs=out_specs, check_vma=False)
```

```python
import functools

import jax
import jax.numpy as jnp
from jax import lax
from jax.experimental import pallas as pl
from jax.experimental.pallas import tpu as pltpu
from jax.sharding import Mesh
from jax.sharding import PartitionSpec as P

D = 2048
FF = 4096
SSM_HEADS = 48
SSM_HEAD = 64
STATE = 256
Q_HEADS = 8
KV_HEADS = 2
HEAD_DIM = 128
CONV_K = 4
D_SSM = 3072
CONV_W = 3584
D_IN = 6704
ATT = 1024
KV = 256
EPSILON = 1e-05
ROPE_BASE = 10000.0
NEGATIVE = -1e30
HIGHEST = lax.Precision.HIGHEST

RANKS = 4
R_HEADS = SSM_HEADS // RANKS
R_SSM = D_SSM // RANKS
R_BC = 2 * STATE // RANKS
R_CONV = R_SSM + R_BC
R_ATT = ATT // RANKS
R_FF = FF // RANKS
R_OUT = R_SSM + R_ATT
HALF = 1024
PART = HALF // 2
MESH = pl.DeviceIdType.MESH
BF = jnp.bfloat16
F32 = jnp.float32


def rank_place():
    return 2 * lax.axis_index("section") + lax.axis_index("y")


def rank_id(rank):
    return {"section": rank // 2, "y": lax.rem(rank, 2)}


def greet(me):
    barrier = pltpu.get_barrier_semaphore()
    for step in range(1, RANKS):
        pl.semaphore_signal(
            barrier, inc=1, device_id=rank_id(lax.rem(me + step, RANKS)), device_id_type=MESH
        )
    pl.semaphore_wait(barrier, RANKS - 1)


def swap_kernel(with_stat, *refs):
    if with_stat:
        send_ref, stat_ref, out_ref, all_stat_ref, send_sem, recv_sem, stat_send, stat_recv = refs
    else:
        send_ref, out_ref, send_sem, recv_sem = refs
    me = rank_place()
    greet(me)
    copies = []
    for step in range(1, RANKS):
        other = lax.rem(me + step, RANKS)
        copies.append(
            pltpu.make_async_remote_copy(
                src_ref=send_ref.at[other] if len(send_ref.shape) == 3 else send_ref,
                dst_ref=out_ref.at[me],
                send_sem=send_sem.at[step - 1],
                recv_sem=recv_sem.at[step - 1],
                device_id=rank_id(other),
                device_id_type=MESH,
            )
        )
        if with_stat:
            copies.append(
                pltpu.make_async_remote_copy(
                    src_ref=stat_ref,
                    dst_ref=all_stat_ref.at[me],
                    send_sem=stat_send.at[step - 1],
                    recv_sem=stat_recv.at[step - 1],
                    device_id=rank_id(other),
                    device_id_type=MESH,
                )
            )
    for copy in copies:
        copy.start()
    if len(send_ref.shape) == 3:
        out_ref[me] = send_ref[me]
    else:
        out_ref[me] = send_ref[...]
    if with_stat:
        all_stat_ref[me] = stat_ref[...]
    for copy in copies:
        copy.wait()


CHANNELS = {}


def channel(name, *operands):
    key = (name,) + tuple((o.shape, str(o.dtype)) for o in operands)
    return CHANNELS.setdefault(key, len(CHANNELS))


def lasting(us):
    return pl.CostEstimate(flops=0, transcendentals=0, bytes_accessed=int(us * 850000))


VMEM_SPEC = pl.BlockSpec(memory_space=pltpu.VMEM)
ANY_SPEC = pl.BlockSpec(memory_space=pl.ANY)


def ignoring(kernel, used, extra):
    if not extra:
        return kernel
    return lambda *refs: kernel(*refs[:used], *refs[used + extra :])


def swap(values, stat=None, after=()):
    out_shape = [jax.ShapeDtypeStruct((RANKS,) + values.shape[-2:], values.dtype)]
    scratch = [pltpu.SemaphoreType.DMA((RANKS - 1,)), pltpu.SemaphoreType.DMA((RANKS - 1,))]
    args = [values]
    if stat is not None:
        out_shape.append(jax.ShapeDtypeStruct((RANKS,) + stat.shape, stat.dtype))
        scratch += scratch
        args.append(stat)
    out = pl.pallas_call(
        ignoring(functools.partial(swap_kernel, stat is not None), len(args), len(after)),
        out_shape=out_shape,
        in_specs=[VMEM_SPEC] * len(args) + [pl.BlockSpec(memory_space=pl.ANY)] * len(after),
        out_specs=[VMEM_SPEC] * len(out_shape),
        scratch_shapes=scratch,
        cost_estimate=lasting(9),
        compiler_params=pltpu.CompilerParams(
            collective_id=channel("swap", *args, *after),
            has_side_effects=True,
            vmem_limit_bytes=32 * 2**20,
        ),
    )(*args, *after)
    return out if stat is not None else out[0]


def scatter_sum(me, rows, part_ref, slots, send_sem, recv_sem):
    copies = []
    for step in range(1, RANKS):
        other = lax.rem(me + step, RANKS)
        copies.append(
            pltpu.make_async_remote_copy(
                src_ref=part_ref.at[pl.ds(pl.multiple_of(other * rows, rows), rows)],
                dst_ref=slots.at[step - 1],
                send_sem=send_sem.at[step - 1],
                recv_sem=recv_sem.at[step - 1],
                device_id=rank_id(other),
                device_id_type=MESH,
            )
        )
    for copy in copies:
        copy.start()
    total = part_ref[pl.ds(pl.multiple_of(me * rows, rows), rows), :].astype(F32)
    for step, copy in enumerate(copies):
        copy.wait()
        total = total + slots[step].astype(F32)
    return total


def spread(me, rows, out_ref, send_sem, recv_sem):
    here = pl.ds(pl.multiple_of(me * rows, rows), rows)
    copies = []
    for step in range(1, RANKS):
        copies.append(
            pltpu.make_async_remote_copy(
                src_ref=out_ref.at[here],
                dst_ref=out_ref.at[here],
                send_sem=send_sem.at[step - 1],
                recv_sem=recv_sem.at[step - 1],
                device_id=rank_id(lax.rem(me + step, RANKS)),
                device_id_type=MESH,
            )
        )
    for copy in copies:
        copy.start()
    for copy in copies:
        copy.wait()


def mid_kernel(part_ref, resid_ref, gain_ref, mid_ref, out_ref, slots, s1, r1, s2, r2):
    rows = resid_ref.shape[0]
    me = rank_place()
    greet(me)
    mid = scatter_sum(me, rows, part_ref, slots, s1, r1) + resid_ref[...].astype(F32)
    mid_ref[...] = mid
    scale = lax.rsqrt(jnp.mean(mid * mid, axis=-1, keepdims=True) + EPSILON)
    out_ref[pl.ds(pl.multiple_of(me * rows, rows), rows), :] = (
        mid * scale * gain_ref[...].astype(F32)
    ).astype(BF)
    spread(me, rows, out_ref, s2, r2)


def end_rows_kernel(part_ref, resid_ref, out_ref, slots, s1, r1, s2, r2):
    me = rank_place()
    greet(me)
    total = scatter_sum(me, resid_ref.shape[0], part_ref, slots, s1, r1) + resid_ref[...]
    out_ref[...] = total.astype(BF)


def back_rows_kernel(
    part_ref, given_ref, value_ref, gain_ref, out_ref, gain_grad_ref, slots, s1, r1, s2, r2
):
    me = rank_place()
    greet(me)
    grad = scatter_sum(me, given_ref.shape[0], part_ref, slots, s1, r1)
    total, gain_grad_ref[...] = norm_back(grad, value_ref[...], gain_ref[...].astype(F32))
    out_ref[...] = (given_ref[...] + total).astype(BF)


def norm_back(grad, value, gain):
    scale = lax.rsqrt(jnp.mean(value * value, axis=-1, keepdims=True) + EPSILON)
    unit = value * scale
    scaled = grad * gain
    total = scale * (scaled - unit * jnp.mean(scaled * unit, axis=-1, keepdims=True))
    return total, jnp.sum(grad * unit, axis=0, keepdims=True)


def end_kernel(part_ref, resid_ref, out_ref, slots, s1, r1, s2, r2):
    rows = resid_ref.shape[0]
    me = rank_place()
    greet(me)
    total = scatter_sum(me, rows, part_ref, slots, s1, r1) + resid_ref[...]
    out_ref[pl.ds(pl.multiple_of(me * rows, rows), rows), :] = total.astype(BF)
    spread(me, rows, out_ref, s2, r2)


def back_kernel(
    part_ref, given_ref, value_ref, gain_ref, wide_ref, out_ref, gain_grad_ref, slots, s1, r1, s2, r2
):
    rows = given_ref.shape[0]
    me = rank_place()
    greet(me)
    grad = scatter_sum(me, rows, part_ref, slots, s1, r1)
    total, gain_grad_ref[...] = norm_back(grad, value_ref[...], gain_ref[...].astype(F32))
    total = given_ref[...] + total
    wide_ref[...] = total
    out_ref[pl.ds(pl.multiple_of(me * rows, rows), rows), :] = total.astype(BF)
    spread(me, rows, out_ref, s2, r2)


def rank_call(kernel, out_shape, rows, *args, after=()):
    return pl.pallas_call(
        ignoring(kernel, len(args), len(after)),
        out_shape=out_shape,
        in_specs=[VMEM_SPEC] * len(args) + [pl.BlockSpec(memory_space=pl.ANY)] * len(after),
        out_specs=[VMEM_SPEC] * len(out_shape),
        scratch_shapes=[pltpu.VMEM((RANKS - 1, rows, D), BF)]
        + [pltpu.SemaphoreType.DMA((RANKS - 1,))] * 4,
        cost_estimate=lasting(27),
        compiler_params=pltpu.CompilerParams(
            collective_id=channel(kernel.__name__, *args, *after),
            has_side_effects=True,
            vmem_limit_bytes=32 * 2**20,
        ),
    )(*args, *after)


def mid_step(part, resid, gain):
    rows = resid.shape[0]
    return rank_call(
        mid_kernel,
        [jax.ShapeDtypeStruct((rows, D), F32), jax.ShapeDtypeStruct(part.shape, BF)],
        rows,
        part,
        resid,
        gain[None],
    )


def end_step(part, resid):
    rows = resid.shape[0]
    return rank_call(end_kernel, [jax.ShapeDtypeStruct(part.shape, BF)], rows, part, resid)[0]


def end_rows(part, resid):
    shape = jax.ShapeDtypeStruct(resid.shape, BF)
    return rank_call(end_rows_kernel, [shape], resid.shape[0], part, resid)[0]


def back_rows(part, given, value, gain):
    shapes = [jax.ShapeDtypeStruct(given.shape, BF), jax.ShapeDtypeStruct((1, D), F32)]
    return rank_call(back_rows_kernel, shapes, given.shape[0], part, given, value, gain[None])


def back_step(part, given, value, gain, after=()):
    rows = given.shape[0]
    return rank_call(
        back_kernel,
        [
            jax.ShapeDtypeStruct((rows, D), F32),
            jax.ShapeDtypeStruct(part.shape, BF),
            jax.ShapeDtypeStruct((1, D), F32),
        ],
        rows,
        part,
        given,
        value,
        gain[None],
        after=after,
    )


def copy_kernel(value_ref, out_ref):
    out_ref[...] = value_ref[...]


def copy_after(value, *tokens):
    rows, width = value.shape
    tile = min(rows, 128)
    block = pl.BlockSpec((tile, width), lambda i: (i, 0))
    return pl.pallas_call(
        ignoring(copy_kernel, 1, len(tokens)),
        grid=(rows // tile,),
        out_shape=jax.ShapeDtypeStruct(value.shape, value.dtype),
        in_specs=[block] + [ANY_SPEC] * len(tokens),
        out_specs=block,
    )(value, *tokens)


def product_kernel(left_a, left_b, right_a, right_b, out_ref):
    turned = lambda left, right: lax.dot_general(
        left[...], right[...], (((0,), (0,)), ((), ())), preferred_element_type=F32
    )
    out_ref[...] = (turned(left_a, right_a) + turned(left_b, right_b)).astype(BF)


def outer_sum(left, right, tokens):
    rows, width = left[0].shape
    columns_right = right[0].shape[1]
    tile = 256
    left_block = pl.BlockSpec((rows, tile), lambda i: (0, i))
    right_block = pl.BlockSpec((rows, columns_right), lambda i: (0, 0))
    return pl.pallas_call(
        ignoring(product_kernel, 4, len(tokens)),
        grid=(width // tile,),
        out_shape=jax.ShapeDtypeStruct((width, columns_right), BF),
        in_specs=[left_block] * 2 + [right_block] * 2 + [ANY_SPEC] * len(tokens),
        out_specs=pl.BlockSpec((tile, columns_right), lambda i: (i, 0)),
        cost_estimate=lasting(3),
        compiler_params=pltpu.CompilerParams(vmem_limit_bytes=56 * 2**20),
    )(*left, *right, *tokens)


def share_kernel(one_ref, zero_ref, *refs):
    own, own_c, across, across_c, local_sem, send_sem, recv_sem = refs[-7:]
    s, y, core = (lax.axis_index(name) for name in ("section", "y", "core"))
    rows = one_ref.shape[0]
    half = rows // 2
    barrier = pltpu.get_barrier_semaphore()
    ids = {"section": {"section": 1 - s}, "y": {"y": 1 - y}, "core": {"core": 1 - core}}
    for who in ids.values():
        pl.semaphore_signal(barrier, inc=1, device_id=who, device_id_type=MESH)
    pl.semaphore_wait(barrier, 3)

    def remote(k, src, dst, axis):
        return pltpu.make_async_remote_copy(
            src_ref=src, dst_ref=dst, send_sem=send_sem.at[k], recv_sem=recv_sem.at[k],
            device_id=ids[axis], device_id_type=MESH,
        )

    part = lambda ref, k: ref.at[pl.ds(half * k, half)]
    slot = lambda ref, place, k: ref.at[place, pl.ds(half * k, half)]
    for section, mine, sent in ((0, zero_ref, one_ref), (1, one_ref, zero_ref)):

        @pl.when(s == section)
        def _():
            for k in range(2):
                remote(k, part(sent, k), slot(own, section, k), "section").start()
            for k in range(2):
                remote(2 + k, part(mine, k), slot(across, section, k), "y").start()
            remote(6, mine, own_c.at[section], "core").start()
            keep = pltpu.make_async_copy(mine, own.at[section], local_sem)
            keep.start()
            for k in range(2):
                remote(k, part(sent, k), slot(own, 1 - section, k), "section").wait_recv()
                remote(4 + k, slot(own, 1 - section, k), slot(across, 1 - section, k), "y").start()
                remote(
                    7 + k, slot(own, 1 - section, k), slot(own_c, 1 - section, k), "core"
                ).start()
            for k in range(2):
                remote(2 + k, part(mine, k), slot(across, section, k), "y").wait_recv()
                remote(
                    9 + k, slot(across, section, k), slot(across_c, section, k), "core"
                ).start()
            for k in range(2):
                there = slot(across, 1 - section, k)
                remote(4 + k, slot(own, 1 - section, k), there, "y").wait_recv()
                remote(11 + k, there, slot(across_c, 1 - section, k), "core").start()
            remote(6, mine, own_c.at[section], "core").wait_recv()
            for k in range(2):
                there = slot(own_c, 1 - section, k)
                remote(7 + k, slot(own, 1 - section, k), there, "core").wait_recv()
                there = slot(across_c, section, k)
                remote(9 + k, slot(across, section, k), there, "core").wait_recv()
                there = slot(across_c, 1 - section, k)
                remote(11 + k, slot(across, 1 - section, k), there, "core").wait_recv()
            for k in range(2):
                remote(k, part(sent, k), slot(own, section, k), "section").wait_send()
                remote(2 + k, part(mine, k), slot(across, section, k), "y").wait_send()
                there = slot(across, 1 - section, k)
                remote(4 + k, slot(own, 1 - section, k), there, "y").wait_send()
                there = slot(own_c, 1 - section, k)
                remote(7 + k, slot(own, 1 - section, k), there, "core").wait_send()
                there = slot(across_c, section, k)
                remote(9 + k, slot(across, section, k), there, "core").wait_send()
                there = slot(across_c, 1 - section, k)
                remote(11 + k, slot(across, 1 - section, k), there, "core").wait_send()
            remote(6, mine, own_c.at[section], "core").wait_send()
            keep.wait()


def share(one, zero, us, after=()):
    shape = jax.ShapeDtypeStruct((2,) + one.shape, one.dtype)
    return pl.pallas_call(
        ignoring(share_kernel, 2, len(after)),
        out_shape=[shape] * 4,
        in_specs=[ANY_SPEC] * (2 + len(after)),
        out_specs=[ANY_SPEC] * 4,
        scratch_shapes=[
            pltpu.SemaphoreType.DMA,
            pltpu.SemaphoreType.DMA((13,)),
            pltpu.SemaphoreType.DMA((13,)),
        ],
        cost_estimate=lasting(us),
        compiler_params=pltpu.CompilerParams(
            collective_id=channel("share", one, zero, *after), has_side_effects=True
        ),
    )(one, zero, *after)


def chosen(place_ref, refs):
    y, core = place_ref[0], place_ref[1]
    values = [ref[...] for ref in refs]
    found = [[None, None], [None, None]]
    for side in range(2):
        flat = [jnp.where(core == side, values[2 * k], values[2 * k + 1]) for k in range(2)]
        for row in range(2):
            found[row][side] = jnp.where(y == row, flat[0], flat[1])
    return found


def rows_kernel(place_ref, a, b, c, d, out_ref):
    found = chosen(place_ref, (a, b, c, d))
    row = lax.rem(pl.program_id(0), 2)
    for side in range(2):
        value = jnp.where(row == 0, found[0][side][0], found[1][side][0])
        out_ref[:, HALF * side : HALF * (side + 1)] = value.astype(F32)


PLACE_SPEC = pl.BlockSpec(memory_space=pltpu.SMEM)


def spread_rows(place, pieces, first, count, tile):
    steps = count // tile
    block = pl.BlockSpec((1, tile, HALF), lambda r, i: (r // 2, first // tile + i, 0))
    return pl.pallas_call(
        rows_kernel,
        grid=(RANKS, steps),
        out_shape=jax.ShapeDtypeStruct((RANKS * count, D), F32),
        in_specs=[PLACE_SPEC] + [block] * 4,
        out_specs=pl.BlockSpec((tile, D), lambda r, i: (r * steps + i, 0)),
        compiler_params=pltpu.CompilerParams(vmem_limit_bytes=56 * 2**20),
    )(place, *pieces)


def gate_up_kernel(nz, place_ref, a, b, c, d, out_ref):
    found = chosen(place_ref, (a, b, c, d))
    width = R_FF // nz
    for side in range(2):
        for shard in range(nz):
            for rank in range(RANKS):
                start = FF * side + (FF // nz) * shard + width * rank
                out_ref[:, start : start + width] = found[rank % 2][side][
                    rank // 2, :, width * shard : width * (shard + 1)
                ].astype(F32)


def spread_gate_up(place, pieces, nz):
    rows = pieces[0].shape[1]
    tile = min(rows, 128)
    block = pl.BlockSpec((2, tile, HALF), lambda i: (0, i, 0))
    return pl.pallas_call(
        functools.partial(gate_up_kernel, nz),
        grid=(rows // tile,),
        out_shape=jax.ShapeDtypeStruct((rows, 2 * FF), F32),
        in_specs=[PLACE_SPEC] + [block] * 4,
        out_specs=pl.BlockSpec((tile, 2 * FF), lambda i: (i, 0)),
        compiler_params=pltpu.CompilerParams(vmem_limit_bytes=56 * 2**20),
    )(place, *pieces)


def in_kernel(place_ref, a, b, c, d, in_ref, qkv_ref):
    found = chosen(place_ref, (a, b, c, d))
    for rank in range(RANKS):
        left, right = (found[rank % 2][side][rank // 2].astype(F32) for side in range(2))
        in_ref[R_SSM * rank : R_SSM * (rank + 1)] = right[:, :R_SSM].T
        start = D_SSM + R_SSM * rank
        in_ref[start : start + R_SSM] = left[:, :R_SSM].T
        start = 2 * D_SSM + R_BC * rank
        in_ref[start : start + R_BC] = left[:, R_SSM:R_CONV].T
        qkv_ref[:, R_ATT * rank : R_ATT * (rank + 1)] = right[:, R_SSM:]
        start = ATT + KV * (rank % 2) + HEAD_DIM * (rank // 2)
        qkv_ref[:, start : start + HEAD_DIM] = left[:, R_CONV:]


def dt_kernel(whole_ref, dt_ref, out_ref):
    out_ref[...] = dt_ref[...]


def with_dt(whole, dt):
    rows, width = dt.shape
    tile = 16
    first = (whole.shape[0] - rows) // tile
    return pl.pallas_call(
        dt_kernel,
        grid=(rows // tile,),
        out_shape=jax.ShapeDtypeStruct(whole.shape, whole.dtype),
        in_specs=[ANY_SPEC, pl.BlockSpec((tile, width), lambda i: (i, 0))],
        out_specs=pl.BlockSpec((tile, width), lambda i: (first + i, 0)),
        input_output_aliases={0: 0},
    )(whole, dt)


def spread_in(place, pieces):
    rows = pieces[0].shape[1]
    tile = min(rows, 128)
    block = pl.BlockSpec((2, tile, HALF), lambda i: (0, i, 0))
    return pl.pallas_call(
        in_kernel,
        grid=(rows // tile,),
        out_shape=[
            jax.ShapeDtypeStruct((D_IN, rows), F32),
            jax.ShapeDtypeStruct((rows, ATT + 2 * KV), F32),
        ],
        in_specs=[PLACE_SPEC] + [block] * 4,
        out_specs=[
            pl.BlockSpec((D_IN, tile), lambda i: (0, i)),
            pl.BlockSpec((tile, ATT + 2 * KV), lambda i: (i, 0)),
        ],
        compiler_params=pltpu.CompilerParams(vmem_limit_bytes=56 * 2**20),
    )(place, *pieces)


LANES = 128


def turned_lanes(values, cosine, sine):
    parts = []
    for start in range(0, values.shape[1], HEAD_DIM):
        head = values[:, start : start + HEAD_DIM]
        parts.append(head * cosine + pltpu.roll(head, HEAD_DIM // 2, 1) * sine)
    return parts[0] if len(parts) == 1 else jnp.concatenate(parts, axis=1)


def exact(left, right, contract):
    return lax.dot_general(
        left, right, (contract, ((), ())), precision=HIGHEST, preferred_element_type=F32
    )


def mixer_back_kernel(
    nz, got_ref, scan_ref, z_ref, norm_ref, gain_ref, x_ref, b_ref, c_ref, raw_ref, heads_ref,
    run_ref, dt_ref, q_ref, k_ref, v_ref, probs_ref, cos_ref, sin_ref,
    message_ref, right_ref, dx_ref, draw_ref, heads_out_ref, lanes_out_ref,
):
    length = scan_ref.shape[0]
    inner = nz // RANKS
    wide, narrow_w = R_OUT // nz, R_SSM // nz
    d_norm = jnp.concatenate(
        [
            got_ref[r][:, wide * i : wide * i + narrow_w].astype(F32)
            for i in range(inner)
            for r in range(RANKS)
        ],
        axis=1,
    )
    d_o = jnp.concatenate(
        [
            got_ref[r][:, wide * i + narrow_w : wide * (i + 1)].astype(F32)
            for i in range(inner)
            for r in range(RANKS)
        ],
        axis=1,
    ).astype(BF)
    spread_of, overlap = norm_ref[:, 0:1], norm_ref[:, 1:2]
    scan, z = scan_ref[...], z_ref[...]
    sig = jax.nn.sigmoid(z)
    silu = z * sig
    gated = scan * silu
    lanes_out_ref[0:1, :] = jnp.sum(d_norm * gated * spread_of, axis=0, keepdims=True)
    d_gated = spread_of * d_norm * gain_ref[...] - gated * (
        spread_of * spread_of * overlap * (1.0 / D_SSM)
    )
    d_scan = d_gated * silu
    right_ref[:, :R_SSM] = (d_gated * scan * (sig * (1.0 + z * (1.0 - sig)))).astype(BF)

    row = lax.broadcasted_iota(jnp.int32, (length, length), 0)
    column = lax.broadcasted_iota(jnp.int32, (length, length), 1)
    allowed = row >= column

    scale = HEAD_DIM**-0.5
    key, value = k_ref[...], v_ref[...]
    d_key = jnp.zeros((length, HEAD_DIM), F32)
    d_value = jnp.zeros((length, HEAD_DIM), F32)
    for head in range(R_ATT // HEAD_DIM):
        cut = slice(HEAD_DIM * head, HEAD_DIM * (head + 1))
        query, grad, probs = q_ref[:, cut], d_o[:, cut], probs_ref[head]
        d_probs = dot_t(grad, value)
        d_scores = (
            probs * (d_probs - jnp.sum(probs * d_probs, axis=1, keepdims=True))
        ).astype(BF)
        d_query = dot(d_scores, key) * scale
        right_ref[:, R_SSM + HEAD_DIM * head : R_SSM + HEAD_DIM * (head + 1)] = turned_lanes(
            d_query, cos_ref[...], -sin_ref[...]
        ).astype(BF)
        d_key = d_key + t_dot(d_scores, query) * scale
        d_value = d_value + t_dot(probs.astype(BF), grad)

    b_rows, c_rows = b_ref[...], c_ref[...]
    mixing = dot_t(c_rows, b_rows)
    x = x_ref[...]
    lanes_out_ref[1:2, :] = jnp.sum(d_scan * x.astype(F32), axis=0, keepdims=True)
    grad_b = d_scan.astype(BF)
    run_t, dt_t = run_ref[...].T, dt_ref[...].T
    d_mixing = jnp.zeros((length, length), F32)
    lane = lax.broadcasted_iota(jnp.int32, (length, LANES), 1)
    head_row = lax.broadcasted_iota(jnp.int32, (LANES, length), 0)
    by_row = jnp.zeros((length, LANES), F32)
    direct = jnp.zeros((LANES, length), F32)
    for pair in range(R_HEADS // 2):
        cut = slice(LANES * pair, LANES * (pair + 1))
        x_pair, g_pair = x[:, cut], grad_b[:, cut]
        d_pair = []
        for side in range(2):
            head = 2 * pair + side
            mine = (lane < SSM_HEAD) if side == 0 else (lane >= SSM_HEAD)
            d_weights = dot_t(jnp.where(mine, g_pair, jnp.zeros_like(g_pair)), x_pair)
            gap = run_ref[:, head : head + 1] - run_t[head : head + 1, :]
            table = jnp.exp(jnp.where(allowed, gap, NEGATIVE))
            dt_row = dt_t[head : head + 1, :]
            faded = d_weights * table
            faded_dt = faded * dt_row
            d_mixing = d_mixing + faded_dt
            plain = faded * mixing
            direct = jnp.where(head_row == head, jnp.sum(plain, axis=0, keepdims=True), direct)
            by_row = jnp.where(
                lane == head, jnp.sum(faded_dt * mixing, axis=1, keepdims=True), by_row
            )
            weights = (table * mixing * dt_row).astype(BF)
            d_pair.append(t_dot(weights, g_pair))
        skip = jnp.where(
            lane[:1] < SSM_HEAD,
            heads_ref[2:3, 2 * pair : 2 * pair + 1],
            heads_ref[2:3, 2 * pair + 1 : 2 * pair + 2],
        )
        dx_ref[:, cut] = jnp.where(lane < SSM_HEAD, d_pair[0], d_pair[1]) + skip * d_scan[:, cut]
    d_mixing = d_mixing.astype(BF)
    d_c = dot(d_mixing, b_rows)
    d_b = t_dot(d_mixing, c_rows)
    for r in range(RANKS):
        source = d_b if r < 2 else d_c
        start = R_BC * (r % 2)
        message_ref[r, :, :R_BC] = source[:, start : start + R_BC].astype(BF)
        message_ref[r, :, R_BC:] = (d_key if r % 2 == 0 else d_value).astype(BF)

    later = (column >= row).astype(F32)
    from_rows_sum = exact(later, by_row, ((1,), (0,)))
    grad_step = from_rows_sum - exact(later, direct * dt_t, ((1,), (1,)))
    grad_dt = direct.T
    bias, log = heads_ref[0:1, :], heads_ref[1:2, :]
    raw = raw_ref[...] + bias
    rate = jnp.exp(log)
    step = -jax.nn.softplus(raw) * rate
    valid = lane < R_HEADS
    grad_dt = grad_dt - grad_step * rate
    grad_raw = jnp.where(valid, grad_dt * jax.nn.sigmoid(raw), 0.0)
    draw_ref[...] = grad_raw.astype(BF)
    heads_out_ref[0:1, :] = jnp.sum(grad_raw, axis=0, keepdims=True)
    heads_out_ref[1:2, :] = jnp.sum(grad_step * step, axis=0, keepdims=True)


def whole_block(array):
    shape = array.shape
    return pl.BlockSpec(shape, lambda i: (0,) * len(shape), pipeline_mode=pl.Buffered(1))


def mixer_back(got, kept, small, overlap, tables):
    length = got.shape[1]
    nz = lax.axis_size("fsdp")
    norm = jnp.stack([kept["spread"], overlap], axis=1)
    shape = jax.ShapeDtypeStruct
    out_shape = [
        shape((RANKS, length, 2 * R_BC), BF),
        shape((length, HALF), BF),
        shape((length, R_SSM), F32),
        shape((length, LANES), BF),
        shape((8, LANES), F32),
        shape((8, R_SSM), F32),
    ]
    args = (
        got, kept["scan"], kept["z"], norm, small["ssm_gain"][None], kept["u"][:, :R_SSM],
        kept["b"], kept["c"], kept["dt_raw"], small["heads"], kept["running"], kept["dt"],
        kept["query"], kept["key"], kept["value"],
        kept["probs"], *tables,
    )
    return pl.pallas_call(
        functools.partial(mixer_back_kernel, nz),
        grid=(1,),
        out_shape=out_shape,
        in_specs=[whole_block(arg) for arg in args],
        out_specs=[whole_block(out) for out in out_shape],
        cost_estimate=lasting(16),
        compiler_params=pltpu.CompilerParams(vmem_limit_bytes=56 * 2**20),
    )(*args)


def conv_back_kernel(
    place_ref, back_ref, dx_ref, xbc_ref, table_ref, cos_ref, sin_ref, left_ref, conv_ref
):
    y, s = place_ref[0], place_ref[1]
    length = dx_ref.shape[0]
    back = [back_ref[r].astype(F32) for r in range(RANKS)]
    d_bc = (back[0] + back[1] + back[2] + back[3])[:, :R_BC]
    d_kv = jnp.where(s == 0, back[0] + back[1], back[2] + back[3])[:, R_BC:]
    d_kv = jnp.where(y == 0, turned_lanes(d_kv, cos_ref[...], -sin_ref[...]), d_kv)
    left_ref[:, R_CONV:] = d_kv.astype(BF)
    d_u = jnp.concatenate([dx_ref[...], d_bc], axis=1)
    wide = xbc_ref[...].astype(F32)
    place = lax.broadcasted_iota(jnp.int32, (length, R_CONV), 0)
    moved = []
    before = table_ref[CONV_K : CONV_K + 1, :] + jnp.zeros_like(wide)
    for tap in range(CONV_K):
        steps = CONV_K - 1 - tap
        value = wide
        if steps:
            value = jnp.where(place >= steps, pltpu.roll(wide, steps, 0), 0.0)
        moved.append(value)
        before = before + table_ref[tap : tap + 1, :] * value
    sig = jax.nn.sigmoid(before)
    d_before = d_u * (sig * (1.0 + before * (1.0 - sig)))
    d_xbc = jnp.zeros_like(wide)
    for tap in range(CONV_K):
        conv_ref[tap : tap + 1, :] = jnp.sum(d_before * moved[tap], axis=0, keepdims=True)
        steps = CONV_K - 1 - tap
        value = d_before
        if steps:
            value = jnp.where(
                place < length - steps, pltpu.roll(d_before, length - steps, 0), 0.0
            )
        d_xbc = d_xbc + table_ref[tap : tap + 1, :] * value
    conv_ref[CONV_K : CONV_K + 1, :] = jnp.sum(d_before, axis=0, keepdims=True)
    left_ref[:, :R_CONV] = d_xbc.astype(BF)


def conv_back(back, d_x, xbc, table, tables):
    length = d_x.shape[0]
    place = jnp.stack([lax.axis_index("y"), lax.axis_index("section")]).astype(jnp.int32)
    args = (back, d_x, xbc, table, *tables)
    out_shape = [
        jax.ShapeDtypeStruct((length, HALF), BF),
        jax.ShapeDtypeStruct((8, R_CONV), F32),
    ]
    return pl.pallas_call(
        conv_back_kernel,
        grid=(1,),
        out_shape=out_shape,
        in_specs=[PLACE_SPEC] + [whole_block(arg) for arg in args],
        out_specs=[whole_block(out) for out in out_shape],
        cost_estimate=lasting(7),
        compiler_params=pltpu.CompilerParams(vmem_limit_bytes=56 * 2**20),
    )(place, *args)


EXTRA = 32


def pack_kernel(nz, *refs):
    out_ref, conv_full, ssm_full = refs[-3:]
    rank = rank_place()
    out_ref[...] = jnp.zeros_like(out_ref)
    width, conv_width, ssm_width = D // nz, CONV_W // nz, D_SSM // nz
    heads_width, inner = SSM_HEADS // nz, nz // RANKS
    head_of = lax.broadcasted_iota(jnp.int32, (R_SSM, LANES), 0) // SSM_HEAD
    lane = lax.broadcasted_iota(jnp.int32, (R_SSM, LANES), 1)
    to_heads = (head_of == lane).astype(F32)
    for layer in range(2):
        heads_ref, lanes_ref, conv_ref, gain0_ref, gain1_ref, dt_ref = refs[6 * layer : 6 * layer + 6]
        conv_full[...] = jnp.zeros_like(conv_full)
        ssm_full[...] = jnp.zeros_like(ssm_full)
        at = lambda start, size: pl.ds(pl.multiple_of(start, LANES), size)
        conv_full[:, at(R_SSM * rank, R_SSM)] = conv_ref[:, :R_SSM]
        conv_full[:, at(D_SSM + R_BC * rank, R_BC)] = conv_ref[:, R_SSM:]
        ssm_full[:, at(R_SSM * rank, R_SSM)] = lanes_ref[...]
        skip = exact(lanes_ref[...], to_heads, ((1,), (0,)))[1:2]
        heads = (heads_ref[0:1], heads_ref[1:2], skip)
        row = 16 + 8 * layer
        for z in range(nz):
            cut = slice(width * z, width * (z + 1))
            out_ref[z, 0:16, PART * layer : PART * layer + width] = dt_ref[:, cut]
            out_ref[z, row : row + 1, 0:width] = gain0_ref[:, cut]
            out_ref[z, row : row + 1, PART : PART + width] = gain1_ref[:, cut]
            out_ref[z, row + 1 : row + 6, 0:conv_width] = conv_full[
                0 : CONV_K + 1, conv_width * z : conv_width * (z + 1)
            ]
            out_ref[z, row + 6 : row + 7, 0:ssm_width] = ssm_full[
                0:1, ssm_width * z : ssm_width * (z + 1)
            ]
            start = heads_width * (z % inner)
            for k in range(3):
                value = jnp.where(rank == z // inner, heads[k], 0.0)
                out_ref[z, row + 7 : row + 8, LANES * k : LANES * k + heads_width] = value[
                    :, start : start + heads_width
                ]


def pack(layers, nz):
    args = [array for layer in layers for array in layer]
    out = jax.ShapeDtypeStruct((nz, EXTRA, HALF), F32)
    return pl.pallas_call(
        functools.partial(pack_kernel, nz),
        grid=(1,),
        out_shape=out,
        in_specs=[whole_block(arg) for arg in args],
        out_specs=whole_block(out),
        scratch_shapes=[pltpu.VMEM((8, CONV_W), F32), pltpu.VMEM((8, D_SSM), F32)],
        cost_estimate=lasting(4),
        compiler_params=pltpu.CompilerParams(vmem_limit_bytes=40 * 2**20),
    )(*args)


def rotation_tables(length):
    half = HEAD_DIM // 2
    frequency = ROPE_BASE ** (-jnp.arange(half, dtype=F32) / half)
    angles = jnp.arange(length, dtype=F32)[:, None] * frequency[None, :]
    cosine, sine = jnp.cos(angles), jnp.sin(angles)
    return jnp.concatenate([cosine, cosine], 1), jnp.concatenate([-sine, sine], 1)


def narrow(values):
    return values.astype(BF)


def dot(left, right):
    return jnp.dot(left, right, preferred_element_type=F32)


def dot_t(left, right):
    return lax.dot_general(left, right, (((1,), (1,)), ((), ())), preferred_element_type=F32)


def t_dot(left, right):
    return lax.dot_general(left, right, (((0,), (0,)), ((), ())), preferred_element_type=F32)


def columns(array, start, width):
    return lax.dynamic_slice_in_dim(array, start, width, axis=1)


def cut_rows(array, start, width):
    return lax.dynamic_slice_in_dim(array, start, width, axis=0)


def rms(values, gain):
    return values * lax.rsqrt(jnp.mean(values * values, axis=-1, keepdims=True) + EPSILON) * gain


def rotary(values, turning):
    length, width = values.shape
    half = HEAD_DIM // 2
    frequency = ROPE_BASE ** (-jnp.arange(half, dtype=F32) / half)
    angles = jnp.arange(length, dtype=F32)[:, None] * frequency[None, :]
    cosine = jnp.cos(angles)[:, None, :]
    sine = turning * jnp.sin(angles)[:, None, :]
    halves = values.reshape(length, width // HEAD_DIM, 2, half)
    first, second = halves[:, :, 0], halves[:, :, 1]
    return jnp.stack(
        [first * cosine - second * sine, second * cosine + first * sine], axis=2
    ).reshape(length, width)


def causal(length):
    position = jnp.arange(length)
    return position[:, None] >= position[None, :]


def shifted(values, steps):
    if steps == 0:
        return values
    blank = jnp.zeros((abs(steps), values.shape[1]), values.dtype)
    if steps > 0:
        return jnp.concatenate([blank, values[:-steps]], axis=0)
    return jnp.concatenate([values[-steps:], blank], axis=0)


def conv_sum(rows, table):
    wide = rows.astype(F32)
    total = table[CONV_K][None, :]
    for tap in range(CONV_K):
        total = total + table[tap][None, :] * shifted(wide, CONV_K - 1 - tap)
    return total


def decays(dt_raw, heads):
    dt = jax.nn.softplus(dt_raw + heads[0][None, :])
    step = -dt * jnp.exp(heads[1])[None, :]
    length = dt.shape[0]
    running = jnp.dot(causal(length).astype(F32), step, precision=HIGHEST)
    return dt, step, running


def decay_table(running):
    length = running.shape[0]
    turned = running.T
    gap = turned[:, :, None] - turned[:, None, :]
    return jnp.exp(jnp.where(causal(length)[None], gap, NEGATIVE))


def by_head(values):
    return values.reshape(values.shape[0], R_HEADS, SSM_HEAD)


def scan_forward(x, b_rows, c_rows, dt_raw, heads):
    dt, _, running = decays(dt_raw, heads)
    mixing = dot_t(c_rows, b_rows)
    weights = narrow(decay_table(running[:, :R_HEADS]) * mixing[None] * dt.T[:R_HEADS, None, :])
    x_heads = by_head(x)
    result = jnp.einsum("hts,shp->thp", weights, x_heads, preferred_element_type=F32)
    result = result + heads[2][None, :R_HEADS, None] * x_heads.astype(F32)
    return result.reshape(x.shape), running, dt


def scan_backward(x, b_rows, c_rows, dt_raw, heads, grad_y):
    dt, step, running = decays(dt_raw, heads)
    length = x.shape[0]
    mixing = dot_t(c_rows, b_rows)
    table = decay_table(running)
    dt_t = dt.T
    x_heads = by_head(x)
    grad_heads = by_head(narrow(grad_y))
    grad_weights = jnp.einsum("thp,shp->hts", grad_heads, x_heads, preferred_element_type=F32)
    faded = grad_weights * table
    weights = table * mixing[None] * dt_t[:, None, :]
    grad_x = jnp.einsum("hts,thp->shp", narrow(weights), grad_heads, preferred_element_type=F32)
    grad_y_heads = by_head(grad_y)
    grad_x = grad_x + heads[2][None, :, None] * grad_y_heads
    grad_skip = jnp.sum(grad_y_heads * x_heads.astype(F32), axis=(0, 2))
    grad_mixing = narrow(jnp.sum(faded * dt_t[:, None, :], axis=0))
    grad_c = dot(grad_mixing, b_rows)
    grad_b = t_dot(grad_mixing, c_rows)
    plain = faded * mixing[None]
    grad_dt = jnp.sum(plain, axis=1)
    grad_gap = plain * dt_t[:, None, :]
    grad_running = jnp.sum(grad_gap, axis=2) - jnp.sum(grad_gap, axis=1)
    grad_step = jnp.dot(grad_running, causal(length).astype(F32), precision=HIGHEST).T
    grad_dt = grad_dt.T - grad_step * jnp.exp(heads[1])[None, :]
    grad_log = jnp.sum(grad_step * step, axis=0)
    grad_raw = grad_dt * jax.nn.sigmoid(dt_raw + heads[0][None, :])
    grad_table = jnp.stack([jnp.sum(grad_raw, axis=0), grad_log, grad_skip])
    return grad_x.reshape(x.shape), grad_b, grad_c, grad_raw, grad_table


def attend(query, key, value):
    length = query.shape[0]
    heads = query.reshape(length, -1, HEAD_DIM)
    scores = jnp.einsum("qhd,sd->hqs", heads, key, preferred_element_type=F32) * HEAD_DIM**-0.5
    scores = jnp.where(causal(length)[None], scores, NEGATIVE)
    weights = jnp.exp(scores - jnp.max(scores, axis=-1, keepdims=True))
    probs = weights / jnp.sum(weights, axis=-1, keepdims=True)
    mixed = jnp.einsum("hqs,sd->qhd", narrow(probs), value, preferred_element_type=F32)
    return narrow(mixed.reshape(query.shape)), probs


def attend_back(query, key, value, probs, grad_out):
    length = query.shape[0]
    heads = query.reshape(length, -1, HEAD_DIM)
    grad_heads = grad_out.reshape(length, -1, HEAD_DIM)
    grad_probs = jnp.einsum("qhd,sd->hqs", grad_heads, value, preferred_element_type=F32)
    grad_scores = narrow(
        probs * (grad_probs - jnp.sum(probs * grad_probs, axis=-1, keepdims=True))
    )
    scale = HEAD_DIM**-0.5
    grad_query = jnp.einsum("hqs,sd->qhd", grad_scores, key, preferred_element_type=F32) * scale
    grad_key = jnp.einsum("hqs,qhd->sd", grad_scores, heads, preferred_element_type=F32) * scale
    grad_value = jnp.einsum("hqs,qhd->sd", narrow(probs), grad_heads, preferred_element_type=F32)
    return grad_query.reshape(query.shape), grad_key, grad_value


def flip(value, axis):
    return lax.ppermute(value, axis, [(0, 1), (1, 0)])


def layer_forward(entering, resid, weights, small, then, last):
    s, y = lax.axis_index("section"), lax.axis_index("y")
    length = entering.shape[0]
    x1 = narrow(rms(entering.astype(F32), small["gain0"][None, :]))
    left = dot(x1, weights["in"][0])
    right = dot(x1, weights["in"][1])
    dt_raw = dot(x1, weights["dt"])
    xbc = narrow(left[:, :R_CONV])
    u = narrow(jax.nn.silu(conv_sum(xbc, small["conv"])))
    kv_raw = left[:, R_CONV:]
    kv = narrow(jnp.where(y == 0, rotary(kv_raw, 1.0), kv_raw))
    shared = swap(jnp.concatenate([u[:, R_SSM:], kv], axis=1))
    then("swap", shared)
    b_rows = jnp.concatenate([shared[0, :, :R_BC], shared[1, :, :R_BC]], axis=1)
    c_rows = jnp.concatenate([shared[2, :, :R_BC], shared[3, :, :R_BC]], axis=1)
    pair = lax.dynamic_slice_in_dim(shared, 2 * s, 2, axis=0)[:, :, R_BC:]
    key, value = pair[0], pair[1]
    z = right[:, :R_SSM]
    query = narrow(rotary(right[:, R_SSM:], 1.0))
    o, probs = attend(query, key, value)
    x = u[:, :R_SSM]
    scan, running, dt = scan_forward(x, b_rows, c_rows, dt_raw, small["heads"])
    gated = scan * jax.nn.silu(z)
    squares = jnp.sum(gated * gated, axis=1)
    scaled = narrow(gated * small["ssm_gain"][None, :])
    message = to_rows(scaled, o)
    stat = jnp.broadcast_to(squares[None, :], (8, length))
    got, stats = swap(message, stat)
    spread_of = lax.rsqrt(jnp.sum(stats[:, 0, :], axis=0) / D_SSM + EPSILON)
    wide = jnp.transpose(got, (1, 0, 2)).reshape(length, R_OUT)
    is_ssm = small["is_ssm"][None, :]
    mo = narrow(jnp.where(is_ssm, wide.astype(F32) * spread_of[:, None], wide.astype(F32)))
    part = jnp.concatenate([dot(mo, weights["out"][0]), dot(mo, weights["out"][1])], axis=1)
    mid, x2 = mid_step(narrow(part), resid, small["gain1"])
    then("mid", mid)
    gate = dot(x2, weights["gu"][0])
    up = dot(x2, weights["gu"][1])
    act = narrow(jax.nn.silu(gate) * up)
    part2 = jnp.concatenate([dot(act, weights["down"][0]), dot(act, weights["down"][1])], axis=1)
    leaving = (end_rows if last else end_step)(narrow(part2), mid)
    kept = dict(
        resid=resid, x1=x1, xbc=xbc, u=u, b=b_rows, c=c_rows, key=key, value=value, query=query,
        probs=probs, z=z, dt_raw=dt_raw, scan=scan, spread=spread_of, mo=mo, mid=mid, x2=x2,
        gate=gate, up=up, act=act, running=running, dt=dt,
    )
    return leaving, kept


def to_rows(ssm_part, att_part):
    length = ssm_part.shape[0]
    nz = lax.axis_size("fsdp")
    inner = nz // RANKS
    a = ssm_part.reshape(length, inner, RANKS, R_SSM // nz)
    b = att_part.reshape(length, inner, RANKS, R_ATT // nz)
    both = jnp.concatenate([a, b], axis=3)
    return jnp.transpose(both, (2, 0, 1, 3)).reshape(RANKS, length, R_OUT // RANKS)


def from_rows(got):
    length = got.shape[1]
    nz = lax.axis_size("fsdp")
    inner = nz // RANKS
    both = jnp.transpose(got.reshape(RANKS, length, inner, R_OUT // nz), (1, 2, 0, 3))
    a = both[..., : R_SSM // nz].reshape(length, R_SSM)
    b = both[..., R_SSM // nz :].reshape(length, R_ATT)
    return a, b


def layer_backward(grad, given, kept, weights, small, queue, layer, tables, first=(), earlier=None):
    s, y = lax.axis_index("section"), lax.axis_index("y")
    core = lax.axis_index("core")
    length = grad.shape[0]
    down, gu, out, win = weights["down"], weights["gu"], weights["out"], weights["in"]

    def product(left, right, *tokens):
        mine = jnp.where(core == 0, right[0], right[1])
        theirs = jnp.where(core == 0, right[1], right[0])
        return outer_sum((left, flip(left, "core")), (mine, flip(theirs, "core")), tokens)

    def reduce(name, block):
        nonlocal queue
        if queue:
            block, queue["last"] = lax.optimization_barrier((block, queue["last"]))
        queue[name] = queue["last"] = lax.psum_scatter(
            block, "fsdp", scatter_dimension=0, tiled=True
        )

    def due(point):
        return [queue[k] for k in WAITS[layer].get(point, ())]

    halves = lambda v: (v[:, :HALF], v[:, HALF:])
    g0, g1 = halves(grad)
    down_block = None
    if layer == 1:
        reduce("down1", product(kept["act"], (g0, g1)))
    grad_act = dot_t(g0, down[0]) + dot_t(g1, down[1])
    gate, up = kept["gate"], kept["up"]
    sig = jax.nn.sigmoid(gate)
    d_gate = narrow(grad_act * up * (sig * (1.0 + gate * (1.0 - sig))))
    d_up = narrow(grad_act * gate * sig)
    part = dot_t(d_gate, gu[0]) + dot_t(d_up, gu[1])
    if layer == 1:
        reduce("gu1", product(kept["x2"], (d_gate, d_up), *first))
    d_mid, db, grad_gain1 = back_step(
        narrow(part), given, kept["mid"], small["gain1"], due("mlp") + list(first)
    )
    if layer == 0:
        reduce("gu0", product(kept["x2"], (d_gate, d_up), db))
    b0, b1 = halves(db)
    if layer == 0:
        down_block = product(kept["act"], (g0, g1), db)
    d_mo = dot_t(b0, out[0]) + dot_t(b1, out[1])
    mo = kept["mo"]
    is_ssm = small["is_ssm"][None, :]
    stat_row = jnp.sum(jnp.where(is_ssm, d_mo * mo.astype(F32), 0.0), axis=1)
    stat = jnp.broadcast_to(stat_row[None, :], (8, length))
    blocks = jnp.transpose(narrow(d_mo).reshape(length, RANKS, R_OUT // RANKS), (1, 0, 2))
    got, stats = swap(blocks, stat, due("norm"))
    overlap = jnp.sum(stats[:, 0, :], axis=0)
    message, d_right, d_x, d_raw, head_sums, lane_sums = mixer_back(
        got, kept, small, overlap, tables
    )
    out_block = product(kept["mo"], (b0, b1), message) if layer == 1 else None
    back = swap(message, None, due("scan"))
    d_left, grad_conv = conv_back(back, d_x, kept["xbc"], small["conv"], tables)
    part = dot_t(d_left, win[0]) + dot_t(d_right, win[1]) + dot_t(d_raw, weights["dt"])
    part = narrow(part)
    if layer == 1:
        reduce("in1", product(kept["x1"], (d_left, d_right), part))
    enter = (part, d_mid, kept["resid"].astype(F32), small["gain0"])
    if layer == 0:
        entering_grad, grad_gain0 = back_rows(*enter)
        reduce("in0", product(kept["x1"], (d_left, d_right), entering_grad))
    else:
        _, entering_grad, grad_gain0 = back_step(*enter, due("in"))
    got_gu = None
    if layer == 0:
        got_gu = share(queue["gu1"], queue["gu0"], 50, (entering_grad,))
        place = jnp.stack([y, core]).astype(jnp.int32)
        got_gu = spread_gate_up(place, got_gu, lax.axis_size("fsdp"))
        nz = lax.axis_size("fsdp")
        out_block = product(kept["mo"], (b0, b1), got_gu, down_block)
        both = [block.reshape(nz, -1, HALF) for block in (earlier, out_block)]
        reduce("outs", jnp.concatenate(both, axis=1).reshape(-1, HALF))
    grad_dt_w = t_dot(d_raw[:, :16], kept["x1"])
    smalls_grad = (head_sums, lane_sums, grad_conv, grad_gain0, grad_gain1, grad_dt_w)
    return entering_grad, smalls_grad, (
        out_block if layer == 1 else (down_block, reduce, got_gu)
    )


WAITS = (
    {"scan": ("in1",)},
    {"norm": ("down1",), "in": ("gu1",)},
)


def body(
    inputs, cotangent, norm_gains, head_params, conv_params, ssm_gain,
    w_in, w_out, w_qkv, w_o, w_gu, w_down,
):
    s, y = lax.axis_index("section"), lax.axis_index("y")
    core = lax.axis_index("core")
    nz = lax.axis_size("fsdp")
    z_place = lax.axis_index("fsdp")
    rank = 2 * s + y
    rows = inputs.shape[2]
    length = RANKS * rows
    w_in, w_out, w_qkv, w_o, w_gu, w_down = (
        w[0] for w in (w_in, w_out, w_qkv, w_o, w_gu, w_down)
    )

    flat = jnp.concatenate(
        [
            norm_gains[0].reshape(-1),
            head_params[0].reshape(-1),
            conv_params[0].reshape(-1),
            ssm_gain[0],
            w_in[:, D_SSM + CONV_W :].reshape(-1),
        ]
    )
    count = flat.shape[0]
    flat = jnp.pad(flat, (0, -count % 2048)).reshape(-1, 128)
    everything = lax.all_gather(flat, "fsdp", axis=0)
    beyond = flip(everything, "section")
    both = jnp.where(s == 0, jnp.stack([everything, beyond]), jnp.stack([beyond, everything]))
    both = both.reshape(2, nz, -1)[..., :count]

    def unpack(layer):
        part = both[layer]
        sizes = [2 * D // nz, 3 * SSM_HEADS // nz, 5 * CONV_W // nz, D_SSM // nz]
        starts = [0]
        for size in sizes:
            starts.append(starts[-1] + size)
        join = lambda k, lead: jnp.transpose(
            part[:, starts[k] : starts[k + 1]].reshape(nz, lead, -1), (1, 0, 2)
        ).reshape(lead, -1).astype(F32)
        gains, heads, conv, gain = join(0, 2), join(1, 3), join(2, 5), join(3, 1)[0]
        conv_own = jnp.concatenate(
            [columns(conv, R_SSM * rank, R_SSM), columns(conv, D_SSM + R_BC * rank, R_BC)], axis=1
        )
        channel = jnp.arange(R_OUT) % (R_OUT // nz)
        small = dict(
            gain0=gains[0],
            gain1=gains[1],
            heads=jnp.pad(
                columns(heads, R_HEADS * rank, R_HEADS), ((0, 0), (0, LANES - R_HEADS))
            ),
            conv=conv_own,
            ssm_gain=lax.dynamic_slice_in_dim(gain, R_SSM * rank, R_SSM),
            is_ssm=channel < R_SSM // nz,
        )
        dt_w = columns(part[:, starts[4] :].reshape(D, SSM_HEADS), R_HEADS * rank, R_HEADS)
        return small, jnp.pad(dt_w, ((0, 0), (0, LANES - R_HEADS)))

    def pieces(section):
        rk = 2 * section + y
        first = columns(w_in, jnp.where(core == 0, D_SSM, 0) + R_SSM * rk, R_SSM)
        second = jnp.where(
            core == 0,
            columns(w_in, 2 * D_SSM + R_BC * rk, R_BC),
            columns(w_qkv, R_ATT * rk, HEAD_DIM),
        )
        third = columns(
            w_qkv,
            jnp.where(core == 0, ATT + KV * y + HEAD_DIM * section, R_ATT * rk + HEAD_DIM),
            HEAD_DIM,
        )
        side = HALF * core
        out_rows, o_rows, down_rows = R_SSM // nz, R_ATT // nz, R_FF // nz
        ff = R_FF // nz
        return {
            "in": jnp.concatenate([first, second, third], axis=1),
            "out": jnp.concatenate(
                [
                    lax.dynamic_slice(w_out, (out_rows * rk, side), (out_rows, HALF)),
                    lax.dynamic_slice(w_o, (o_rows * rk, side), (o_rows, HALF)),
                ],
                axis=0,
            ),
            "gu": jnp.concatenate(
                [
                    columns(w_gu, FF * core + (FF // nz) * k + ff * rk, ff) for k in range(nz)
                ],
                axis=1,
            ),
            "down": lax.dynamic_slice(w_down, (down_rows * rk, side), (down_rows, HALF)),
        }

    order = []

    def in_turn(value):
        if order:
            value, order[-1] = lax.optimization_barrier((value, order[-1]))
        return value

    def gather(piece):
        order.append(lax.all_gather(in_turn(piece), ("core", "fsdp"), axis=0))
        return order[-1]

    own, other = pieces(s), pieces(1 - s)
    out_own = gather(own["out"])
    mlp = lambda found: jnp.concatenate([found["gu"], found["down"]], axis=0)
    in_arrived = flip(other["in"], "section")
    out_sent, in_arrived = lax.optimization_barrier((other["out"], in_arrived))
    out_arrived = flip(out_sent, "section")
    mlp_own = mlp(own)
    mlp_sent, out_arrived = lax.optimization_barrier((mlp(other), out_arrived))
    mlp_arrived = flip(mlp_sent, "section")
    of_layer = lambda layer, mine, theirs: jnp.where(s == layer, mine, theirs)
    flat_rows = lambda whole: whole.reshape(2, -1, HALF)
    in0 = gather(copy_after(of_layer(0, own["in"], in_arrived), everything, out_own))
    wide = own["gu"].shape[0]
    mlp0, mlp1 = (of_layer(layer, mlp_own, mlp_arrived) for layer in range(2))

    def together(token, *parts):
        whole = gather(copy_after(jnp.concatenate(parts, axis=0), token))
        whole = whole.reshape(2, nz, -1, HALF)
        found, at = [], 0
        for part in parts:
            found.append(flat_rows(whole[:, :, at : at + part.shape[0]]))
            at += part.shape[0]
        return found

    out_other, gu0, down0 = together(in0, out_arrived, mlp0[:wide], mlp0[wide:])
    weights = [
        dict(out=of_layer(layer, flat_rows(out_own), out_other)) for layer in range(2)
    ]
    weights[0].update({"in": flat_rows(in0), "gu": gu0, "down": down0})

    def then(point, token):
        if point == "swap":
            piece = of_layer(1, own["in"], in_arrived)
            weights[1]["in"] = flat_rows(gather(copy_after(piece, token)))
        elif point == "mid":
            weights[1]["gu"], weights[1]["down"] = together(token, mlp1[:wide], mlp1[wide:])

    def whole_sequence(own_rows):
        place = 2 * y + core
        result = jnp.zeros((RANKS, rows, D), BF)
        result = lax.dynamic_update_index_in_dim(
            result, lax.dynamic_index_in_dim(own_rows, core, 0, False), place, 0
        )
        for dy, dc in ((0, 1), (1, 0), (1, 1)):
            sent = lax.dynamic_index_in_dim(own_rows, core ^ dc, 0, False)
            pairs = [
                (2 * a + b, 2 * (a ^ dy) + (b ^ dc)) for a in range(2) for b in range(2)
            ]
            here = lax.ppermute(sent, ("y", "core"), pairs)
            result = lax.dynamic_update_index_in_dim(
                result, here, 2 * (y ^ dy) + (core ^ dc), 0
            )
        return result.reshape(length, D)

    def rank_rows(whole):
        return cut_rows(whole, rows * rank, rows)

    smalls = []
    for layer in range(2):
        small, weights[layer]["dt"] = unpack(layer)
        smalls.append(small)
    hidden = whole_sequence(inputs[:, 0])
    grad = whole_sequence(cotangent[:, 0])
    outs, kept = [], []
    for layer in range(2):
        hidden, keep = layer_forward(
            hidden,
            rank_rows(hidden),
            weights[layer],
            smalls[layer],
            then if layer == 0 else lambda *_: None,
            layer == 1,
        )
        outs.append(hidden)
        kept.append(keep)
    tables = rotation_tables(length)
    grads = [None, None]
    smalls_grad, queue, blocks = [None, None], {}, None
    for layer in (1, 0):
        grad, smalls_grad[layer], blocks = layer_backward(
            grad,
            rank_rows(grad).astype(F32),
            kept[layer],
            weights[layer],
            smalls[layer],
            queue,
            layer,
            tables,
            (outs[1],) if layer == 1 else (),
            blocks,
        )
        grads[layer] = grad

    def block_rows(whole):
        blocks = whole.reshape(RANKS, rows, D)
        mine = lax.dynamic_index_in_dim(blocks, 2 * y + core, 0, False)
        sent = lax.dynamic_index_in_dim(blocks, 2 * y + (1 - core), 0, False)
        theirs = flip(sent, "core")
        return jnp.where(core == 0, jnp.stack([mine, theirs]), jnp.stack([theirs, mine]))

    def block_from_ranks(part, section):
        moved = []
        for micro in range(2):
            pairs = [
                (4 * a + 2 * b + micro, 4 * section + 2 * a + b)
                for a in range(2)
                for b in range(2)
            ]
            moved.append(lax.ppermute(part, ("section", "y", "core"), pairs))
        return jnp.stack(moved)

    layer_outputs = jnp.where(s == 0, block_rows(outs[0]), block_from_ranks(outs[1], 1))
    grad_inputs = jnp.where(s == 1, block_rows(grads[1]), block_from_ranks(grads[0], 0))

    down_block, reduce, got_gu = blocks
    extra = pack(smalls_grad, nz)
    extra = extra + flip(extra, "core")
    down_rows = R_FF // nz
    extra_count = extra.shape[1]
    got_in = share(queue["in1"], queue["in0"], 50, (grad_inputs, layer_outputs))
    extra = copy_after(narrow(extra).reshape(-1, HALF), got_in[0]).reshape(extra.shape)
    last = jnp.concatenate([down_block.reshape(nz, down_rows, HALF), extra], axis=1)
    reduce("down0", last.reshape(-1, HALF))
    down0, extra = queue["down0"][:down_rows], queue["down0"][down_rows:]

    place = jnp.stack([y, core]).astype(jnp.int32)
    grad_w_gu = got_gu
    half_rows = queue["outs"].shape[0] // 2
    got_out = share(
        queue["outs"][:half_rows], queue["outs"][half_rows:], 30, (got_in[0],)
    )
    shared = swap(extra).astype(F32)
    grad_w_in, grad_w_qkv = spread_in(place, got_in)
    got_down = share(queue["down1"], down0, 30, (grad_w_in,))
    out_rows, o_rows = R_SSM // nz, R_ATT // nz
    grad_w_out = spread_rows(place, got_out, 0, out_rows, out_rows)
    grad_w_o = spread_rows(place, got_out, out_rows, o_rows, o_rows)
    grad_w_down = spread_rows(place, got_down, 0, down_rows, down_rows)

    width, conv_width, ssm_width = D // nz, CONV_W // nz, D_SSM // nz
    heads_width = SSM_HEADS // nz
    dt_all = jnp.where(s == 0, shared[:, :R_HEADS, :width], shared[:, :R_HEADS, PART : PART + width])
    grad_w_in = with_dt(grad_w_in, dt_all.reshape(SSM_HEADS, width)).T
    small_sum = jnp.sum(shared[:, 16:], axis=0)
    small_sum = jnp.where(s == 0, small_sum[:8], small_sum[8:])
    head_row = small_sum[7, : 3 * LANES].reshape(3, LANES)
    cuts = (
        jnp.stack([small_sum[0, :width], small_sum[0, PART : PART + width]]),
        head_row[:, :heads_width],
        small_sum[1:6, :conv_width],
        small_sum[6:7, :ssm_width],
    )
    return (
        layer_outputs[None, :, None],
        grad_inputs[None, :, None],
        cuts[0][None],
        cuts[1][None],
        cuts[2][None],
        cuts[3],
        grad_w_in[None],
        grad_w_out[None],
        grad_w_qkv[None],
        grad_w_o[None],
        grad_w_gu[None],
        grad_w_down[None],
    )


def solution(mesh):
    CHANNELS.clear()
    sections, ctx, fsdp = mesh.devices.shape
    fine = Mesh(
        mesh.devices.reshape(sections, ctx // 2, 2, fsdp), ("section", "y", "core", "fsdp")
    )
    tokens = ("y", "core")
    in_specs = (
        P(None, "fsdp", tokens, None),
        P(None, "fsdp", tokens, None),
        P("section", None, "fsdp"),
        P("section", None, "fsdp"),
        P("section", None, "fsdp"),
        P("section", "fsdp"),
    ) + (P("section", "fsdp", None),) * 6
    out_specs = (
        P("section", None, "fsdp", tokens, None),
        P("section", None, "fsdp", tokens, None),
        P("section", None, "fsdp"),
        P("section", None, "fsdp"),
        P("section", None, "fsdp"),
        P("section", "fsdp"),
    ) + (P("section", "fsdp", None),) * 6
    return jax.shard_map(body, mesh=fine, in_specs=in_specs, out_specs=out_specs, check_vma=False)
```
